128 devices in a mesh: section: 2 (over core), dp: 4 (over x), shard: 16 (over z, y).
Axes of the slice: x: 4, y: 4, z: 4, core: 2. Of those that a mesh axis runs over, the one named last changes fastest.
Arguments:
- tokens: bfloat16 [2, 64, 128, 1024], P(None, ('dp', 'shard')), may hold values from -6 to 6
- lengths: int32 [2, 64], P(None, ('dp', 'shard')), may hold values from 64 to 128, as said below
- cotangent: bfloat16 [2, 64, 128, 1024], P(None, ('dp', 'shard')), may hold values from -6 to 6
- w_qkv: bfloat16 [2, 1024, 3072], P('section', 'shard'), may hold values from -0.1875 to 0.1875
- bias_q: bfloat16 [2, 1024], P('section', 'shard'), may hold values from -3 to 3
- bias_v: bfloat16 [2, 1024], P('section', 'shard'), may hold values from -3 to 3
- w_out: bfloat16 [2, 1024, 1024], P('section', 'shard'), may hold values from -0.75 to 0.75
- bias_out: bfloat16 [2, 1024], P('section', 'shard'), may hold values from -3 to 3
- gain_attn: bfloat16 [2, 1024], P('section', 'shard'), may hold values from 0.25 to 1.75
- shift_attn: bfloat16 [2, 1024], P('section', 'shard'), may hold values from -3 to 3
- w_up: bfloat16 [2, 1024, 4096], P('section', 'shard'), may hold values from -0.1875 to 0.1875
- bias_up: bfloat16 [2, 4096], P('section', 'shard'), may hold values from -3 to 3
- w_down: bfloat16 [2, 4096, 1024], P('section', 'shard'), may hold values from -0.09375 to 0.09375
- bias_down: bfloat16 [2, 1024], P('section', 'shard'), may hold values from -3 to 3
- gain_mlp: bfloat16 [2, 1024], P('section', 'shard'), may hold values from 0.25 to 1.75
- shift_mlp: bfloat16 [2, 1024], P('section', 'shard'), may hold values from -3 to 3
Outputs:
- activations: bfloat16 [2, 2, 64, 128, 1024], P('section', None, ('dp', 'shard'))
- input_grads: bfloat16 [2, 2, 64, 128, 1024], P('section', None, ('dp', 'shard'))
- grad_w_qkv: float32 [2, 1024, 3072], P('section', 'shard')
- grad_bias_q: float32 [2, 1024], P('section', 'shard')
- grad_bias_v: float32 [2, 1024], P('section', 'shard')
- grad_w_out: float32 [2, 1024, 1024], P('section', 'shard')
- grad_bias_out: float32 [2, 1024], P('section', 'shard')
- grad_gain_attn: float32 [2, 1024], P('section', 'shard')
- grad_shift_attn: float32 [2, 1024], P('section', 'shard')
- grad_w_up: float32 [2, 1024, 4096], P('section', 'shard')
- grad_bias_up: float32 [2, 4096], P('section', 'shard')
- grad_w_down: float32 [2, 4096, 1024], P('section', 'shard')
- grad_bias_down: float32 [2, 1024], P('section', 'shard')
- grad_gain_mlp: float32 [2, 1024], P('section', 'shard')
- grad_shift_mlp: float32 [2, 1024], P('section', 'shard')
The draws below stay inside these ranges and needn't reach their ends.
Inputs may be any that keep to these rules, and one draw needn't show every extreme that they name: `lengths`: the number of real tokens of each sequence; the first sequence of the first micro-batch is full.
All inputs are finite; a program needn't handle non-finite values.
Results may differ from the reference program's by a relative error of at most 0.023.
Values may be sent and summed in bfloat16 or wider, within the bound.
No kernel may reach another device: no remote copies, remote signals or barrier semaphores. Data moves between devices by JAX's collectives and lax.ppermute only.
A program may use at most 256 MiB of HBM per device.

```python
import jax
import jax.numpy as jnp
from jax import lax

D = 1024
HEADS = 16
HEAD_DIM = 64
FF = 4096
SEQ = 128
MICRO = 2
BATCH = 64
N_SECTION = 2


def draw_lengths(key, part):
    key = jax.random.fold_in(key, 7)
    drawn = jax.random.randint(key, (MICRO, BATCH), SEQ // 2, SEQ + 1, dtype=jnp.int32)
    return drawn.at[0, 0].set(SEQ)


def level_of(rng, extent, pieces, least, top_value):
    loudness = 1.0
    for dim, shards_of in pieces:
        heights = jax.random.uniform(jax.random.fold_in(jax.random.fold_in(rng, 6), dim), (shards_of,), jnp.float32, least / len(pieces), top_value / len(pieces))
        loudness = loudness * jnp.repeat(jnp.exp(heights), extent[dim] // shards_of).reshape((-1,) + (1,) * (len(extent) - 1 - dim))
    return loudness


def scatter_about(rng, shape, spread, bound, cuts=(), held_as=jnp.bfloat16):
    array = jax.random.normal(rng, shape, jnp.float32) * spread
    if len(cuts) > 0:
        array = level_of(rng, shape, cuts, -0.22, 0.18) * array
    return jnp.clip(array, min=-bound, max=bound).astype(held_as)


def setup_inputs(seed: int = 0) -> dict:
    key_list = jax.random.split(jax.random.key(seed), 17)
    tokens = scatter_about(key_list[0], (MICRO, BATCH, SEQ, D), 1.0, 6.0, ((1, 64),))
    lengths = draw_lengths(jax.random.fold_in(key_list[16], 71), 0)
    cotangent = scatter_about(key_list[2], (MICRO, BATCH, SEQ, D), 1.0, 6.0, ((1, 64),))
    w_qkv = scatter_about(key_list[3], (N_SECTION, D, 3 * D), D ** -0.5, 0.1875, ((0, 2), (1, 16)))
    bias_q = scatter_about(key_list[4], (N_SECTION, D), 0.3, 3.0, ((0, 2), (1, 16)))
    bias_v = scatter_about(key_list[5], (N_SECTION, D), 0.3, 3.0, ((0, 2), (1, 16)))
    w_out = scatter_about(key_list[6], (N_SECTION, D, D), (D * 8 // SEQ) ** -0.5, 0.75, ((0, 2), (1, 16)))
    bias_out = scatter_about(key_list[7], (N_SECTION, D), 0.3, 3.0, ((0, 2), (1, 16)))
    gain_attn = jnp.clip(1.0 + 0.15 * jax.random.normal(key_list[8], (N_SECTION, D), jnp.float32), 0.25, 1.75).astype(jnp.bfloat16)
    shift_attn = scatter_about(key_list[9], (N_SECTION, D), 0.3, 3.0, ((0, 2), (1, 16)))
    w_up = scatter_about(key_list[10], (N_SECTION, D, FF), D ** -0.5, 0.1875, ((0, 2), (1, 16)))
    bias_up = scatter_about(key_list[11], (N_SECTION, FF), 0.3, 3.0, ((0, 2), (1, 16)))
    w_down = scatter_about(key_list[12], (N_SECTION, FF, D), FF ** -0.5, 0.09375, ((0, 2), (1, 16)))
    bias_down = scatter_about(key_list[13], (N_SECTION, D), 0.3, 3.0, ((0, 2), (1, 16)))
    gain_mlp = jnp.clip(1.0 + 0.15 * jax.random.normal(key_list[14], (N_SECTION, D), jnp.float32), 0.25, 1.75).astype(jnp.bfloat16)
    shift_mlp = scatter_about(key_list[15], (N_SECTION, D), 0.3, 3.0, ((0, 2), (1, 16)))
    return dict(tokens=tokens, lengths=lengths, cotangent=cotangent, w_qkv=w_qkv, bias_q=bias_q, bias_v=bias_v, w_out=w_out, bias_out=bias_out, gain_attn=gain_attn, shift_attn=shift_attn, w_up=w_up, bias_up=bias_up, w_down=w_down, bias_down=bias_down, gain_mlp=gain_mlp, shift_mlp=shift_mlp)


@jax.custom_vjp
def low(v):
    return lax.optimization_barrier(v.astype(jnp.bfloat16)).astype(jnp.float32)

@jax.custom_vjp
def low_back(v):
    return v

def low_keep(v):
    return (low(v), None)

def low_pass(kept, grad):
    return (grad,)

def back_keep(v):
    return (v, None)

def back_low(kept, grad):
    return (low(grad),)
low.defvjp(low_keep, low_pass)
low_back.defvjp(back_keep, back_low)
EPSILON = 1e-06

def normalize(values):
    centered = values - lax.optimization_barrier(jnp.mean(values, axis=-1, keepdims=True))
    return centered * lax.rsqrt(lax.optimization_barrier(jnp.mean(centered * centered, axis=-1, keepdims=True)) + EPSILON)

def layer(inputs, params, seq_lengths):
    w_qkv, bias_q, bias_v, w_out, bias_out, gain_attn, shift_attn, w_up, bias_up, w_down, bias_down, gain_mlp, shift_mlp = params
    highest = lax.Precision.HIGHEST
    count = inputs.shape[0]
    bias_all = jnp.concatenate([bias_q, jnp.zeros_like(bias_q), bias_v])
    packed = low_back(low(jnp.einsum('nld,de->nle', inputs, w_qkv, precision=highest) + bias_all))
    queries = packed[..., :D].reshape(count, SEQ, HEADS, HEAD_DIM)
    keys_all = packed[..., D:2 * D].reshape(count, SEQ, HEADS, HEAD_DIM)
    values_all = packed[..., 2 * D:].reshape(count, SEQ, HEADS, HEAD_DIM)
    scores = low_back(jnp.einsum('nqhd,nkhd->nhqk', queries, keys_all, precision=highest) * HEAD_DIM ** (-0.5))
    positions = jnp.arange(SEQ, dtype=jnp.int32)
    visible = positions[None, None, None, :] < seq_lengths[:, None, None, None]
    scores = jnp.where(visible, scores, -1000000000.0)
    soft_weights = jax.nn.softmax(scores, axis=-1)
    attended = jnp.einsum('nhqk,nkhd->nqhd', low(soft_weights), values_all, precision=highest)
    attended = low_back(low(attended)).reshape(count, SEQ, D)
    branch = low_back(jnp.einsum('nld,de->nle', attended, w_out, precision=highest) + bias_out)
    hidden = low(normalize(inputs + branch) * gain_attn + shift_attn)
    upward = low_back(jnp.einsum('nld,df->nlf', hidden, w_up, precision=highest) + bias_up)
    activated = low(jax.nn.gelu(upward, approximate=False))
    mixed = low_back(jnp.einsum('nlf,fd->nld', activated, w_down, precision=highest) + bias_down)
    return normalize(hidden + mixed) * gain_mlp + shift_mlp

def reference(tokens, lengths, cotangent, w_qkv, bias_q, bias_v, w_out, bias_out, gain_attn, shift_attn, w_up, bias_up, w_down, bias_down, gain_mlp, shift_mlp):
    total = MICRO * BATCH
    inputs = tokens.astype(jnp.float32).reshape(total, SEQ, D)
    seq_lengths = lengths.reshape(total).astype(jnp.int32)
    params = tuple((member.astype(jnp.float32) for member in (w_qkv, bias_q, bias_v, w_out, bias_out, gain_attn, shift_attn, w_up, bias_up, w_down, bias_down, gain_mlp, shift_mlp)))

    def forward(first_in, probe, *weights):
        first_params = tuple((member[0] for member in weights))
        second_params = tuple((member[1] for member in weights))
        first_out = layer(first_in, first_params, seq_lengths)
        passed = low_back(low(first_out)) + probe
        second_out = layer(passed, second_params, seq_lengths)
        return (second_out, passed)
    probe = jnp.zeros((total, SEQ, D), jnp.float32)
    second_out, pull_back, first_out = jax.vjp(forward, inputs, probe, *params, has_aux=True)
    grads = pull_back(cotangent.astype(jnp.float32).reshape(total, SEQ, D))
    activations = jnp.stack([first_out, second_out]).reshape(2, MICRO, BATCH, SEQ, D).astype(jnp.bfloat16)
    input_grads = jnp.stack([grads[0], grads[1]]).reshape(2, MICRO, BATCH, SEQ, D).astype(jnp.bfloat16)
    return (activations, input_grads, grads[2], grads[3], grads[4], grads[5], grads[6], grads[7], grads[8], grads[9], grads[10], grads[11], grads[12], grads[13], grads[14])
```

```python
import jax
import jax.numpy as jnp
from jax import lax
from jax.sharding import PartitionSpec as P


HEAD_DIM = 64
EPSILON = 1e-06
LANES = 128
BF = jnp.bfloat16
F32 = jnp.float32


def swap(value):
    return lax.ppermute(value, "section", [(0, 1), (1, 0)])


def pair_sum(part):
    low = part.astype(BF)
    other = swap(low)
    return low.astype(F32) + other.astype(F32)


def dot(left, right):
    return jnp.dot(left, right, preferred_element_type=F32)


def transpose_dot(left, right):
    return lax.dot_general(left, right, (((0,), (0,)), ((), ())), preferred_element_type=F32)


def dot_transposed(left, right):
    return lax.dot_general(left, right, (((1,), (1,)), ((), ())), preferred_element_type=F32)


def norm_rows(values):
    centered = values - jnp.mean(values, axis=-1, keepdims=True)
    inverse = lax.rsqrt(jnp.mean(centered * centered, axis=-1, keepdims=True) + EPSILON)
    return (centered * inverse, inverse)


def norm_back(grad_norm, normed, inverse):
    return inverse * (
        grad_norm
        - jnp.mean(grad_norm, axis=-1, keepdims=True)
        - normed * jnp.mean(grad_norm * normed, axis=-1, keepdims=True)
    )


def heads_of(packed, number, count):
    width = packed.shape[1] // 3
    piece = packed[:, number * width : (number + 1) * width]
    return piece.reshape(count, -1, width // HEAD_DIM, HEAD_DIM).transpose(0, 2, 1, 3)


def join_heads(parts):
    count, heads, rows, size = parts.shape
    return parts.transpose(0, 2, 1, 3).reshape(count * rows, heads * size)


def masked_scores(queries, keys, seq_lengths):
    scores = jnp.einsum("nhqd,nhkd->nhqk", queries, keys, preferred_element_type=F32)
    scores = scores * HEAD_DIM ** (-0.5)
    positions = lax.broadcasted_iota(jnp.int32, scores.shape, 3)
    return jnp.where(positions < seq_lengths[:, None, None, None], scores, -1000000000.0)


def layer_forward(inputs, weights, seq_lengths):
    count = seq_lengths.shape[0]
    packed = (dot(inputs, weights["qkv"]) + weights["bias_qkv"]).astype(BF)
    queries, keys, values = (heads_of(packed, n, count) for n in range(3))
    scores = masked_scores(queries, keys, seq_lengths)
    row_max = jnp.max(scores, axis=-1, keepdims=True)
    exponent = jnp.exp(scores - row_max)
    soft_weights = exponent / jnp.sum(exponent, axis=-1, keepdims=True)
    attended = jnp.einsum(
        "nhqk,nhkd->nhqd", soft_weights.astype(BF), values, preferred_element_type=F32
    )
    attended = join_heads(attended.astype(BF))
    branch = pair_sum(dot(attended, weights["out"])) + weights["bias_out"]
    normed_attn, inverse_attn = norm_rows(inputs.astype(F32) + branch)
    hidden = (normed_attn * weights["gain_attn"] + weights["shift_attn"]).astype(BF)
    upward = [dot(hidden, w) + b for w, b in zip(weights["up"], weights["bias_up"])]
    activated = [jax.nn.gelu(u, approximate=False).astype(BF) for u in upward]
    mixed = sum(dot(g, w) for g, w in zip(activated, weights["down"]))
    mixed = pair_sum(mixed) + weights["bias_down"]
    normed_mlp, inverse_mlp = norm_rows(hidden.astype(F32) + mixed)
    result = (normed_mlp * weights["gain_mlp"] + weights["shift_mlp"]).astype(BF)
    kept = dict(
        inputs=inputs,
        qkv=(queries, keys, values),
        soft_weights=soft_weights,
        attended=attended,
        normed_attn=normed_attn,
        inverse_attn=inverse_attn,
        hidden=hidden,
        upward=upward,
        activated=activated,
        normed_mlp=normed_mlp,
        inverse_mlp=inverse_mlp,
    )
    return (result, kept)


def layer_backward(grad_result, kept, weights):
    scaling = HEAD_DIM ** (-0.5)
    grad_result = grad_result.astype(F32)
    normed_mlp = kept["normed_mlp"]
    grad_gain_mlp = jnp.sum(grad_result * normed_mlp, axis=0)
    grad_shift_mlp = jnp.sum(grad_result, axis=0)
    grad_resid_mlp = norm_back(grad_result * weights["gain_mlp"], normed_mlp, kept["inverse_mlp"])
    grad_mixed = grad_resid_mlp.astype(BF)
    grad_bias_down = jnp.sum(grad_mixed.astype(F32), axis=0)
    grad_down = [transpose_dot(g, grad_mixed).astype(BF) for g in kept["activated"]]
    grad_upward = []
    for up, w in zip(kept["upward"], weights["down"]):
        pull = jax.vjp(lambda point: jax.nn.gelu(point, approximate=False), up)[1]
        grad_upward.append(pull(dot_transposed(grad_mixed, w))[0].astype(BF))
    grad_bias_up = [jnp.sum(u.astype(F32), axis=0) for u in grad_upward]
    grad_up = [transpose_dot(kept["hidden"], u).astype(BF) for u in grad_upward]
    passed = sum(dot_transposed(u, w) for u, w in zip(grad_upward, weights["up"]))
    grad_hidden = grad_resid_mlp + pair_sum(passed)
    normed_attn = kept["normed_attn"]
    grad_gain_attn = jnp.sum(grad_hidden * normed_attn, axis=0)
    grad_shift_attn = jnp.sum(grad_hidden, axis=0)
    grad_resid_attn = norm_back(
        grad_hidden * weights["gain_attn"], normed_attn, kept["inverse_attn"]
    )
    grad_branch = grad_resid_attn.astype(BF)
    grad_bias_out = jnp.sum(grad_branch.astype(F32), axis=0)
    grad_out = transpose_dot(kept["attended"], grad_branch).astype(BF)
    queries, keys, values = kept["qkv"]
    count = queries.shape[0]
    grad_attended = dot_transposed(grad_branch, weights["out"]).astype(BF)
    grad_attended = grad_attended.reshape(count, -1, queries.shape[1], HEAD_DIM)
    grad_attended = grad_attended.transpose(0, 2, 1, 3)
    soft_weights = kept["soft_weights"]
    grad_values = jnp.einsum(
        "nhqk,nhqd->nhkd", soft_weights.astype(BF), grad_attended, preferred_element_type=F32
    )
    grad_soft = jnp.einsum(
        "nhqd,nhkd->nhqk", grad_attended, values, preferred_element_type=F32
    )
    grad_scores = soft_weights * (
        grad_soft - jnp.sum(grad_soft * soft_weights, axis=-1, keepdims=True)
    )
    grad_scores = grad_scores.astype(BF)
    grad_queries = scaling * jnp.einsum(
        "nhqk,nhkd->nhqd", grad_scores, keys, preferred_element_type=F32
    )
    grad_keys = scaling * jnp.einsum(
        "nhqk,nhqd->nhkd", grad_scores, queries, preferred_element_type=F32
    )
    grad_packed = jnp.concatenate(
        [join_heads(g.astype(BF)) for g in (grad_queries, grad_keys, grad_values)], axis=1
    )
    columns = jnp.sum(grad_packed.astype(F32), axis=0)
    width = columns.shape[0] // 3
    grad_qkv = transpose_dot(kept["inputs"], grad_packed).astype(BF)
    grad_inputs = grad_resid_attn + pair_sum(dot_transposed(grad_packed, weights["qkv"]))
    grads = dict(
        qkv=grad_qkv,
        out=grad_out,
        up=grad_up,
        down=grad_down,
        bias_q=columns[:width],
        bias_v=columns[2 * width :],
        bias_up=grad_bias_up,
        whole=(
            grad_bias_out,
            grad_gain_attn,
            grad_shift_attn,
            grad_bias_down,
            grad_gain_mlp,
            grad_shift_mlp,
        ),
    )
    return (grad_inputs.astype(BF), grads)


def per_device(
    tokens,
    lengths,
    cotangent,
    w_qkv,
    bias_q,
    bias_v,
    w_out,
    bias_out,
    gain_attn,
    shift_attn,
    w_up,
    bias_up,
    w_down,
    bias_down,
    gain_mlp,
    shift_mlp,
):
    first = lax.axis_index("section") == 0
    shards = lax.axis_size("shard")
    rows = w_qkv.shape[1]
    model = w_qkv.shape[2] // 3
    ff = w_up.shape[2]
    half = model // 2
    unit = ff // shards // 2
    vector_count = 8 * rows + 2 * unit

    def choose(low, high):
        return jnp.where(first, low, high)

    def mine_of(low, high):
        return (choose(low, high), choose(high, low))

    def parts_of(part):
        qkv = w_qkv[0].reshape(rows, 3, 2, half)[:, :, part].reshape(rows, 3 * half)
        out = w_out[0][:, part * half : (part + 1) * half]
        up = w_up[0].reshape(rows, shards, 2, unit)[:, :, part].reshape(rows, shards * unit)
        down = w_down[0][part * unit : (part + 1) * unit].reshape(rows, -1)
        return jnp.concatenate([qkv, out, up, down], axis=1)

    vectors = jnp.concatenate(
        [
            v[0]
            for v in (
                bias_q,
                bias_v,
                bias_out,
                gain_attn,
                shift_attn,
                bias_down,
                gain_mlp,
                shift_mlp,
                bias_up,
            )
        ]
    )
    vectors = jnp.pad(vectors, (0, rows * LANES - vector_count)).reshape(rows, LANES)
    kept_part, sent_part = mine_of(parts_of(0), parts_of(1))
    own = jnp.concatenate([vectors, kept_part], axis=1)
    got = swap(jnp.concatenate([vectors, sent_part], axis=1))
    layers = mine_of(own, got)
    edges = (LANES + 3 * half, LANES + 4 * half, LANES + 4 * half + shards * unit)

    def gather(block):
        return lax.all_gather(block, "shard", axis=0, tiled=True)

    def gather_layer(block):
        attn = gather(block[:, : edges[1]])
        up = gather(block[:, edges[1] : edges[2]])
        down = gather(block[:, edges[2] :].reshape(unit, model))
        flat = attn[:, :LANES].reshape(shards, rows * LANES)[:, :vector_count].astype(F32)
        whole = [flat[:, n * rows : (n + 1) * rows].reshape(-1) for n in range(8)]
        bias_up_part = flat[:, 8 * rows :].reshape(shards, 2, unit)
        bias_up_part = choose(bias_up_part[:, 0], bias_up_part[:, 1]).reshape(-1)
        bias_q_part = choose(whole[0][:half], whole[0][half:])
        bias_v_part = choose(whole[1][:half], whole[1][half:])
        out = attn[:, edges[0] : edges[1]]
        held, handed = mine_of(out[:half], out[half:])
        arrived = swap(handed)
        return dict(
            qkv=attn[:, LANES : edges[0]],
            out=jnp.concatenate(mine_of(held, arrived), axis=1),
            up=[up],
            down=[down],
            bias_qkv=jnp.concatenate([bias_q_part, jnp.zeros_like(bias_q_part), bias_v_part]),
            bias_out=whole[2],
            gain_attn=whole[3],
            shift_attn=whole[4],
            bias_down=whole[5],
            gain_mlp=whole[6],
            shift_mlp=whole[7],
            bias_up=[bias_up_part],
        )

    weights = [gather_layer(block) for block in layers]

    def scatter(block):
        return lax.psum_scatter(block, "shard", scatter_dimension=0, tiled=True)

    def scatter_layer(grads):
        down = scatter(grads["down"][0])
        up = scatter(grads["up"][0])
        held, handed = mine_of(grads["out"][:, :half], grads["out"][:, half:])
        out = jnp.concatenate(mine_of(held, swap(handed)), axis=0)

        def widened(part):
            return jnp.concatenate([choose(part, 0.0), choose(0.0, part)])

        whole = [widened(grads["bias_q"]), widened(grads["bias_v"])]
        whole += [0.5 * v for v in grads["whole"]]
        part = grads["bias_up"][0].reshape(shards, unit)
        spread = jnp.concatenate([choose(part, 0.0), choose(0.0, part)], axis=1)
        flat = jnp.concatenate([v.reshape(shards, rows) for v in whole] + [spread], axis=1)
        flat = jnp.pad(flat.astype(BF), ((0, 0), (0, rows * LANES - vector_count)))
        flat = flat.reshape(shards * rows, LANES)
        attn = scatter(jnp.concatenate([flat, grads["qkv"], out], axis=1))
        return jnp.concatenate([attn, up, down.reshape(rows, -1)], axis=1)

    count = tokens.shape[0]
    seq_lengths = lengths[:, 0]
    middle, kept_first = layer_forward(tokens.reshape(-1, model), weights[0], seq_lengths)
    last, kept_second = layer_forward(middle, weights[1], seq_lengths)
    grad_middle, grads_second = layer_backward(cotangent.reshape(-1, model), kept_second, weights[1])
    summed_second = scatter_layer(grads_second)
    grad_first, grads_first = layer_backward(grad_middle, kept_first, weights[0])
    summed_first = scatter_layer(grads_first)
    summed_first, summed_second = lax.psum((summed_first, summed_second), "dp")

    held, handed = mine_of(summed_first, summed_second)
    low, high = mine_of(held, swap(handed))
    low, high = (low.astype(F32), high.astype(F32))

    def cut(block):
        flat = block[:, :LANES].reshape(-1)[:vector_count]
        qkv = block[:, LANES : edges[0]].reshape(rows, 3, half)
        up = block[:, edges[1] : edges[2]].reshape(rows, shards, unit)
        return (flat, qkv, block[:, edges[0] : edges[1]], up, block[:, edges[2] :].reshape(unit, -1))

    (flat_a, qkv_a, out_a, up_a, down_a), (flat_b, qkv_b, out_b, up_b, down_b) = (cut(low), cut(high))
    flat = flat_a + flat_b
    whole = [flat[n * rows : (n + 1) * rows] for n in range(8)]
    grads = (
        jnp.stack([qkv_a, qkv_b], axis=2).reshape(rows, -1),
        whole[0],
        whole[1],
        jnp.concatenate([out_a, out_b], axis=1),
        whole[2],
        whole[3],
        whole[4],
        jnp.stack([up_a, up_b], axis=2).reshape(rows, -1),
        flat[8 * rows :],
        jnp.concatenate([down_a, down_b], axis=0),
        whole[5],
        whole[6],
        whole[7],
    )
    shape = (1, count, 1, -1, model)
    activations = choose(middle, last).reshape(shape)
    input_grads = choose(grad_first, grad_middle).reshape(shape)
    return (activations, input_grads) + tuple(member[None] for member in grads)


def solution(mesh):
    rows = P(None, ("dp", "shard"), None, None)
    matrix = P("section", "shard", None)
    vector = P("section", "shard")
    weight_specs = (matrix, vector, vector, matrix, vector, vector, vector)
    weight_specs += (matrix, vector, matrix, vector, vector, vector)
    in_specs = (rows, P(None, ("dp", "shard")), rows) + weight_specs
    result = P("section", None, ("dp", "shard"), None, None)
    return jax.shard_map(
        per_device,
        mesh=mesh,
        in_specs=in_specs,
        out_specs=(result, result) + weight_specs,
        check_vma=False,
    )
```

```python
import jax
import jax.numpy as jnp
from jax import lax
from jax.sharding import PartitionSpec as P


HEAD_DIM = 64
EPSILON = 1e-06
LANES = 128
RING = 4
BF = jnp.bfloat16
F32 = jnp.float32


def swap(value):
    return lax.ppermute(value, "section", [(0, 1), (1, 0)])


def pair_sum(part):
    low = part.astype(BF)
    other = swap(low)
    return low.astype(F32) + other.astype(F32)


def dot(left, right):
    return jnp.dot(left, right, preferred_element_type=F32)


def transpose_dot(left, right):
    return lax.dot_general(left, right, (((0,), (0,)), ((), ())), preferred_element_type=F32)


def dot_transposed(left, right):
    return lax.dot_general(left, right, (((1,), (1,)), ((), ())), preferred_element_type=F32)


def norm_rows(values):
    centered = values - jnp.mean(values, axis=-1, keepdims=True)
    inverse = lax.rsqrt(jnp.mean(centered * centered, axis=-1, keepdims=True) + EPSILON)
    return (centered * inverse, inverse)


def norm_back(grad_norm, normed, inverse):
    return inverse * (
        grad_norm
        - jnp.mean(grad_norm, axis=-1, keepdims=True)
        - normed * jnp.mean(grad_norm * normed, axis=-1, keepdims=True)
    )


def heads_of(packed, number, count):
    width = packed.shape[1] // 3
    piece = packed[:, number * width : (number + 1) * width]
    return piece.reshape(count, -1, width // HEAD_DIM, HEAD_DIM).transpose(0, 2, 1, 3)


def join_heads(parts):
    count, heads, rows, size = parts.shape
    return parts.transpose(0, 2, 1, 3).reshape(count * rows, heads * size)


def masked_scores(queries, keys, seq_lengths):
    scores = jnp.einsum("nhqd,nhkd->nhqk", queries, keys, preferred_element_type=F32)
    scores = scores * HEAD_DIM ** (-0.5)
    positions = lax.broadcasted_iota(jnp.int32, scores.shape, 3)
    return jnp.where(positions < seq_lengths[:, None, None, None], scores, -1000000000.0)


def layer_forward(inputs, weights, seq_lengths):
    count = seq_lengths.shape[0]
    packed = (dot(inputs, weights["qkv"]) + weights["bias_qkv"]).astype(BF)
    queries, keys, values = (heads_of(packed, n, count) for n in range(3))
    scores = masked_scores(queries, keys, seq_lengths)
    row_max = jnp.max(scores, axis=-1, keepdims=True)
    exponent = jnp.exp(scores - row_max)
    soft_weights = exponent / jnp.sum(exponent, axis=-1, keepdims=True)
    attended = jnp.einsum(
        "nhqk,nhkd->nhqd", soft_weights.astype(BF), values, preferred_element_type=F32
    )
    attended = join_heads(attended.astype(BF))
    branch = pair_sum(dot(attended, weights["out"])) + weights["bias_out"]
    normed_attn, inverse_attn = norm_rows(inputs.astype(F32) + branch)
    hidden = (normed_attn * weights["gain_attn"] + weights["shift_attn"]).astype(BF)
    upward = [dot(hidden, w) + b for w, b in zip(weights["up"], weights["bias_up"])]
    activated = [jax.nn.gelu(u, approximate=False).astype(BF) for u in upward]
    mixed = sum(dot(g, w) for g, w in zip(activated, weights["down"]))
    mixed = pair_sum(mixed) + weights["bias_down"]
    normed_mlp, inverse_mlp = norm_rows(hidden.astype(F32) + mixed)
    result = (normed_mlp * weights["gain_mlp"] + weights["shift_mlp"]).astype(BF)
    kept = dict(
        inputs=inputs,
        qkv=(queries, keys, values),
        soft_weights=soft_weights,
        attended=attended,
        normed_attn=normed_attn,
        inverse_attn=inverse_attn,
        hidden=hidden,
        upward=upward,
        activated=activated,
        normed_mlp=normed_mlp,
        inverse_mlp=inverse_mlp,
    )
    return (result, kept)


def layer_backward(grad_result, kept, weights):
    scaling = HEAD_DIM ** (-0.5)
    grad_result = grad_result.astype(F32)
    normed_mlp = kept["normed_mlp"]
    grad_gain_mlp = jnp.sum(grad_result * normed_mlp, axis=0)
    grad_shift_mlp = jnp.sum(grad_result, axis=0)
    grad_resid_mlp = norm_back(grad_result * weights["gain_mlp"], normed_mlp, kept["inverse_mlp"])
    grad_mixed = grad_resid_mlp.astype(BF)
    grad_bias_down = jnp.sum(grad_mixed.astype(F32), axis=0)
    grad_down = [transpose_dot(g, grad_mixed).astype(BF) for g in kept["activated"]]
    grad_upward = []
    for up, w in zip(kept["upward"], weights["down"]):
        pull = jax.vjp(lambda point: jax.nn.gelu(point, approximate=False), up)[1]
        grad_upward.append(pull(dot_transposed(grad_mixed, w))[0].astype(BF))
    grad_bias_up = [jnp.sum(u.astype(F32), axis=0) for u in grad_upward]
    grad_up = [transpose_dot(kept["hidden"], u).astype(BF) for u in grad_upward]
    passed = sum(dot_transposed(u, w) for u, w in zip(grad_upward, weights["up"]))
    grad_hidden = grad_resid_mlp + pair_sum(passed)
    normed_attn = kept["normed_attn"]
    grad_gain_attn = jnp.sum(grad_hidden * normed_attn, axis=0)
    grad_shift_attn = jnp.sum(grad_hidden, axis=0)
    grad_resid_attn = norm_back(
        grad_hidden * weights["gain_attn"], normed_attn, kept["inverse_attn"]
    )
    grad_branch = grad_resid_attn.astype(BF)
    grad_bias_out = jnp.sum(grad_branch.astype(F32), axis=0)
    grad_out = transpose_dot(kept["attended"], grad_branch).astype(BF)
    queries, keys, values = kept["qkv"]
    count = queries.shape[0]
    grad_attended = dot_transposed(grad_branch, weights["out"]).astype(BF)
    grad_attended = grad_attended.reshape(count, -1, queries.shape[1], HEAD_DIM)
    grad_attended = grad_attended.transpose(0, 2, 1, 3)
    soft_weights = kept["soft_weights"]
    grad_values = jnp.einsum(
        "nhqk,nhqd->nhkd", soft_weights.astype(BF), grad_attended, preferred_element_type=F32
    )
    grad_soft = jnp.einsum(
        "nhqd,nhkd->nhqk", grad_attended, values, preferred_element_type=F32
    )
    grad_scores = soft_weights * (
        grad_soft - jnp.sum(grad_soft * soft_weights, axis=-1, keepdims=True)
    )
    grad_scores = grad_scores.astype(BF)
    grad_queries = scaling * jnp.einsum(
        "nhqk,nhkd->nhqd", grad_scores, keys, preferred_element_type=F32
    )
    grad_keys = scaling * jnp.einsum(
        "nhqk,nhqd->nhkd", grad_scores, queries, preferred_element_type=F32
    )
    grad_packed = jnp.concatenate(
        [join_heads(g.astype(BF)) for g in (grad_queries, grad_keys, grad_values)], axis=1
    )
    columns = jnp.sum(grad_packed.astype(F32), axis=0)
    width = columns.shape[0] // 3
    grad_qkv = transpose_dot(kept["inputs"], grad_packed).astype(BF)
    grad_inputs = grad_resid_attn + pair_sum(dot_transposed(grad_packed, weights["qkv"]))
    grads = dict(
        qkv=grad_qkv,
        out=grad_out,
        up=grad_up,
        down=grad_down,
        bias_q=columns[:width],
        bias_v=columns[2 * width :],
        bias_up=grad_bias_up,
        whole=(
            grad_bias_out,
            grad_gain_attn,
            grad_shift_attn,
            grad_bias_down,
            grad_gain_mlp,
            grad_shift_mlp,
        ),
    )
    return (grad_inputs.astype(BF), grads)


def per_device(
    tokens,
    lengths,
    cotangent,
    w_qkv,
    bias_q,
    bias_v,
    w_out,
    bias_out,
    gain_attn,
    shift_attn,
    w_up,
    bias_up,
    w_down,
    bias_down,
    gain_mlp,
    shift_mlp,
):
    first = lax.axis_index("section") == 0
    shards = lax.axis_size("shard")
    rows = w_qkv.shape[1]
    model = w_qkv.shape[2] // 3
    ff = w_up.shape[2]
    half = model // 2
    unit = ff // shards // 2
    vector_count = 8 * rows + 2 * unit

    def choose(low, high):
        return jnp.where(first, low, high)

    def mine_of(low, high):
        return (choose(low, high), choose(high, low))

    shard = lax.axis_index("shard")
    place = {"x": lax.axis_index("dp"), "y": shard % RING, "z": shard // RING}
    step = jnp.where(first, 1, -1)

    def around(value, axis):
        name = "dp" if axis == "x" else "shard"
        size = lax.axis_size(name)
        stride = RING if axis == "z" else 1
        route = []
        for core in range(2):
            for at in range(size):
                position = at // stride % RING
                moved = (position + (1 if core == 0 else -1)) % RING
                target = at + (moved - position) * stride
                route.append((core * size + at, core * size + target))
        return lax.ppermute(value, ("section", name), route)

    def hop(value, axis, distance):
        name = "dp" if axis == "x" else "shard"
        stride = RING if axis == "z" else 1
        route = []
        for at in range(lax.axis_size(name)):
            position = at // stride % RING
            moved = (position + distance) % RING
            route.append((at, at + (moved - position) * stride))
        return lax.ppermute(value, name, route)

    def put(whole, piece, at, dim):
        start = [0] * whole.ndim
        start[dim] = at
        return lax.dynamic_update_slice(whole, jnp.expand_dims(piece, dim), start)

    def ring_gather(block, axis, dim):
        shape = block.shape[:dim] + (RING,) + block.shape[dim:]
        whole = put(jnp.zeros(shape, block.dtype), block, place[axis], dim)
        for n in range(1, RING):
            block = around(block, axis)
            whole = put(whole, block, (place[axis] - n * step) % RING, dim)
        return whole

    def direct_gather(block, axis, dim):
        shape = block.shape[:dim] + (RING,) + block.shape[dim:]
        whole = put(jnp.zeros(shape, block.dtype), block, place[axis], dim)
        for n in range(1, RING):
            whole = put(whole, hop(block, axis, n), (place[axis] - n) % RING, dim)
        return whole

    def chunk(value, at, dim):
        return lax.dynamic_index_in_dim(value, at % RING, dim, keepdims=False).astype(F32)

    def ring_scatter(value, axis, dim):
        run = chunk(value, place[axis] - step, dim).astype(BF)
        for n in range(2, RING + 1):
            mine = chunk(value, place[axis] - n * step, dim)
            run = (around(run, axis).astype(F32) + mine).astype(BF)
        return run

    def direct_scatter(value, axis, dim):
        total = chunk(value, place[axis], dim)
        for n in range(1, RING):
            sent = chunk(value, place[axis] + n, dim).astype(BF)
            total = total + hop(sent, axis, n).astype(F32)
        return total.astype(BF)

    def placed(width, pieces):
        whole = jnp.zeros((pieces[0][1].shape[0], width), BF)
        for at, piece in pieces:
            whole = lax.dynamic_update_slice(whole, piece, (0, at))
        return whole

    def parts_of(part):
        qkv = w_qkv[0].reshape(rows, 3, 2, half)[:, :, part].reshape(rows, 3 * half)
        out = w_out[0][:, part * half : (part + 1) * half]
        up = w_up[0].reshape(rows, shards, 2, unit)[:, :, part].reshape(rows, shards * unit)
        return (qkv, out, up, w_down[0][part * unit : (part + 1) * unit])

    vectors = jnp.concatenate(
        [
            v[0]
            for v in (
                bias_q,
                bias_v,
                bias_out,
                gain_attn,
                shift_attn,
                bias_down,
                gain_mlp,
                shift_mlp,
                bias_up,
            )
        ]
    )
    vectors = jnp.pad(vectors, (0, rows * LANES - vector_count)).reshape(rows, LANES)
    split = [mine_of(low, high) for low, high in zip(parts_of(0), parts_of(1))]
    kept_part = (vectors,) + tuple(low for low, high in split)
    sent_part = (vectors,) + tuple(high for low, high in split)
    got_part = tuple(swap(member) for member in sent_part)
    blocks = [mine_of(own, got) for own, got in zip(kept_part, got_part)]
    edges = (LANES, LANES + 3 * half, LANES + 4 * half, LANES + 4 * half + shards * unit)

    def joined(layer, count):
        return placed(edges[count - 1], list(zip((0,) + edges, [b[layer] for b in blocks[:count]])))

    quarter = unit // RING
    down = jnp.stack(blocks[4]).reshape(2, RING, quarter, model)
    down = lax.dynamic_index_in_dim(down, place["x"], 1, keepdims=False)
    down = ring_gather(ring_gather(down, "y", 1), "z", 1)
    down = [ring_gather(down[layer], "x", 2).reshape(-1, model) for layer in range(2)]

    first_whole = lax.all_gather(joined(0, 4), "shard", axis=0, tiled=True)
    attn_whole = ring_gather(ring_gather(joined(1, 3), "y", 0), "z", 0).reshape(model, -1)
    up_whole = ring_gather(ring_gather(blocks[3][1], "z", 0), "y", 1).reshape(model, -1)

    def arranged(attn, up, down):
        flat = attn[:, :LANES].reshape(shards, rows * LANES)[:, :vector_count].astype(F32)
        whole = [flat[:, n * rows : (n + 1) * rows].reshape(-1) for n in range(8)]
        bias_up_part = flat[:, 8 * rows :].reshape(shards, 2, unit)
        bias_up_part = choose(bias_up_part[:, 0], bias_up_part[:, 1]).reshape(-1)
        bias_q_part = choose(whole[0][:half], whole[0][half:])
        bias_v_part = choose(whole[1][:half], whole[1][half:])
        out = attn[:, edges[1] : edges[2]]
        held, handed = mine_of(out[:half], out[half:])
        arrived = swap(handed)
        return dict(
            qkv=attn[:, LANES : edges[1]],
            out=jnp.concatenate(mine_of(held, arrived), axis=1),
            up=[up],
            down=[down],
            bias_qkv=jnp.concatenate([bias_q_part, jnp.zeros_like(bias_q_part), bias_v_part]),
            bias_out=whole[2],
            gain_attn=whole[3],
            shift_attn=whole[4],
            bias_down=whole[5],
            gain_mlp=whole[6],
            shift_mlp=whole[7],
            bias_up=[bias_up_part],
        )

    weights = [
        arranged(first_whole[:, : edges[2]], first_whole[:, edges[2] :], down[0]),
        arranged(attn_whole, up_whole, down[1]),
    ]

    def side_by_side(grads):
        held, handed = mine_of(grads["out"][:, :half], grads["out"][:, half:])
        out = jnp.concatenate(mine_of(held, swap(handed)), axis=0)

        def widened(part):
            return jnp.concatenate([choose(part, 0.0), choose(0.0, part)])

        whole = [widened(grads["bias_q"]), widened(grads["bias_v"])]
        whole += [0.5 * v for v in grads["whole"]]
        part = grads["bias_up"][0].reshape(shards, unit)
        spread = jnp.concatenate([choose(part, 0.0), choose(0.0, part)], axis=1)
        flat = jnp.concatenate([v.reshape(shards, rows) for v in whole] + [spread], axis=1)
        flat = jnp.pad(flat.astype(BF), ((0, 0), (0, rows * LANES - vector_count)))
        return (flat.reshape(shards * rows, LANES), grads["qkv"], out, grads["up"][0])

    def over_x(value):
        return ring_scatter(value.reshape(RING * RING, RING, quarter, model), "x", 1)

    count = tokens.shape[0]
    seq_lengths = lengths[:, 0]
    middle, kept_first = layer_forward(tokens.reshape(-1, model), weights[0], seq_lengths)
    last, kept_second = layer_forward(middle, weights[1], seq_lengths)
    grad_middle, grads_second = layer_backward(cotangent.reshape(-1, model), kept_second, weights[1])
    down_second = over_x(grads_second["down"][0])
    pieces = list(zip((0,) + edges, side_by_side(grads_second)))
    side_second = placed(edges[3], pieces)
    grad_middle, side_second = lax.optimization_barrier((grad_middle, side_second))
    side_second = lax.psum_scatter(side_second, "shard", scatter_dimension=0, tiled=True)
    side_second = lax.psum(side_second, "dp")

    grad_first, grads_first = layer_backward(grad_middle, kept_first, weights[0])
    down_first = over_x(grads_first["down"][0])
    pieces = list(zip((0,) + edges, side_by_side(grads_first)))
    up = pieces[3][1].reshape(RING, RING, rows, -1)
    up = ring_scatter(ring_scatter(up, "y", 1), "z", 0)
    attn = placed(edges[2], pieces[:3]).reshape(RING, RING, rows, -1)
    attn = ring_scatter(ring_scatter(attn, "z", 0), "y", 0)
    down = jnp.stack([down_first, down_second]).reshape(2, RING, RING, quarter, model)
    down = direct_scatter(ring_scatter(down, "z", 1), "y", 1)
    down = direct_gather(down, "x", 1).reshape(2, unit, model)
    side_first = placed(edges[3], [(0, attn), (edges[2], up)]).reshape(RING, rows // RING, -1)
    side_first = direct_scatter(side_first, "x", 0)
    side_first = direct_gather(side_first, "x", 0).reshape(rows, -1)

    summed_first, summed_second = ((side_first, down[0]), (side_second, down[1]))
    mine, sent = zip(*(mine_of(a, b) for a, b in zip(summed_first, summed_second)))
    both = [mine_of(a, swap(b)) for a, b in zip(mine, sent)]
    (side_a, side_b), (down_a, down_b) = [[v.astype(F32) for v in pair] for pair in both]

    def cut(block):
        flat = block[:, :LANES].reshape(-1)[:vector_count]
        qkv = block[:, LANES : edges[1]].reshape(rows, 3, half)
        up = block[:, edges[2] :].reshape(rows, shards, unit)
        return (flat, qkv, block[:, edges[1] : edges[2]], up)

    (flat_a, qkv_a, out_a, up_a), (flat_b, qkv_b, out_b, up_b) = (cut(side_a), cut(side_b))
    flat = flat_a + flat_b
    whole = [flat[n * rows : (n + 1) * rows] for n in range(8)]
    grads = (
        jnp.stack([qkv_a, qkv_b], axis=2).reshape(rows, -1),
        whole[0],
        whole[1],
        jnp.concatenate([out_a, out_b], axis=1),
        whole[2],
        whole[3],
        whole[4],
        jnp.stack([up_a, up_b], axis=2).reshape(rows, -1),
        flat[8 * rows :],
        jnp.concatenate([down_a, down_b], axis=0),
        whole[5],
        whole[6],
        whole[7],
    )
    shape = (1, count, 1, -1, model)
    activations = choose(middle, last).reshape(shape)
    input_grads = choose(grad_first, grad_middle).reshape(shape)
    return (activations, input_grads) + tuple(member[None] for member in grads)


def solution(mesh):
    rows = P(None, ("dp", "shard"), None, None)
    matrix = P("section", "shard", None)
    vector = P("section", "shard")
    weight_specs = (matrix, vector, vector, matrix, vector, vector, vector)
    weight_specs += (matrix, vector, matrix, vector, vector, vector)
    in_specs = (rows, P(None, ("dp", "shard")), rows) + weight_specs
    result = P("section", None, ("dp", "shard"), None, None)
    return jax.shard_map(
        per_device,
        mesh=mesh,
        in_specs=in_specs,
        out_specs=(result, result) + weight_specs,
        check_vma=False,
    )
```

```python
import jax
import jax.numpy as jnp
from jax import lax
from jax.sharding import PartitionSpec as P


HEAD_DIM = 64
EPSILON = 1e-06
TAU = 6.283185307179586
LANES = 128
RING = 4
BF = jnp.bfloat16
F32 = jnp.float32


def swap(value):
    return lax.ppermute(value, "section", [(0, 1), (1, 0)])


def pair_sum(part):
    low = part.astype(BF)
    other = swap(low)
    return low.astype(F32) + other.astype(F32)


def dot(left, right):
    return jnp.dot(left, right, preferred_element_type=F32)


def transpose_dot(left, right):
    return lax.dot_general(left, right, (((0,), (0,)), ((), ())), preferred_element_type=F32)


def dot_transposed(left, right):
    return lax.dot_general(left, right, (((1,), (1,)), ((), ())), preferred_element_type=F32)


def norm_rows(values):
    centered = values - jnp.mean(values, axis=-1, keepdims=True)
    inverse = lax.rsqrt(jnp.mean(centered * centered, axis=-1, keepdims=True) + EPSILON)
    return (centered * inverse, inverse)


def norm_back(grad_norm, normed, inverse):
    return inverse * (
        grad_norm
        - jnp.mean(grad_norm, axis=-1, keepdims=True)
        - normed * jnp.mean(grad_norm * normed, axis=-1, keepdims=True)
    )


def heads_of(packed, number, count):
    width = packed.shape[1] // 3
    piece = packed[:, number * width : (number + 1) * width]
    return piece.reshape(count, -1, width // HEAD_DIM, HEAD_DIM).transpose(0, 2, 1, 3)


def join_heads(parts):
    count, heads, rows, size = parts.shape
    return parts.transpose(0, 2, 1, 3).reshape(count * rows, heads * size)


def masked_scores(queries, keys, seq_lengths):
    scores = jnp.einsum("nhqd,nhkd->nhqk", queries, keys, preferred_element_type=F32)
    scores = scores * HEAD_DIM ** (-0.5)
    positions = lax.broadcasted_iota(jnp.int32, scores.shape, 3)
    return jnp.where(positions < seq_lengths[:, None, None, None], scores, -1000000000.0)


def layer_forward(inputs, weights, seq_lengths):
    count = seq_lengths.shape[0]
    packed = (dot(inputs, weights["qkv"]) + weights["bias_qkv"]).astype(BF)
    queries, keys, values = (heads_of(packed, n, count) for n in range(3))
    scores = masked_scores(queries, keys, seq_lengths)
    row_max = jnp.max(scores, axis=-1, keepdims=True)
    exponent = jnp.exp(scores - row_max)
    soft_weights = exponent / jnp.sum(exponent, axis=-1, keepdims=True)
    attended = jnp.einsum(
        "nhqk,nhkd->nhqd", soft_weights.astype(BF), values, preferred_element_type=F32
    )
    attended = join_heads(attended.astype(BF))
    branch = pair_sum(dot(attended, weights["out"])) + weights["bias_out"]
    normed_attn, inverse_attn = norm_rows(inputs.astype(F32) + branch)
    hidden = (normed_attn * weights["gain_attn"] + weights["shift_attn"]).astype(BF)
    upward = [dot(hidden, w) + b for w, b in zip(weights["up"], weights["bias_up"])]
    share = [0.5 + 0.5 * lax.erf(u * 0.5**0.5) for u in upward]
    activated = [(u * c).astype(BF) for u, c in zip(upward, share)]
    slope = [c + u * jnp.exp(-0.5 * u * u) * TAU ** (-0.5) for u, c in zip(upward, share)]
    mixed = sum(dot(g, w) for g, w in zip(activated, weights["down"]))
    mixed = pair_sum(mixed) + weights["bias_down"]
    normed_mlp, inverse_mlp = norm_rows(hidden.astype(F32) + mixed)
    result = (normed_mlp * weights["gain_mlp"] + weights["shift_mlp"]).astype(BF)
    kept = dict(
        inputs=inputs,
        qkv=(queries, keys, values),
        soft_weights=soft_weights,
        attended=attended,
        normed_attn=normed_attn,
        inverse_attn=inverse_attn,
        hidden=hidden,
        slope=slope,
        activated=activated,
        normed_mlp=normed_mlp,
        inverse_mlp=inverse_mlp,
    )
    return (result, kept)


def layer_backward(grad_result, kept, weights):
    scaling = HEAD_DIM ** (-0.5)
    grad_result = grad_result.astype(F32)
    normed_mlp = kept["normed_mlp"]
    grad_gain_mlp = jnp.sum(grad_result * normed_mlp, axis=0)
    grad_shift_mlp = jnp.sum(grad_result, axis=0)
    grad_resid_mlp = norm_back(grad_result * weights["gain_mlp"], normed_mlp, kept["inverse_mlp"])
    grad_mixed = grad_resid_mlp.astype(BF)
    grad_bias_down = jnp.sum(grad_mixed.astype(F32), axis=0)
    grad_down = [transpose_dot(g, grad_mixed).astype(BF) for g in kept["activated"]]
    grad_upward = [
        (dot_transposed(grad_mixed, w) * c).astype(BF)
        for c, w in zip(kept["slope"], weights["down"])
    ]
    grad_bias_up = [jnp.sum(u.astype(F32), axis=0) for u in grad_upward]
    grad_up = [transpose_dot(kept["hidden"], u).astype(BF) for u in grad_upward]
    passed = sum(dot_transposed(u, w) for u, w in zip(grad_upward, weights["up"]))
    grad_hidden = grad_resid_mlp + pair_sum(passed)
    normed_attn = kept["normed_attn"]
    grad_gain_attn = jnp.sum(grad_hidden * normed_attn, axis=0)
    grad_shift_attn = jnp.sum(grad_hidden, axis=0)
    grad_resid_attn = norm_back(
        grad_hidden * weights["gain_attn"], normed_attn, kept["inverse_attn"]
    )
    grad_branch = grad_resid_attn.astype(BF)
    grad_bias_out = jnp.sum(grad_branch.astype(F32), axis=0)
    grad_out = transpose_dot(kept["attended"], grad_branch).astype(BF)
    queries, keys, values = kept["qkv"]
    count = queries.shape[0]
    grad_attended = dot_transposed(grad_branch, weights["out"]).astype(BF)
    grad_attended = grad_attended.reshape(count, -1, queries.shape[1], HEAD_DIM)
    grad_attended = grad_attended.transpose(0, 2, 1, 3)
    soft_weights = kept["soft_weights"]
    grad_values = jnp.einsum(
        "nhqk,nhqd->nhkd", soft_weights.astype(BF), grad_attended, preferred_element_type=F32
    )
    grad_soft = jnp.einsum(
        "nhqd,nhkd->nhqk", grad_attended, values, preferred_element_type=F32
    )
    grad_scores = soft_weights * (
        grad_soft - jnp.sum(grad_soft * soft_weights, axis=-1, keepdims=True)
    )
    grad_scores = grad_scores.astype(BF)
    grad_queries = scaling * jnp.einsum(
        "nhqk,nhkd->nhqd", grad_scores, keys, preferred_element_type=F32
    )
    grad_keys = scaling * jnp.einsum(
        "nhqk,nhqd->nhkd", grad_scores, queries, preferred_element_type=F32
    )
    grad_packed = jnp.concatenate(
        [join_heads(g.astype(BF)) for g in (grad_queries, grad_keys, grad_values)], axis=1
    )
    columns = jnp.sum(grad_packed.astype(F32), axis=0)
    width = columns.shape[0] // 3
    grad_qkv = transpose_dot(kept["inputs"], grad_packed).astype(BF)
    grad_inputs = grad_resid_attn + pair_sum(dot_transposed(grad_packed, weights["qkv"]))
    grads = dict(
        qkv=grad_qkv,
        out=grad_out,
        up=grad_up,
        down=grad_down,
        bias_q=columns[:width],
        bias_v=columns[2 * width :],
        bias_up=grad_bias_up,
        whole=(
            grad_bias_out,
            grad_gain_attn,
            grad_shift_attn,
            grad_bias_down,
            grad_gain_mlp,
            grad_shift_mlp,
        ),
    )
    return (grad_inputs.astype(BF), grads)


def per_device(
    tokens,
    lengths,
    cotangent,
    w_qkv,
    bias_q,
    bias_v,
    w_out,
    bias_out,
    gain_attn,
    shift_attn,
    w_up,
    bias_up,
    w_down,
    bias_down,
    gain_mlp,
    shift_mlp,
):
    first = lax.axis_index("section") == 0
    shards = lax.axis_size("shard")
    rows = w_qkv.shape[1]
    model = w_qkv.shape[2] // 3
    ff = w_up.shape[2]
    half = model // 2
    unit = ff // shards // 2
    vector_count = 8 * rows + 2 * unit

    def choose(low, high):
        return jnp.where(first, low, high)

    def mine_of(low, high):
        return (choose(low, high), choose(high, low))

    shard = lax.axis_index("shard")
    place = {"x": lax.axis_index("dp"), "y": shard % RING, "z": shard // RING}

    near = {axis: at ^ choose(1, 3) for axis, at in place.items()}
    far = {axis: at ^ choose(3, 1) for axis, at in place.items()}

    def trade(value, axis, masks):
        name = "dp" if axis == "x" else "shard"
        size = lax.axis_size(name)
        stride = RING if axis == "z" else 1
        route = []
        for core in range(2):
            for at in range(size):
                position = at // stride % RING
                target = at + ((position ^ masks[core]) - position) * stride
                route.append((core * size + at, core * size + target))
        return lax.ppermute(value, ("section", name), route)

    def after(value, earlier):
        return lax.optimization_barrier((value, earlier))[0]

    def put(whole, piece, at, dim):
        start = [0] * whole.ndim
        start[dim] = at
        return lax.dynamic_update_slice(whole, jnp.expand_dims(piece, dim), start)

    def ring_gather(block, axis, dim, between=None, behind=None):
        beside = trade(block, axis, (1, 3))
        both = jnp.stack([block, beside])
        across = trade(both if between is None else after(both, between), axis, (3, 1))
        across = across if behind is None else after(across, behind)
        whole = jnp.zeros(block.shape[:dim] + (RING,) + block.shape[dim:], block.dtype)
        whole = put(whole, block, place[axis], dim)
        whole = put(whole, beside, near[axis], dim)
        whole = put(whole, across[0], far[axis], dim)
        return put(whole, across[1], place[axis] ^ 2, dim)

    def ring_scatter(value, axis, dim):
        def chunk(at):
            return lax.dynamic_index_in_dim(value, at, dim, keepdims=False)

        sent = jnp.stack([chunk(near[axis]), chunk(place[axis] ^ 2)])
        beside = trade(sent, axis, (1, 3)).astype(F32)
        sent = (chunk(far[axis]).astype(F32) + beside[1]).astype(BF)
        across = trade(sent, axis, (3, 1)).astype(F32)
        return (chunk(place[axis]).astype(F32) + beside[0] + across).astype(BF)

    def placed(width, pieces):
        whole = jnp.zeros((pieces[0][1].shape[0], width), BF)
        for at, piece in pieces:
            whole = lax.dynamic_update_slice(whole, piece, (0, at))
        return whole

    def parts_of(part):
        qkv = w_qkv[0].reshape(rows, 3, 2, half)[:, :, part].reshape(rows, 3 * half)
        out = w_out[0][:, part * half : (part + 1) * half]
        up = w_up[0].reshape(rows, shards, 2, unit)[:, :, part].reshape(rows, shards * unit)
        return (qkv, out, up, w_down[0][part * unit : (part + 1) * unit])

    vectors = jnp.concatenate(
        [
            v[0]
            for v in (
                bias_q,
                bias_v,
                bias_out,
                gain_attn,
                shift_attn,
                bias_down,
                gain_mlp,
                shift_mlp,
                bias_up,
            )
        ]
    )
    vectors = jnp.pad(vectors, (0, rows * LANES - vector_count)).reshape(rows, LANES)
    split = [mine_of(low, high) for low, high in zip(parts_of(0), parts_of(1))]
    kept_part = (vectors,) + tuple(low for low, high in split)
    sent_part = (vectors,) + tuple(high for low, high in split)
    got_part = tuple(swap(member) for member in sent_part)
    blocks = [mine_of(own, got) for own, got in zip(kept_part, got_part)]
    edges = (LANES, LANES + 3 * half, LANES + 4 * half, LANES + 4 * half + shards * unit)

    def joined(layer, count):
        return placed(edges[count - 1], list(zip((0,) + edges, [b[layer] for b in blocks[:count]])))

    quarter = unit // RING

    def down_quarter(block, order):
        mine = lax.dynamic_index_in_dim(
            block.reshape(RING, quarter, model), place["x"], 0, keepdims=False
        )
        mine = ring_gather(mine, order[0], 0)
        mine = ring_gather(mine, order[1], 0 if order[1] == "z" else 1)
        return mine.reshape(shards, quarter, model)

    attn_first = ring_gather(joined(0, 3), "y", 0)
    up_first = ring_gather(blocks[3][0], "z", 0)
    low_first = down_quarter(blocks[4][0], "yz")
    attn_second = ring_gather(after(joined(1, 3), attn_first), "y", 0)
    up_second = ring_gather(after(blocks[3][1], up_first), "z", 0)
    low_second = down_quarter(after(blocks[4][1], low_first), "zy")
    attn_first = ring_gather(attn_first, "z", 0)
    up_first = ring_gather(up_first, "y", 1)
    low_first = ring_gather(low_first, "x", 1)
    attn_second = after(attn_second, attn_first)
    up_second = after(up_second, up_first)
    low_second = after(low_second, low_first)

    def arranged(attn, up, down):
        flat = attn[:, :LANES].reshape(shards, rows * LANES)[:, :vector_count].astype(F32)
        whole = [flat[:, n * rows : (n + 1) * rows].reshape(-1) for n in range(8)]
        bias_up_part = flat[:, 8 * rows :].reshape(shards, 2, unit)
        bias_up_part = choose(bias_up_part[:, 0], bias_up_part[:, 1]).reshape(-1)
        bias_q_part = choose(whole[0][:half], whole[0][half:])
        bias_v_part = choose(whole[1][:half], whole[1][half:])
        out = attn[:, edges[1] : edges[2]]
        held, handed = mine_of(out[:half], out[half:])
        arrived = swap(handed)
        return dict(
            qkv=attn[:, LANES : edges[1]],
            out=jnp.concatenate(mine_of(held, arrived), axis=1),
            up=[up],
            down=[down],
            bias_qkv=jnp.concatenate([bias_q_part, jnp.zeros_like(bias_q_part), bias_v_part]),
            bias_out=whole[2],
            gain_attn=whole[3],
            shift_attn=whole[4],
            bias_down=whole[5],
            gain_mlp=whole[6],
            shift_mlp=whole[7],
            bias_up=[bias_up_part],
        )

    def flat_rows(*members):
        return arranged(*(member.reshape(-1, member.shape[-1]) for member in members))

    def side_by_side(grads):
        held, handed = mine_of(grads["out"][:, :half], grads["out"][:, half:])
        out = jnp.concatenate(mine_of(held, swap(handed)), axis=0)

        def widened(part):
            return jnp.concatenate([choose(part, 0.0), choose(0.0, part)])

        whole = [widened(grads["bias_q"]), widened(grads["bias_v"])]
        whole += [0.5 * v for v in grads["whole"]]
        part = grads["bias_up"][0].reshape(shards, unit)
        spread = jnp.concatenate([choose(part, 0.0), choose(0.0, part)], axis=1)
        flat = jnp.concatenate([v.reshape(shards, rows) for v in whole] + [spread], axis=1)
        flat = jnp.pad(flat.astype(BF), ((0, 0), (0, rows * LANES - vector_count)))
        return (flat.reshape(shards * rows, LANES), grads["qkv"], out, grads["up"][0])

    def over_x(value):
        return ring_scatter(value.reshape(RING * RING, RING, quarter, model), "x", 1)

    count = tokens.shape[0]
    seq_lengths = lengths[:, 0]
    weights = [flat_rows(attn_first, up_first, low_first)]
    middle, kept_first = layer_forward(tokens.reshape(-1, model), weights[0], seq_lengths)
    points = (kept_first["attended"], kept_first["activated"][0])
    attn_second = ring_gather(attn_second, "z", 0, *points)
    up_second = ring_gather(up_second, "y", 1, *points)
    low_second = ring_gather(low_second, "x", 1)
    weights.append(flat_rows(attn_second, up_second, low_second))
    last, kept_second = layer_forward(middle, weights[1], seq_lengths)
    grad_middle, grads_second = layer_backward(cotangent.reshape(-1, model), kept_second, weights[1])
    down_second = over_x(grads_second["down"][0])
    pieces = list(zip((0,) + edges, side_by_side(grads_second)))
    side_second = placed(edges[3], pieces)
    grad_middle, side_second = lax.optimization_barrier((grad_middle, side_second))
    side_second = lax.psum_scatter(side_second, "shard", scatter_dimension=0, tiled=True)

    grad_first, grads_first = layer_backward(grad_middle, kept_first, weights[0])
    down_first = over_x(grads_first["down"][0])
    pieces = list(zip((0,) + edges, side_by_side(grads_first)))
    up = pieces[3][1].reshape(RING, RING, rows, -1)
    up = ring_scatter(ring_scatter(up, "y", 1), "z", 0)
    attn = placed(edges[2], pieces[:3]).reshape(RING, RING, rows, -1)
    attn = ring_scatter(ring_scatter(attn, "z", 0), "y", 0)
    down = jnp.stack([down_first, down_second]).reshape(2, RING, RING, quarter, model)
    down = ring_scatter(ring_scatter(down, "z", 1), "y", 1)
    down = ring_gather(down, "x", 1).reshape(2, unit, model)
    side_first = placed(edges[3], [(0, attn), (edges[2], up)])
    side = jnp.stack([side_first, side_second]).reshape(2, RING, rows // RING, -1)
    side = ring_gather(ring_scatter(side, "x", 1), "x", 1).reshape(2, rows, -1)

    summed_first, summed_second = ((side[0], down[0]), (side[1], down[1]))
    mine, sent = zip(*(mine_of(a, b) for a, b in zip(summed_first, summed_second)))
    both = [mine_of(a, swap(b)) for a, b in zip(mine, sent)]
    (side_a, side_b), (down_a, down_b) = [[v.astype(F32) for v in pair] for pair in both]

    def cut(block):
        flat = block[:, :LANES].reshape(-1)[:vector_count]
        qkv = block[:, LANES : edges[1]].reshape(rows, 3, half)
        up = block[:, edges[2] :].reshape(rows, shards, unit)
        return (flat, qkv, block[:, edges[1] : edges[2]], up)

    (flat_a, qkv_a, out_a, up_a), (flat_b, qkv_b, out_b, up_b) = (cut(side_a), cut(side_b))
    flat = flat_a + flat_b
    whole = [flat[n * rows : (n + 1) * rows] for n in range(8)]
    grads = (
        jnp.stack([qkv_a, qkv_b], axis=2).reshape(rows, -1),
        whole[0],
        whole[1],
        jnp.concatenate([out_a, out_b], axis=1),
        whole[2],
        whole[3],
        whole[4],
        jnp.stack([up_a, up_b], axis=2).reshape(rows, -1),
        flat[8 * rows :],
        jnp.concatenate([down_a, down_b], axis=0),
        whole[5],
        whole[6],
        whole[7],
    )
    shape = (1, count, 1, -1, model)
    activations = choose(middle, last).reshape(shape)
    input_grads = choose(grad_first, grad_middle).reshape(shape)
    return (activations, input_grads) + tuple(member[None] for member in grads)


def solution(mesh):
    rows = P(None, ("dp", "shard"), None, None)
    matrix = P("section", "shard", None)
    vector = P("section", "shard")
    weight_specs = (matrix, vector, vector, matrix, vector, vector, vector)
    weight_specs += (matrix, vector, matrix, vector, vector, vector)
    in_specs = (rows, P(None, ("dp", "shard")), rows) + weight_specs
    result = P("section", None, ("dp", "shard"), None, None)
    return jax.shard_map(
        per_device,
        mesh=mesh,
        in_specs=in_specs,
        out_specs=(result, result) + weight_specs,
        check_vma=False,
    )
```

```python
import jax
import jax.numpy as jnp
from jax import lax
from jax.sharding import PartitionSpec as P


HEAD_DIM = 64
EPSILON = 1e-06
TAU = 6.283185307179586
LANES = 128
RING = 4
BF = jnp.bfloat16
F32 = jnp.float32


def swap(value):
    return lax.ppermute(value, "section", [(0, 1), (1, 0)])


def pair_sum(part):
    low = part.astype(BF)
    other = swap(low)
    return low.astype(F32) + other.astype(F32)


def dot(left, right):
    return jnp.dot(left, right, preferred_element_type=F32)


def transpose_dot(left, right):
    return lax.dot_general(left, right, (((0,), (0,)), ((), ())), preferred_element_type=F32)


def dot_transposed(left, right):
    return lax.dot_general(left, right, (((1,), (1,)), ((), ())), preferred_element_type=F32)


def norm_rows(values):
    centered = values - jnp.mean(values, axis=-1, keepdims=True)
    inverse = lax.rsqrt(jnp.mean(centered * centered, axis=-1, keepdims=True) + EPSILON)
    return (centered * inverse, inverse)


def norm_back(grad_norm, normed, inverse):
    return inverse * (
        grad_norm
        - jnp.mean(grad_norm, axis=-1, keepdims=True)
        - normed * jnp.mean(grad_norm * normed, axis=-1, keepdims=True)
    )


def heads_of(packed, number, count):
    width = packed.shape[1] // 3
    piece = packed[:, number * width : (number + 1) * width]
    return piece.reshape(count, -1, width // HEAD_DIM, HEAD_DIM).transpose(0, 2, 1, 3)


def join_heads(parts):
    count, heads, rows, size = parts.shape
    return parts.transpose(0, 2, 1, 3).reshape(count * rows, heads * size)


def masked_scores(queries, keys, seq_lengths):
    scores = jnp.einsum("nhqd,nhkd->nhqk", queries, keys, preferred_element_type=F32)
    scores = scores * HEAD_DIM ** (-0.5)
    positions = lax.broadcasted_iota(jnp.int32, scores.shape, 3)
    return jnp.where(positions < seq_lengths[:, None, None, None], scores, -1000000000.0)


def forward_attention(inputs, weights, seq_lengths):
    count = seq_lengths.shape[0]
    packed = (dot(inputs, weights["qkv"]) + weights["bias_qkv"]).astype(BF)
    queries, keys, values = (heads_of(packed, n, count) for n in range(3))
    scores = masked_scores(queries, keys, seq_lengths)
    row_max = jnp.max(scores, axis=-1, keepdims=True)
    exponent = jnp.exp(scores - row_max)
    soft_weights = exponent / jnp.sum(exponent, axis=-1, keepdims=True)
    attended = jnp.einsum(
        "nhqk,nhkd->nhqd", soft_weights.astype(BF), values, preferred_element_type=F32
    )
    attended = join_heads(attended.astype(BF))
    return (attended, dict(inputs=inputs, qkv=(queries, keys, values), soft_weights=soft_weights))


def forward_hidden(attended, kept, weights):
    branch = pair_sum(dot(attended, weights["out"])) + weights["bias_out"]
    normed, inverse = norm_rows(kept["inputs"].astype(F32) + branch)
    hidden = (normed * weights["gain_attn"] + weights["shift_attn"]).astype(BF)
    upward = dot(hidden, weights["up"]) + weights["bias_up"]
    share = 0.5 + 0.5 * lax.erf(upward * 0.5**0.5)
    activated = (upward * share).astype(BF)
    slope = share + upward * jnp.exp(-0.5 * upward * upward) * TAU ** (-0.5)
    kept.update(attended=attended, normed_attn=normed, inverse_attn=inverse)
    kept.update(hidden=hidden, slope=slope)
    return activated


def forward_output(activated, kept, weights):
    mixed = pair_sum(dot(activated, weights["down"])) + weights["bias_down"]
    normed, inverse = norm_rows(kept["hidden"].astype(F32) + mixed)
    kept.update(activated=activated, normed_mlp=normed, inverse_mlp=inverse)
    return (normed * weights["gain_mlp"] + weights["shift_mlp"]).astype(BF)


def backward_mlp(grad_result, kept, weights):
    grad_result = grad_result.astype(F32)
    normed = kept["normed_mlp"]
    grad_gain = jnp.sum(grad_result * normed, axis=0)
    grad_shift = jnp.sum(grad_result, axis=0)
    grad_resid = norm_back(grad_result * weights["gain_mlp"], normed, kept["inverse_mlp"])
    grad_mixed = grad_resid.astype(BF)
    grad_upward = (dot_transposed(grad_mixed, weights["down"]) * kept["slope"]).astype(BF)
    passed = dot_transposed(grad_upward, weights["up"])
    grads = dict(
        down=transpose_dot(kept["activated"], grad_mixed).astype(BF),
        up=transpose_dot(kept["hidden"], grad_upward).astype(BF),
        bias_up=jnp.sum(grad_upward.astype(F32), axis=0),
        bias_down=jnp.sum(grad_mixed.astype(F32), axis=0),
        gain_mlp=grad_gain,
        shift_mlp=grad_shift,
    )
    return (grad_resid + pair_sum(passed), grads)


def backward_attention(grad_hidden, grads, kept, weights):
    scaling = HEAD_DIM ** (-0.5)
    normed = kept["normed_attn"]
    grad_resid = norm_back(grad_hidden * weights["gain_attn"], normed, kept["inverse_attn"])
    grad_branch = grad_resid.astype(BF)
    grads.update(
        gain_attn=jnp.sum(grad_hidden * normed, axis=0),
        shift_attn=jnp.sum(grad_hidden, axis=0),
        bias_out=jnp.sum(grad_branch.astype(F32), axis=0),
        out=transpose_dot(kept["attended"], grad_branch).astype(BF),
    )
    queries, keys, values = kept["qkv"]
    count = queries.shape[0]
    grad_attended = dot_transposed(grad_branch, weights["out"]).astype(BF)
    grad_attended = grad_attended.reshape(count, -1, queries.shape[1], HEAD_DIM)
    grad_attended = grad_attended.transpose(0, 2, 1, 3)
    soft_weights = kept["soft_weights"]
    grad_values = jnp.einsum(
        "nhqk,nhqd->nhkd", soft_weights.astype(BF), grad_attended, preferred_element_type=F32
    )
    grad_soft = jnp.einsum(
        "nhqd,nhkd->nhqk", grad_attended, values, preferred_element_type=F32
    )
    grad_scores = soft_weights * (
        grad_soft - jnp.sum(grad_soft * soft_weights, axis=-1, keepdims=True)
    )
    grad_scores = grad_scores.astype(BF)
    grad_queries = scaling * jnp.einsum(
        "nhqk,nhkd->nhqd", grad_scores, keys, preferred_element_type=F32
    )
    grad_keys = scaling * jnp.einsum(
        "nhqk,nhqd->nhkd", grad_scores, queries, preferred_element_type=F32
    )
    grad_packed = jnp.concatenate(
        [join_heads(g.astype(BF)) for g in (grad_queries, grad_keys, grad_values)], axis=1
    )
    return (grad_resid, grad_packed)


def backward_inputs(grad_resid, grad_packed, grads, kept, weights):
    columns = jnp.sum(grad_packed.astype(F32), axis=0)
    width = columns.shape[0] // 3
    grads.update(
        bias_q=columns[:width],
        bias_v=columns[2 * width :],
        qkv=transpose_dot(kept["inputs"], grad_packed).astype(BF),
    )
    passed = dot_transposed(grad_packed, weights["qkv"])
    return (grad_resid + pair_sum(passed)).astype(BF)


def per_device(
    tokens,
    lengths,
    cotangent,
    w_qkv,
    bias_q,
    bias_v,
    w_out,
    bias_out,
    gain_attn,
    shift_attn,
    w_up,
    bias_up,
    w_down,
    bias_down,
    gain_mlp,
    shift_mlp,
):
    first = lax.axis_index("section") == 0
    shards = lax.axis_size("shard")
    rows = w_qkv.shape[1]
    model = w_qkv.shape[2] // 3
    ff = w_up.shape[2]
    half = model // 2
    unit = ff // shards // 2
    vector_count = 8 * rows + 2 * unit

    def choose(low, high):
        return jnp.where(first, low, high)

    def mine_of(low, high):
        return (choose(low, high), choose(high, low))

    shard = lax.axis_index("shard")
    place = {"x": lax.axis_index("dp"), "y": shard % RING, "z": shard // RING}

    near = {axis: at ^ choose(1, 3) for axis, at in place.items()}
    far = {axis: at ^ choose(3, 1) for axis, at in place.items()}

    def trade(value, axis, masks):
        name = "dp" if axis == "x" else "shard"
        size = lax.axis_size(name)
        stride = RING if axis == "z" else 1
        route = []
        for core in range(2):
            for at in range(size):
                position = at // stride % RING
                target = at + ((position ^ masks[core]) - position) * stride
                route.append((core * size + at, core * size + target))
        return lax.ppermute(value, ("section", name), route)

    def after(value, earlier):
        return lax.optimization_barrier((value, earlier))[0]

    def put(whole, piece, at, dim):
        start = [0] * whole.ndim
        start[dim] = at
        return lax.dynamic_update_slice(whole, jnp.expand_dims(piece, dim), start)

    def gather_one(block, axis):
        return trade(block, axis, (1, 3))

    def gather_two(block, beside, axis):
        return trade(jnp.stack([block, beside]), axis, (3, 1))

    def gather_end(block, beside, across, axis, dim):
        whole = jnp.zeros(block.shape[:dim] + (RING,) + block.shape[dim:], block.dtype)
        whole = put(whole, block, place[axis], dim)
        whole = put(whole, beside, near[axis], dim)
        whole = put(whole, across[0], far[axis], dim)
        return put(whole, across[1], place[axis] ^ 2, dim)

    def chunk(value, at, dim):
        return lax.dynamic_index_in_dim(value, at, dim, keepdims=False)

    def scatter_one(value, axis, dim):
        sent = [chunk(value, near[axis], dim), chunk(value, place[axis] ^ 2, dim)]
        return trade(jnp.stack(sent), axis, (1, 3))

    def scatter_two(value, beside, axis, dim):
        sent = chunk(value, far[axis], dim).astype(F32) + beside[1].astype(F32)
        return trade(sent.astype(BF), axis, (3, 1))

    def scatter_end(value, beside, across, axis, dim):
        kept = chunk(value, place[axis], dim).astype(F32) + beside[0].astype(F32)
        return (kept + across.astype(F32)).astype(BF)

    def together(*values):
        return lax.optimization_barrier(values)

    def placed(width, pieces):
        whole = jnp.zeros((pieces[0][1].shape[0], width), BF)
        for at, piece in pieces:
            whole = lax.dynamic_update_slice(whole, piece, (0, at))
        return whole

    def parts_of(part):
        qkv = w_qkv[0].reshape(rows, 3, 2, half)[:, :, part].reshape(rows, 3 * half)
        out = w_out[0][:, part * half : (part + 1) * half]
        up = w_up[0].reshape(rows, shards, 2, unit)[:, :, part].reshape(rows, shards * unit)
        return (qkv, out, up, w_down[0][part * unit : (part + 1) * unit])

    vectors = jnp.concatenate(
        [
            v[0]
            for v in (
                bias_q,
                bias_v,
                bias_out,
                gain_attn,
                shift_attn,
                bias_down,
                gain_mlp,
                shift_mlp,
                bias_up,
            )
        ]
    )
    vectors = jnp.pad(vectors, (0, rows * LANES - vector_count)).reshape(rows, LANES)
    split = [mine_of(low, high) for low, high in zip(parts_of(0), parts_of(1))]
    kept_part = (vectors,) + tuple(low for low, high in split)
    sent_part = (vectors,) + tuple(high for low, high in split)
    got_part = tuple(swap(member) for member in sent_part)
    blocks = [mine_of(own, got) for own, got in zip(kept_part, got_part)]
    edges = (LANES, LANES + 3 * half, LANES + 4 * half, LANES + 4 * half + shards * unit)

    def joined(layer, count):
        return placed(edges[count - 1], list(zip((0,) + edges, [b[layer] for b in blocks[:count]])))

    quarter = unit // RING

    def quarter_of(block):
        return chunk(block.reshape(RING, quarter, model), place["x"], 0)

    a0, b0, c0 = (joined(0, 3), blocks[3][0], quarter_of(blocks[4][0]))
    a1, b1, c1 = (joined(1, 3), blocks[3][1], quarter_of(blocks[4][1]))
    an, bn, cn = together(gather_one(a0, "y"), gather_one(b0, "z"), gather_one(c0, "y"))
    af, bf, cf = together(
        gather_two(a0, an, "y"), gather_two(b0, bn, "z"), gather_two(c0, cn, "y")
    )
    a0 = gather_end(a0, an, af, "y", 0)
    b0 = gather_end(b0, bn, bf, "z", 0)
    c0 = gather_end(c0, cn, cf, "y", 0)
    an0, bn0, cn0 = together(gather_one(a0, "z"), gather_one(b0, "y"), gather_one(c0, "z"))
    af0, bf0, cf0 = (
        gather_two(a0, an0, "z"),
        gather_two(b0, bn0, "y"),
        gather_two(c0, cn0, "z"),
    )
    a1, b1, c1 = (after(a1, an0), after(b1, an0), after(c1, an0))
    an, bn, cn = together(gather_one(a1, "y"), gather_one(b1, "z"), gather_one(c1, "z"))
    af, bf, cf = together(
        gather_two(a1, an, "y"), gather_two(b1, bn, "z"), gather_two(c1, cn, "z")
    )
    c1 = gather_end(c1, cn, cf, "z", 0)
    cn1 = gather_one(c1, "y")
    cf1 = gather_two(c1, cn1, "y")
    a1 = gather_end(a1, an, af, "y", 0)
    b1 = gather_end(b1, bn, bf, "z", 0)
    af0, bf0, cf0, cf1 = together(af0, bf0, cf0, cf1)
    a0 = gather_end(a0, an0, af0, "z", 0)
    b0 = gather_end(b0, bn0, bf0, "y", 1)
    c0 = gather_end(c0, cn0, cf0, "z", 0).reshape(shards, quarter, model)
    c1 = gather_end(c1, cn1, cf1, "y", 1).reshape(shards, quarter, model)
    a1, b1 = (after(a1, af0), after(b1, bf0))

    def arranged(attn, up):
        attn, up = (attn.reshape(model, -1), up.reshape(model, -1))
        flat = attn[:, :LANES].reshape(shards, rows * LANES)[:, :vector_count].astype(F32)
        whole = [flat[:, n * rows : (n + 1) * rows].reshape(-1) for n in range(8)]
        bias_up_part = flat[:, 8 * rows :].reshape(shards, 2, unit)
        bias_up_part = choose(bias_up_part[:, 0], bias_up_part[:, 1]).reshape(-1)
        bias_q_part = choose(whole[0][:half], whole[0][half:])
        bias_v_part = choose(whole[1][:half], whole[1][half:])
        out = attn[:, edges[1] : edges[2]]
        held, handed = mine_of(out[:half], out[half:])
        arrived = swap(handed)
        return dict(
            qkv=attn[:, LANES : edges[1]],
            out=jnp.concatenate(mine_of(held, arrived), axis=1),
            up=up,
            bias_qkv=jnp.concatenate([bias_q_part, jnp.zeros_like(bias_q_part), bias_v_part]),
            bias_out=whole[2],
            gain_attn=whole[3],
            shift_attn=whole[4],
            bias_down=whole[5],
            gain_mlp=whole[6],
            shift_mlp=whole[7],
            bias_up=bias_up_part,
        )

    def side_by_side(grads):
        held, handed = mine_of(grads["out"][:, :half], grads["out"][:, half:])
        out = jnp.concatenate(mine_of(held, swap(handed)), axis=0)

        def widened(part):
            return jnp.concatenate([choose(part, 0.0), choose(0.0, part)])

        whole = [widened(grads["bias_q"]), widened(grads["bias_v"])]
        names = ("bias_out", "gain_attn", "shift_attn", "bias_down", "gain_mlp", "shift_mlp")
        whole += [0.5 * grads[name] for name in names]
        part = grads["bias_up"].reshape(shards, unit)
        spread = jnp.concatenate([choose(part, 0.0), choose(0.0, part)], axis=1)
        flat = jnp.concatenate([v.reshape(shards, rows) for v in whole] + [spread], axis=1)
        flat = jnp.pad(flat.astype(BF), ((0, 0), (0, rows * LANES - vector_count)))
        pieces = (flat.reshape(shards * rows, LANES), grads["qkv"], out)
        return placed(edges[2], list(zip((0,) + edges, pieces))).reshape(RING, RING, rows, -1)

    count = tokens.shape[0]
    seq_lengths = lengths[:, 0]

    first_weights = arranged(a0, b0)
    an, bn, cn = (gather_one(a1, "z"), gather_one(b1, "y"), gather_one(c0, "x"))
    attended, kept0 = forward_attention(tokens.reshape(-1, model), first_weights, seq_lengths)
    an, bn, cn, attended = together(an, bn, cn, attended)
    af, bf, cf = (gather_two(a1, an, "z"), gather_two(b1, bn, "y"), gather_two(c0, cn, "x"))
    activated = forward_hidden(attended, kept0, first_weights)
    af, bf, cf, activated = together(af, bf, cf, activated)
    first_weights["down"] = gather_end(c0, cn, cf, "x", 1).reshape(-1, model)
    cn = gather_one(after(c1, cf), "x")
    middle = forward_output(activated, kept0, first_weights)
    cn, middle = together(cn, middle)
    cf = gather_two(c1, cn, "x")
    second_weights = arranged(
        gather_end(a1, an, af, "z", 0), gather_end(b1, bn, bf, "y", 1)
    )
    attended, kept1 = forward_attention(middle, second_weights, seq_lengths)
    activated = forward_hidden(attended, kept1, second_weights)
    cf, activated = together(cf, activated)
    second_weights["down"] = gather_end(c1, cn, cf, "x", 1).reshape(-1, model)
    last = forward_output(activated, kept1, second_weights)

    def down_of(grads):
        return grads["down"].reshape(shards, RING, quarter, model)

    def up_of(grads):
        return grads["up"].reshape(RING, RING, rows, -1)

    grad_hidden, grads1 = backward_mlp(cotangent.reshape(-1, model), kept1, second_weights)
    c1, b1 = (down_of(grads1), up_of(grads1))
    cn, bn = (scatter_one(c1, "x", 1), scatter_one(b1, "y", 1))
    grad_resid, grad_packed = backward_attention(grad_hidden, grads1, kept1, second_weights)
    cn, bn, grad_packed = together(cn, bn, grad_packed)
    cf, bf = (scatter_two(c1, cn, "x", 1), scatter_two(b1, bn, "y", 1))
    grad_middle = backward_inputs(grad_resid, grad_packed, grads1, kept1, second_weights)
    a1 = side_by_side(grads1)
    a1, cf, bf, grad_middle = together(a1, cf, bf, grad_middle)
    c1, b1 = (scatter_end(c1, cn, cf, "x", 1), scatter_end(b1, bn, bf, "y", 1))
    an1 = scatter_one(a1, "z", 0)

    grad_hidden, grads0 = backward_mlp(grad_middle, kept0, first_weights)
    c0, b0 = (down_of(grads0), up_of(grads0))
    cn, bn = (scatter_one(c0, "x", 1), scatter_one(b0, "y", 1))
    an1, grad_hidden = together(an1, grad_hidden)
    af1 = scatter_two(a1, an1, "z", 0)
    grad_resid, grad_packed = backward_attention(grad_hidden, grads0, kept0, first_weights)
    af1, cn, bn, grad_packed = together(af1, cn, bn, grad_packed)
    a1 = scatter_end(a1, an1, af1, "z", 0)
    cf, bf = (scatter_two(c0, cn, "x", 1), scatter_two(b0, bn, "y", 1))
    grad_first = backward_inputs(grad_resid, grad_packed, grads0, kept0, first_weights)
    a0 = side_by_side(grads0)
    a0, cf, bf = together(a0, cf, bf)
    c0, b0 = (scatter_end(c0, cn, cf, "x", 1), scatter_end(b0, bn, bf, "y", 1))

    b = jnp.stack([b0, b1]).reshape(2, RING, RING, rows // RING, -1)
    c = jnp.stack([c0, c1]).reshape(2, RING, RING, quarter, model)
    an, bn, cn, dn = together(
        scatter_one(a0, "z", 0), scatter_one(b, "x", 2), scatter_one(c, "y", 2), scatter_one(a1, "y", 0)
    )
    af, bf, cf, df = together(
        scatter_two(a0, an, "z", 0),
        scatter_two(b, bn, "x", 2),
        scatter_two(c, cn, "y", 2),
        scatter_two(a1, dn, "y", 0),
    )
    a0 = scatter_end(a0, an, af, "z", 0)
    a1 = scatter_end(a1, dn, df, "y", 0).reshape(RING, rows // RING, -1)
    b, c = (scatter_end(b, bn, bf, "x", 2), scatter_end(c, cn, cf, "y", 2))
    an, bn, cn, dn = together(
        scatter_one(a0, "y", 0), scatter_one(b, "z", 1), scatter_one(c, "z", 1), scatter_one(a1, "x", 0)
    )
    af, bf, cf, df = together(
        scatter_two(a0, an, "y", 0),
        scatter_two(b, bn, "z", 1),
        scatter_two(c, cn, "z", 1),
        scatter_two(a1, dn, "x", 0),
    )
    a0 = scatter_end(a0, an, af, "y", 0).reshape(RING, rows // RING, -1)
    a1 = scatter_end(a1, dn, df, "x", 0)
    b, c = (scatter_end(b, bn, bf, "z", 1), scatter_end(c, cn, cf, "z", 1))
    c = c.reshape(2, rows // RING, -1)
    bc = jnp.concatenate([b, c], axis=2)
    an, bn = together(scatter_one(a0, "x", 0), gather_one(bc, "x"))
    af, bf = together(scatter_two(a0, an, "x", 0), gather_two(bc, bn, "x"))
    a = jnp.stack([scatter_end(a0, an, af, "x", 0), a1])
    bc = gather_end(bc, bn, bf, "x", 1)
    b = bc[..., : b.shape[2]].reshape(2, rows, -1)
    c = bc[..., b.shape[2] :].reshape(2, unit, model)
    an = gather_one(a, "x")
    af = gather_two(a, an, "x")
    a = gather_end(a, an, af, "x", 1).reshape(2, rows, -1)

    summed_first, summed_second = ((a[0], b[0], c[0]), (a[1], b[1], c[1]))
    mine, sent = zip(*(mine_of(a, b) for a, b in zip(summed_first, summed_second)))
    both = [mine_of(a, swap(b)) for a, b in zip(mine, sent)]
    both = [[v.astype(F32) for v in pair] for pair in both]
    (side_a, side_b), (up_a, up_b), (down_a, down_b) = both

    def cut(block):
        flat = block[:, :LANES].reshape(-1)[:vector_count]
        return (flat, block[:, LANES : edges[1]].reshape(rows, 3, half), block[:, edges[1] :])

    (flat_a, qkv_a, out_a), (flat_b, qkv_b, out_b) = (cut(side_a), cut(side_b))
    up_a, up_b = (up_a.reshape(rows, shards, unit), up_b.reshape(rows, shards, unit))
    flat = flat_a + flat_b
    whole = [flat[n * rows : (n + 1) * rows] for n in range(8)]
    grads = (
        jnp.stack([qkv_a, qkv_b], axis=2).reshape(rows, -1),
        whole[0],
        whole[1],
        jnp.concatenate([out_a, out_b], axis=1),
        whole[2],
        whole[3],
        whole[4],
        jnp.stack([up_a, up_b], axis=2).reshape(rows, -1),
        flat[8 * rows :],
        jnp.concatenate([down_a, down_b], axis=0),
        whole[5],
        whole[6],
        whole[7],
    )
    shape = (1, count, 1, -1, model)
    activations = choose(middle, last).reshape(shape)
    input_grads = choose(grad_first, grad_middle).reshape(shape)
    return (activations, input_grads) + tuple(member[None] for member in grads)


def solution(mesh):
    rows = P(None, ("dp", "shard"), None, None)
    matrix = P("section", "shard", None)
    vector = P("section", "shard")
    weight_specs = (matrix, vector, vector, matrix, vector, vector, vector)
    weight_specs += (matrix, vector, matrix, vector, vector, vector)
    in_specs = (rows, P(None, ("dp", "shard")), rows) + weight_specs
    result = P("section", None, ("dp", "shard"), None, None)
    return jax.shard_map(
        per_device,
        mesh=mesh,
        in_specs=in_specs,
        out_specs=(result, result) + weight_specs,
        check_vma=False,
    )
```

```python
import jax
import jax.numpy as jnp
from jax import lax
from jax.sharding import PartitionSpec as P


HEAD_DIM = 64
EPSILON = 1e-06
TAU = 6.283185307179586
LANES = 128
RING = 4
BF = jnp.bfloat16
F32 = jnp.float32


def swap(value):
    return lax.ppermute(value, "section", [(0, 1), (1, 0)])


def pair_sum(part):
    low = part.astype(BF)
    other = swap(low)
    return low.astype(F32) + other.astype(F32)


def dot(left, right):
    return jnp.dot(left, right, preferred_element_type=F32)


def transpose_dot(left, right):
    return lax.dot_general(left, right, (((0,), (0,)), ((), ())), preferred_element_type=F32)


def dot_transposed(left, right):
    return lax.dot_general(left, right, (((1,), (1,)), ((), ())), preferred_element_type=F32)


def norm_rows(values):
    centered = values - jnp.mean(values, axis=-1, keepdims=True)
    inverse = lax.rsqrt(jnp.mean(centered * centered, axis=-1, keepdims=True) + EPSILON)
    return (centered * inverse, inverse)


def norm_back(grad_norm, normed, inverse):
    return inverse * (
        grad_norm
        - jnp.mean(grad_norm, axis=-1, keepdims=True)
        - normed * jnp.mean(grad_norm * normed, axis=-1, keepdims=True)
    )


def heads_of(packed, number, count):
    width = packed.shape[1] // 3
    piece = packed[:, number * width : (number + 1) * width]
    return piece.reshape(count, -1, width // HEAD_DIM, HEAD_DIM).transpose(0, 2, 1, 3)


def join_heads(parts):
    count, heads, rows, size = parts.shape
    return parts.transpose(0, 2, 1, 3).reshape(count * rows, heads * size)


def masked_scores(queries, keys, seq_lengths):
    scores = jnp.einsum("nhqd,nhkd->nhqk", queries, keys, preferred_element_type=F32)
    scores = scores * HEAD_DIM ** (-0.5)
    positions = lax.broadcasted_iota(jnp.int32, scores.shape, 3)
    return jnp.where(positions < seq_lengths[:, None, None, None], scores, -1000000000.0)


def forward_attention(inputs, weights, seq_lengths):
    count = seq_lengths.shape[0]
    packed = (dot(inputs, weights["qkv"]) + weights["bias_qkv"]).astype(BF)
    queries, keys, values = (heads_of(packed, n, count) for n in range(3))
    scores = masked_scores(queries, keys, seq_lengths)
    row_max = jnp.max(scores, axis=-1, keepdims=True)
    exponent = jnp.exp(scores - row_max)
    soft_weights = exponent / jnp.sum(exponent, axis=-1, keepdims=True)
    attended = jnp.einsum(
        "nhqk,nhkd->nhqd", soft_weights.astype(BF), values, preferred_element_type=F32
    )
    attended = join_heads(attended.astype(BF))
    return (attended, dict(inputs=inputs, qkv=(queries, keys, values), soft_weights=soft_weights))


def forward_hidden(attended, kept, weights):
    branch = pair_sum(dot(attended, weights["out"])) + weights["bias_out"]
    normed, inverse = norm_rows(kept["inputs"].astype(F32) + branch)
    hidden = (normed * weights["gain_attn"] + weights["shift_attn"]).astype(BF)
    upward = dot(hidden, weights["up"]) + weights["bias_up"]
    share = 0.5 + 0.5 * lax.erf(upward * 0.5**0.5)
    activated = (upward * share).astype(BF)
    slope = share + upward * jnp.exp(-0.5 * upward * upward) * TAU ** (-0.5)
    kept.update(attended=attended, normed_attn=normed, inverse_attn=inverse)
    kept.update(hidden=hidden, slope=slope)
    return activated


def forward_output(activated, kept, weights):
    mixed = pair_sum(dot(activated, weights["down"])) + weights["bias_down"]
    normed, inverse = norm_rows(kept["hidden"].astype(F32) + mixed)
    kept.update(activated=activated, normed_mlp=normed, inverse_mlp=inverse)
    return (normed * weights["gain_mlp"] + weights["shift_mlp"]).astype(BF)


def backward_mlp(grad_result, kept, weights):
    grad_result = grad_result.astype(F32)
    normed = kept["normed_mlp"]
    grad_gain = jnp.sum(grad_result * normed, axis=0)
    grad_shift = jnp.sum(grad_result, axis=0)
    grad_resid = norm_back(grad_result * weights["gain_mlp"], normed, kept["inverse_mlp"])
    grad_mixed = grad_resid.astype(BF)
    grad_upward = (dot_transposed(grad_mixed, weights["down"]) * kept["slope"]).astype(BF)
    passed = dot_transposed(grad_upward, weights["up"])
    grads = dict(
        down=transpose_dot(kept["activated"], grad_mixed).astype(BF),
        up=transpose_dot(kept["hidden"], grad_upward).astype(BF),
        bias_up=jnp.sum(grad_upward.astype(F32), axis=0),
        bias_down=jnp.sum(grad_mixed.astype(F32), axis=0),
        gain_mlp=grad_gain,
        shift_mlp=grad_shift,
    )
    return (grad_resid + pair_sum(passed), grads)


def backward_attention(grad_hidden, grads, kept, weights):
    scaling = HEAD_DIM ** (-0.5)
    normed = kept["normed_attn"]
    grad_resid = norm_back(grad_hidden * weights["gain_attn"], normed, kept["inverse_attn"])
    grad_branch = grad_resid.astype(BF)
    grads.update(
        gain_attn=jnp.sum(grad_hidden * normed, axis=0),
        shift_attn=jnp.sum(grad_hidden, axis=0),
        bias_out=jnp.sum(grad_branch.astype(F32), axis=0),
        out=transpose_dot(kept["attended"], grad_branch).astype(BF),
    )
    queries, keys, values = kept["qkv"]
    count = queries.shape[0]
    grad_attended = dot_transposed(grad_branch, weights["out"]).astype(BF)
    grad_attended = grad_attended.reshape(count, -1, queries.shape[1], HEAD_DIM)
    grad_attended = grad_attended.transpose(0, 2, 1, 3)
    soft_weights = kept["soft_weights"]
    grad_values = jnp.einsum(
        "nhqk,nhqd->nhkd", soft_weights.astype(BF), grad_attended, preferred_element_type=F32
    )
    grad_soft = jnp.einsum(
        "nhqd,nhkd->nhqk", grad_attended, values, preferred_element_type=F32
    )
    grad_scores = soft_weights * (
        grad_soft - jnp.sum(grad_soft * soft_weights, axis=-1, keepdims=True)
    )
    grad_scores = grad_scores.astype(BF)
    grad_queries = scaling * jnp.einsum(
        "nhqk,nhkd->nhqd", grad_scores, keys, preferred_element_type=F32
    )
    grad_keys = scaling * jnp.einsum(
        "nhqk,nhqd->nhkd", grad_scores, queries, preferred_element_type=F32
    )
    grad_packed = jnp.concatenate(
        [join_heads(g.astype(BF)) for g in (grad_queries, grad_keys, grad_values)], axis=1
    )
    return (grad_resid, grad_packed)


def backward_inputs(grad_resid, grad_packed, grads, kept, weights):
    columns = jnp.sum(grad_packed.astype(F32), axis=0)
    width = columns.shape[0] // 3
    grads.update(
        bias_q=columns[:width],
        bias_v=columns[2 * width :],
        qkv=transpose_dot(kept["inputs"], grad_packed).astype(BF),
    )
    passed = dot_transposed(grad_packed, weights["qkv"])
    return (grad_resid + pair_sum(passed)).astype(BF)


def per_device(
    tokens,
    lengths,
    cotangent,
    w_qkv,
    bias_q,
    bias_v,
    w_out,
    bias_out,
    gain_attn,
    shift_attn,
    w_up,
    bias_up,
    w_down,
    bias_down,
    gain_mlp,
    shift_mlp,
):
    first = lax.axis_index("section") == 0
    shards = lax.axis_size("shard")
    rows = w_qkv.shape[1]
    model = w_qkv.shape[2] // 3
    ff = w_up.shape[2]
    half = model // 2
    unit = ff // shards // 2

    def choose(low, high):
        return jnp.where(first, low, high)

    def mine_of(low, high):
        return (choose(low, high), choose(high, low))

    shard = lax.axis_index("shard")
    place = {"x": lax.axis_index("dp"), "y": shard % RING, "z": shard // RING}

    near = {axis: at ^ choose(1, 3) for axis, at in place.items()}
    far = {axis: at ^ choose(3, 1) for axis, at in place.items()}

    def trade(value, axis, masks):
        name = "dp" if axis == "x" else "shard"
        size = lax.axis_size(name)
        stride = RING if axis == "z" else 1
        route = []
        for core in range(2):
            for at in range(size):
                position = at // stride % RING
                target = at + ((position ^ masks[core]) - position) * stride
                route.append((core * size + at, core * size + target))
        return lax.ppermute(value, ("section", name), route)

    def after(value, earlier):
        return lax.optimization_barrier((value, earlier))[0]

    def hop(value, distance):
        route = [(at, (at + distance) % RING) for at in range(RING)]
        return lax.ppermute(value, "dp", route)

    def put(whole, piece, at, dim):
        start = [0] * whole.ndim
        start[dim] = at
        return lax.dynamic_update_slice(whole, jnp.expand_dims(piece, dim), start)

    def gather_one(block, axis):
        return trade(block, axis, (1, 3))

    def gather_two(block, beside, axis):
        return trade(jnp.stack([block, beside]), axis, (3, 1))

    def gather_end(block, beside, across, axis, dim):
        whole = jnp.zeros(block.shape[:dim] + (RING,) + block.shape[dim:], block.dtype)
        whole = put(whole, block, place[axis], dim)
        whole = put(whole, beside, near[axis], dim)
        whole = put(whole, across[0], far[axis], dim)
        return put(whole, across[1], place[axis] ^ 2, dim)

    def chunk(value, at, dim):
        return lax.dynamic_index_in_dim(value, at, dim, keepdims=False)

    def scatter_one(value, axis, dim):
        sent = [chunk(value, near[axis], dim), chunk(value, place[axis] ^ 2, dim)]
        return trade(jnp.stack(sent), axis, (1, 3))

    def scatter_two(value, beside, axis, dim):
        sent = chunk(value, far[axis], dim).astype(F32) + beside[1].astype(F32)
        return trade(sent.astype(BF), axis, (3, 1))

    def scatter_end(value, beside, across, axis, dim):
        kept = chunk(value, place[axis], dim).astype(F32) + beside[0].astype(F32)
        return (kept + across.astype(F32)).astype(BF)

    def together(*values):
        return lax.optimization_barrier(values)

    def placed(width, pieces):
        whole = jnp.zeros((pieces[0][1].shape[0], width), BF)
        for at, piece in pieces:
            whole = lax.dynamic_update_slice(whole, piece, (0, at))
        return whole

    def parts_of(part):
        qkv = w_qkv[0].reshape(rows, 3, 2, half)[:, :, part].reshape(rows, 3 * half)
        out = w_out[0][:, part * half : (part + 1) * half]
        up = w_up[0].reshape(rows, shards, 2, unit)[:, :, part].reshape(rows, shards * unit)
        return (qkv, out, up, w_down[0][part * unit : (part + 1) * unit])

    lines = [
        v.reshape(-1, rows)
        for v in (
            bias_q,
            bias_v,
            bias_out,
            gain_attn,
            shift_attn,
            bias_down,
            gain_mlp,
            shift_mlp,
            bias_up,
        )
    ]
    vectors, at = (jnp.zeros((rows, LANES), BF), 0)
    for line in lines:
        height = line.shape[0]
        vectors += jnp.pad(line, ((at, rows - at - height), (0, LANES - rows)))
        at += height
    vector_rows = at
    split = [mine_of(low, high) for low, high in zip(parts_of(0), parts_of(1))]
    kept_part = (vectors,) + tuple(low for low, high in split)
    sent_part = (vectors,) + tuple(high for low, high in split)
    got_part = tuple(swap(member) for member in sent_part)
    blocks = [mine_of(own, got) for own, got in zip(kept_part, got_part)]
    edges = (LANES, LANES + 3 * half, LANES + 4 * half, LANES + 4 * half + shards * unit)

    side = []
    for layer in range(2):
        side += [(layer * edges[3] + at, b[layer]) for at, b in zip((0,) + edges, blocks[:4])]
    side = placed(2 * edges[3], side)

    quarter = unit // RING

    def quarter_of(block):
        return chunk(block.reshape(RING, quarter, model), place["x"], 0)

    c = jnp.stack([quarter_of(block) for block in blocks[4]])
    cn = gather_one(c, "y")
    c = gather_end(c, cn, gather_two(c, cn, "y"), "y", 1)
    cn = gather_one(c, "z")
    c = gather_end(c, cn, gather_two(c, cn, "z"), "z", 1).reshape(2, shards, quarter, model)
    cn = gather_one(c, "x")
    c = gather_end(c, cn, gather_two(c, cn, "x"), "x", 2).reshape(2, -1, model)

    side = lax.all_gather(side, "shard", axis=0, tiled=True)
    sides = [side[:, layer * edges[3] : (layer + 1) * edges[3]] for layer in range(2)]

    def arranged(attn, down):
        flat = attn[:, :LANES].reshape(shards, rows, LANES)[:, :vector_rows, :rows].astype(F32)
        whole = [flat[:, n].reshape(-1) for n in range(8)]
        bias_up_part = flat[:, 8:].reshape(shards, 2, unit)
        bias_up_part = choose(bias_up_part[:, 0], bias_up_part[:, 1]).reshape(-1)
        bias_q_part = choose(whole[0][:half], whole[0][half:])
        bias_v_part = choose(whole[1][:half], whole[1][half:])
        out = attn[:, edges[1] : edges[2]]
        held, handed = mine_of(out[:half], out[half:])
        arrived = swap(handed)
        return dict(
            qkv=attn[:, LANES : edges[1]],
            out=jnp.concatenate(mine_of(held, arrived), axis=1),
            up=attn[:, edges[2] :],
            down=down,
            bias_qkv=jnp.concatenate([bias_q_part, jnp.zeros_like(bias_q_part), bias_v_part]),
            bias_out=whole[2],
            gain_attn=whole[3],
            shift_attn=whole[4],
            bias_down=whole[5],
            gain_mlp=whole[6],
            shift_mlp=whole[7],
            bias_up=bias_up_part,
        )

    def side_by_side(grads):
        held, handed = mine_of(grads["out"][:, :half], grads["out"][:, half:])
        out = jnp.concatenate(mine_of(held, swap(handed)), axis=0)

        def widened(part):
            return jnp.concatenate([choose(part, 0.0), choose(0.0, part)])

        whole = [widened(grads["bias_q"]), widened(grads["bias_v"])]
        names = ("bias_out", "gain_attn", "shift_attn", "bias_down", "gain_mlp", "shift_mlp")
        whole += [0.5 * grads[name] for name in names]
        part = grads["bias_up"].reshape(shards, unit)
        spread = jnp.concatenate([choose(part, 0.0), choose(0.0, part)], axis=1)
        flat = [v.reshape(shards, 1, rows) for v in whole] + [spread.reshape(shards, -1, rows)]
        flat = jnp.concatenate(flat, axis=1).astype(BF)
        flat = jnp.pad(flat, ((0, 0), (0, rows - vector_rows), (0, LANES - rows)))
        return (flat.reshape(shards * rows, LANES), grads["qkv"], out)

    count = tokens.shape[0]
    seq_lengths = lengths[:, 0]

    first_weights = arranged(sides[0], c[0])
    attended, kept0 = forward_attention(tokens.reshape(-1, model), first_weights, seq_lengths)
    activated = forward_hidden(attended, kept0, first_weights)
    middle = forward_output(activated, kept0, first_weights)
    second_weights = arranged(sides[1], c[1])
    attended, kept1 = forward_attention(middle, second_weights, seq_lengths)
    activated = forward_hidden(attended, kept1, second_weights)
    last = forward_output(activated, kept1, second_weights)

    def down_of(grads):
        return grads["down"].reshape(shards, RING, quarter, model)

    grad_hidden, grads1 = backward_mlp(cotangent.reshape(-1, model), kept1, second_weights)
    c1 = down_of(grads1)
    cn = scatter_one(c1, "x", 1)
    grad_resid, grad_packed = backward_attention(grad_hidden, grads1, kept1, second_weights)
    cn, grad_packed = together(cn, grad_packed)
    cf = scatter_two(c1, cn, "x", 1)
    grad_middle = backward_inputs(grad_resid, grad_packed, grads1, kept1, second_weights)
    pieces = side_by_side(grads1) + (grads1["up"],)
    side1 = placed(edges[3], list(zip((0,) + edges, pieces)))
    side1, cf, grad_middle = together(side1, cf, grad_middle)
    side1 = lax.psum_scatter(side1, "shard", scatter_dimension=0, tiled=True)
    c1 = scatter_end(c1, cn, cf, "x", 1)

    grad_hidden, grads0 = backward_mlp(grad_middle, kept0, first_weights)
    c0, b0 = (down_of(grads0), grads0["up"].reshape(RING, RING, rows, -1))
    cn, bn = (scatter_one(c0, "x", 1), scatter_one(b0, "y", 1))
    grad_resid, grad_packed = backward_attention(grad_hidden, grads0, kept0, first_weights)
    cn, bn, grad_packed = together(cn, bn, grad_packed)
    cf, bf = (scatter_two(c0, cn, "x", 1), scatter_two(b0, bn, "y", 1))
    grad_first = backward_inputs(grad_resid, grad_packed, grads0, kept0, first_weights)
    a0 = placed(edges[2], list(zip((0,) + edges, side_by_side(grads0))))
    a0 = a0.reshape(RING, RING, rows, -1)
    a0, cf, bf = together(a0, cf, bf)
    c0, b0 = (scatter_end(c0, cn, cf, "x", 1), scatter_end(b0, bn, bf, "y", 1))

    b = b0.reshape(RING, RING, rows // RING, -1)
    c = jnp.stack([c0, c1]).reshape(2, RING, RING, quarter, model)
    an, bn, cn = together(scatter_one(a0, "z", 0), scatter_one(b, "x", 1), scatter_one(c, "y", 2))
    af, bf, cf, side1 = together(
        scatter_two(a0, an, "z", 0), scatter_two(b, bn, "x", 1), scatter_two(c, cn, "y", 2), side1
    )
    side1 = side1.reshape(RING, rows // RING, -1)
    a0 = scatter_end(a0, an, af, "z", 0)
    b, c = (scatter_end(b, bn, bf, "x", 1), scatter_end(c, cn, cf, "y", 2))
    an, bn, cn, dn = together(
        scatter_one(a0, "y", 0), scatter_one(b, "z", 0), scatter_one(c, "z", 1), scatter_one(side1, "x", 0)
    )
    af, bf, cf, df = together(
        scatter_two(a0, an, "y", 0),
        scatter_two(b, bn, "z", 0),
        scatter_two(c, cn, "z", 1),
        scatter_two(side1, dn, "x", 0),
    )
    a0 = scatter_end(a0, an, af, "y", 0)
    b, c = (scatter_end(b, bn, bf, "z", 0), scatter_end(c, cn, cf, "z", 1))
    side1 = scatter_end(side1, dn, df, "x", 0)
    wide = b.shape[1]
    bc = jnp.concatenate([b, c[0].reshape(b.shape), c[1].reshape(b.shape), side1], axis=1)
    bn = gather_one(bc, "x")
    others = [hop(a0, n) for n in range(1, RING)]
    bn, others = together(bn, others)
    a0 = a0.astype(F32) + sum(other.astype(F32) for other in others)
    bc = gather_end(bc, bn, gather_two(bc, bn, "x"), "x", 0).reshape(rows, -1)
    b0, side1 = (bc[:, :wide], bc[:, 3 * wide :])
    c0, c1 = (bc[:, n * wide : (n + 1) * wide].reshape(unit, model) for n in (1, 2))

    summed_first = (a0.astype(BF), b0, c0)
    summed_second = (side1[:, : edges[2]], side1[:, edges[2] :], c1)
    mine, sent = zip(*(mine_of(a, b) for a, b in zip(summed_first, summed_second)))
    both = [mine_of(a, swap(b)) for a, b in zip(mine, sent)]
    both = [[v.astype(F32) for v in pair] for pair in both]
    (side_a, side_b), (up_a, up_b), (down_a, down_b) = both

    def cut(block):
        flat = block[:vector_rows, :rows]
        return (flat, block[:, LANES : edges[1]].reshape(rows, 3, half), block[:, edges[1] :])

    (flat_a, qkv_a, out_a), (flat_b, qkv_b, out_b) = (cut(side_a), cut(side_b))
    up_a, up_b = (up_a.reshape(rows, shards, unit), up_b.reshape(rows, shards, unit))
    flat = flat_a + flat_b
    whole = [flat[n] for n in range(8)]
    grads = (
        jnp.stack([qkv_a, qkv_b], axis=2).reshape(rows, -1),
        whole[0],
        whole[1],
        jnp.concatenate([out_a, out_b], axis=1),
        whole[2],
        whole[3],
        whole[4],
        jnp.stack([up_a, up_b], axis=2).reshape(rows, -1),
        flat[8:].reshape(-1),
        jnp.concatenate([down_a, down_b], axis=0),
        whole[5],
        whole[6],
        whole[7],
    )
    shape = (1, count, 1, -1, model)
    activations = choose(middle, last).reshape(shape)
    input_grads = choose(grad_first, grad_middle).reshape(shape)
    return (activations, input_grads) + tuple(member[None] for member in grads)


def solution(mesh):
    rows = P(None, ("dp", "shard"), None, None)
    matrix = P("section", "shard", None)
    vector = P("section", "shard")
    weight_specs = (matrix, vector, vector, matrix, vector, vector, vector)
    weight_specs += (matrix, vector, matrix, vector, vector, vector)
    in_specs = (rows, P(None, ("dp", "shard")), rows) + weight_specs
    result = P("section", None, ("dp", "shard"), None, None)
    return jax.shard_map(
        per_device,
        mesh=mesh,
        in_specs=in_specs,
        out_specs=(result, result) + weight_specs,
        check_vma=False,
    )
```

```python
import jax
import jax.numpy as jnp
from jax import lax
from jax.sharding import PartitionSpec as P


HEAD_DIM = 64
EPSILON = 1e-06
TAU = 6.283185307179586
LANES = 128
RING = 4
BF = jnp.bfloat16
F32 = jnp.float32


def swap(value):
    return lax.ppermute(value, "section", [(0, 1), (1, 0)])


def pair_sum(part):
    low = part.astype(BF)
    other = swap(low)
    return low.astype(F32) + other.astype(F32)


def dot(left, right):
    return jnp.dot(left, right, preferred_element_type=F32)


def transpose_dot(left, right):
    return lax.dot_general(left, right, (((0,), (0,)), ((), ())), preferred_element_type=F32)


def dot_transposed(left, right):
    return lax.dot_general(left, right, (((1,), (1,)), ((), ())), preferred_element_type=F32)


def norm_rows(values):
    centered = values - jnp.mean(values, axis=-1, keepdims=True)
    inverse = lax.rsqrt(jnp.mean(centered * centered, axis=-1, keepdims=True) + EPSILON)
    return (centered * inverse, inverse)


def norm_back(grad_norm, normed, inverse):
    return inverse * (
        grad_norm
        - jnp.mean(grad_norm, axis=-1, keepdims=True)
        - normed * jnp.mean(grad_norm * normed, axis=-1, keepdims=True)
    )


def heads_of(packed, number, count):
    width = packed.shape[1] // 3
    piece = packed[:, number * width : (number + 1) * width]
    return piece.reshape(count, -1, width // HEAD_DIM, HEAD_DIM).transpose(0, 2, 1, 3)


def join_heads(parts):
    count, heads, rows, size = parts.shape
    return parts.transpose(0, 2, 1, 3).reshape(count * rows, heads * size)


def masked_scores(queries, keys, seq_lengths):
    scores = jnp.einsum("nhqd,nhkd->nhqk", queries, keys, preferred_element_type=F32)
    scores = scores * HEAD_DIM ** (-0.5)
    positions = lax.broadcasted_iota(jnp.int32, scores.shape, 3)
    return jnp.where(positions < seq_lengths[:, None, None, None], scores, -1000000000.0)


def forward_attention(inputs, weights, seq_lengths):
    count = seq_lengths.shape[0]
    packed = (dot(inputs, weights["qkv"]) + weights["bias_qkv"]).astype(BF)
    queries, keys, values = (heads_of(packed, n, count) for n in range(3))
    scores = masked_scores(queries, keys, seq_lengths)
    row_max = jnp.max(scores, axis=-1, keepdims=True)
    exponent = jnp.exp(scores - row_max)
    soft_weights = exponent / jnp.sum(exponent, axis=-1, keepdims=True)
    attended = jnp.einsum(
        "nhqk,nhkd->nhqd", soft_weights.astype(BF), values, preferred_element_type=F32
    )
    attended = join_heads(attended.astype(BF))
    return (attended, dict(inputs=inputs, qkv=(queries, keys, values), soft_weights=soft_weights))


def forward_hidden(attended, kept, weights):
    branch = pair_sum(dot(attended, weights["out"])) + weights["bias_out"]
    normed, inverse = norm_rows(kept["inputs"].astype(F32) + branch)
    hidden = (normed * weights["gain_attn"] + weights["shift_attn"]).astype(BF)
    upward = dot(hidden, weights["up"]) + weights["bias_up"]
    share = 0.5 + 0.5 * lax.erf(upward * 0.5**0.5)
    activated = (upward * share).astype(BF)
    slope = share + upward * jnp.exp(-0.5 * upward * upward) * TAU ** (-0.5)
    kept.update(attended=attended, normed_attn=normed, inverse_attn=inverse)
    kept.update(hidden=hidden, slope=slope)
    return activated


def forward_output(activated, kept, weights):
    mixed = pair_sum(dot(activated, weights["down"])) + weights["bias_down"]
    normed, inverse = norm_rows(kept["hidden"].astype(F32) + mixed)
    kept.update(activated=activated, normed_mlp=normed, inverse_mlp=inverse)
    return (normed * weights["gain_mlp"] + weights["shift_mlp"]).astype(BF)


def backward_mlp(grad_result, kept, weights):
    grad_result = grad_result.astype(F32)
    normed = kept["normed_mlp"]
    grad_gain = jnp.sum(grad_result * normed, axis=0)
    grad_shift = jnp.sum(grad_result, axis=0)
    grad_resid = norm_back(grad_result * weights["gain_mlp"], normed, kept["inverse_mlp"])
    grad_mixed = grad_resid.astype(BF)
    grad_upward = (dot_transposed(grad_mixed, weights["down"]) * kept["slope"]).astype(BF)
    passed = dot_transposed(grad_upward, weights["up"])
    grads = dict(
        mixed=grad_mixed,
        upward=grad_upward,
        bias_up=jnp.sum(grad_upward.astype(F32), axis=0),
        bias_down=jnp.sum(grad_mixed.astype(F32), axis=0),
        gain_mlp=grad_gain,
        shift_mlp=grad_shift,
    )
    return (grad_resid + pair_sum(passed), grads)


def backward_attention(grad_hidden, grads, kept, weights):
    scaling = HEAD_DIM ** (-0.5)
    normed = kept["normed_attn"]
    grad_resid = norm_back(grad_hidden * weights["gain_attn"], normed, kept["inverse_attn"])
    grad_branch = grad_resid.astype(BF)
    grads.update(
        gain_attn=jnp.sum(grad_hidden * normed, axis=0),
        shift_attn=jnp.sum(grad_hidden, axis=0),
        bias_out=jnp.sum(grad_branch.astype(F32), axis=0),
        out=transpose_dot(kept["attended"], grad_branch).astype(BF),
    )
    queries, keys, values = kept["qkv"]
    count = queries.shape[0]
    grad_attended = dot_transposed(grad_branch, weights["out"]).astype(BF)
    grad_attended = grad_attended.reshape(count, -1, queries.shape[1], HEAD_DIM)
    grad_attended = grad_attended.transpose(0, 2, 1, 3)
    soft_weights = kept["soft_weights"]
    grad_values = jnp.einsum(
        "nhqk,nhqd->nhkd", soft_weights.astype(BF), grad_attended, preferred_element_type=F32
    )
    grad_soft = jnp.einsum(
        "nhqd,nhkd->nhqk", grad_attended, values, preferred_element_type=F32
    )
    grad_scores = soft_weights * (
        grad_soft - jnp.sum(grad_soft * soft_weights, axis=-1, keepdims=True)
    )
    grad_scores = grad_scores.astype(BF)
    grad_queries = scaling * jnp.einsum(
        "nhqk,nhkd->nhqd", grad_scores, keys, preferred_element_type=F32
    )
    grad_keys = scaling * jnp.einsum(
        "nhqk,nhqd->nhkd", grad_scores, queries, preferred_element_type=F32
    )
    grad_packed = jnp.concatenate(
        [join_heads(g.astype(BF)) for g in (grad_queries, grad_keys, grad_values)], axis=1
    )
    return (grad_resid, grad_packed)


def backward_inputs(grad_resid, grad_packed, grads, kept, weights):
    columns = jnp.sum(grad_packed.astype(F32), axis=0)
    width = columns.shape[0] // 3
    grads.update(
        bias_q=columns[:width],
        bias_v=columns[2 * width :],
        qkv=transpose_dot(kept["inputs"], grad_packed).astype(BF),
    )
    passed = dot_transposed(grad_packed, weights["qkv"])
    return (grad_resid + pair_sum(passed)).astype(BF)


def per_device(
    tokens,
    lengths,
    cotangent,
    w_qkv,
    bias_q,
    bias_v,
    w_out,
    bias_out,
    gain_attn,
    shift_attn,
    w_up,
    bias_up,
    w_down,
    bias_down,
    gain_mlp,
    shift_mlp,
):
    first = lax.axis_index("section") == 0
    shards = lax.axis_size("shard")
    rows = w_qkv.shape[1]
    model = w_qkv.shape[2] // 3
    ff = w_up.shape[2]
    half = model // 2
    unit = ff // shards // 2

    def choose(low, high):
        return jnp.where(first, low, high)

    def mine_of(low, high):
        return (choose(low, high), choose(high, low))

    shard = lax.axis_index("shard")
    place = {"x": lax.axis_index("dp"), "y": shard % RING, "z": shard // RING}

    near = {axis: at ^ choose(1, 3) for axis, at in place.items()}
    far = {axis: at ^ choose(3, 1) for axis, at in place.items()}

    def trade(value, axis, masks):
        name = "dp" if axis == "x" else "shard"
        size = lax.axis_size(name)
        stride = RING if axis == "z" else 1
        route = []
        for core in range(2):
            for at in range(size):
                position = at // stride % RING
                target = at + ((position ^ masks[core]) - position) * stride
                route.append((core * size + at, core * size + target))
        return lax.ppermute(value, ("section", name), route)

    def after(value, earlier):
        return lax.optimization_barrier((value, earlier))[0]

    def hop(value, distance):
        route = [(at, (at + distance) % RING) for at in range(RING)]
        return lax.ppermute(value, "dp", route)

    def put(whole, piece, at, dim):
        start = [0] * whole.ndim
        start[dim] = at
        return lax.dynamic_update_slice(whole, jnp.expand_dims(piece, dim), start)

    def gather_one(block, axis):
        return trade(block, axis, (1, 3))

    def gather_two(block, beside, axis):
        return trade(jnp.stack([block, beside]), axis, (3, 1))

    def gather_end(block, beside, across, axis, dim):
        whole = jnp.zeros(block.shape[:dim] + (RING,) + block.shape[dim:], block.dtype)
        whole = put(whole, block, place[axis], dim)
        whole = put(whole, beside, near[axis], dim)
        whole = put(whole, across[0], far[axis], dim)
        return put(whole, across[1], place[axis] ^ 2, dim)

    def chunk(value, at, dim):
        return lax.dynamic_index_in_dim(value, at, dim, keepdims=False)

    def slices(value, dim):
        def two(at, other):
            return jnp.stack([chunk(value, at, dim), chunk(value, other, dim)])

        return (lambda at: chunk(value, at, dim).astype(F32), two)

    def products(left, right, shape):
        def one(at):
            return transpose_dot(chunk(left, at, 0), right).reshape(shape)

        def two(at, other):
            pair = jnp.stack([chunk(left, at, 0), chunk(left, other, 0)])
            both = lax.dot_general(pair, right, (((1,), (0,)), ((), ())), preferred_element_type=F32)
            return both.astype(BF).reshape((2,) + shape)

        return (one, two)

    def scatter_one(parts, axis):
        return trade(parts[1](near[axis], place[axis] ^ 2), axis, (1, 3))

    def scatter_two(parts, beside, axis):
        sent = parts[0](far[axis]) + beside[1].astype(F32)
        return trade(sent.astype(BF), axis, (3, 1))

    def scatter_end(parts, beside, across, axis):
        kept = parts[0](place[axis]) + beside[0].astype(F32)
        return (kept + across.astype(F32)).astype(BF)

    def together(*values):
        return lax.optimization_barrier(values)

    def placed(width, pieces):
        whole = jnp.zeros((pieces[0][1].shape[0], width), BF)
        for at, piece in pieces:
            whole = lax.dynamic_update_slice(whole, piece, (0, at))
        return whole

    def parts_of(part):
        qkv = w_qkv[0].reshape(rows, 3, 2, half)[:, :, part].reshape(rows, 3 * half)
        out = w_out[0][:, part * half : (part + 1) * half]
        up = w_up[0].reshape(rows, shards, 2, unit)[:, :, part].reshape(rows, shards * unit)
        return (qkv, out, up, w_down[0][part * unit : (part + 1) * unit])

    lines = [
        v.reshape(-1, rows)
        for v in (
            bias_q,
            bias_v,
            bias_out,
            gain_attn,
            shift_attn,
            bias_down,
            gain_mlp,
            shift_mlp,
            bias_up,
        )
    ]
    vectors, at = (jnp.zeros((rows, LANES), BF), 0)
    for line in lines:
        height = line.shape[0]
        vectors += jnp.pad(line, ((at, rows - at - height), (0, LANES - rows)))
        at += height
    vector_rows = at
    split = [mine_of(low, high) for low, high in zip(parts_of(0), parts_of(1))]
    kept_part = (vectors,) + tuple(low for low, high in split)
    sent_part = (vectors,) + tuple(high for low, high in split)
    got_part = tuple(swap(member) for member in sent_part)
    blocks = [mine_of(own, got) for own, got in zip(kept_part, got_part)]
    edges = (LANES, LANES + 3 * half, LANES + 4 * half, LANES + 4 * half + shards * unit)

    quarter = unit // RING

    def quarter_of(block):
        return chunk(block.reshape(RING, quarter, model), place["x"], 0)

    span = quarter * model // rows

    def gathered(layer, extra):
        pieces = list(zip((0,) + edges, [b[layer] for b in blocks[:4]]))
        pieces += [(edges[3] + n * span, piece) for n, piece in enumerate(extra)]
        return placed(edges[3] + len(extra) * span, pieces)

    def whole(block):
        return lax.all_gather(block, "shard", axis=0, tiled=True)

    side0 = whole(gathered(0, [quarter_of(block).reshape(rows, span) for block in blocks[4]]))
    side1 = whole(after(gathered(1, []), side0))
    c0, c1 = (
        side0[:, edges[3] + n * span : edges[3] + (n + 1) * span].reshape(shards, quarter, model)
        for n in range(2)
    )

    def arranged(attn, down):
        flat = attn[:, :LANES].reshape(shards, rows, LANES)[:, :vector_rows, :rows].astype(F32)
        whole = [flat[:, n].reshape(-1) for n in range(8)]
        bias_up_part = flat[:, 8:].reshape(shards, 2, unit)
        bias_up_part = choose(bias_up_part[:, 0], bias_up_part[:, 1]).reshape(-1)
        bias_q_part = choose(whole[0][:half], whole[0][half:])
        bias_v_part = choose(whole[1][:half], whole[1][half:])
        out = attn[:, edges[1] : edges[2]]
        held, handed = mine_of(out[:half], out[half:])
        arrived = swap(handed)
        return dict(
            qkv=attn[:, LANES : edges[1]],
            out=jnp.concatenate(mine_of(held, arrived), axis=1),
            up=attn[:, edges[2] :],
            down=down,
            bias_qkv=jnp.concatenate([bias_q_part, jnp.zeros_like(bias_q_part), bias_v_part]),
            bias_out=whole[2],
            gain_attn=whole[3],
            shift_attn=whole[4],
            bias_down=whole[5],
            gain_mlp=whole[6],
            shift_mlp=whole[7],
            bias_up=bias_up_part,
        )

    def side_by_side(grads):
        held, handed = mine_of(grads["out"][:, :half], grads["out"][:, half:])
        out = jnp.concatenate(mine_of(held, swap(handed)), axis=0)

        def widened(part):
            return jnp.concatenate([choose(part, 0.0), choose(0.0, part)])

        whole = [widened(grads["bias_q"]), widened(grads["bias_v"])]
        names = ("bias_out", "gain_attn", "shift_attn", "bias_down", "gain_mlp", "shift_mlp")
        whole += [0.5 * grads[name] for name in names]
        part = grads["bias_up"].reshape(shards, unit)
        spread = jnp.concatenate([choose(part, 0.0), choose(0.0, part)], axis=1)
        flat = [v.reshape(shards, 1, rows) for v in whole] + [spread.reshape(shards, -1, rows)]
        flat = jnp.concatenate(flat, axis=1).astype(BF)
        flat = jnp.pad(flat, ((0, 0), (0, rows - vector_rows), (0, LANES - rows)))
        return (flat.reshape(shards * rows, LANES), grads["qkv"], out)

    count = tokens.shape[0]
    seq_lengths = lengths[:, 0]

    first_weights = arranged(side0[:, : edges[3]], None)
    cn = gather_one(c0, "x")
    attended, kept0 = forward_attention(tokens.reshape(-1, model), first_weights, seq_lengths)
    cn, attended = together(cn, attended)
    cf = gather_two(c0, cn, "x")
    activated = forward_hidden(attended, kept0, first_weights)
    cf, activated = together(cf, activated)
    first_weights["down"] = gather_end(c0, cn, cf, "x", 1).reshape(-1, model)
    cn = gather_one(after(c1, cf), "x")
    middle = forward_output(activated, kept0, first_weights)
    cn, middle, side1 = together(cn, middle, side1)
    cf = gather_two(c1, cn, "x")
    second_weights = arranged(side1, None)
    attended, kept1 = forward_attention(middle, second_weights, seq_lengths)
    activated = forward_hidden(attended, kept1, second_weights)
    cf, activated = together(cf, activated)
    second_weights["down"] = gather_end(c1, cn, cf, "x", 1).reshape(-1, model)
    last = forward_output(activated, kept1, second_weights)

    def down_of(grads, kept):
        left = kept["activated"].reshape(-1, shards, RING, quarter).transpose(2, 0, 1, 3)
        left = left.reshape(RING, -1, shards * quarter)
        return products(left, grads["mixed"], (shards, quarter, model))

    def up_of(grads, kept):
        left = kept["hidden"].reshape(-1, RING, RING, rows).transpose(2, 0, 1, 3)
        return products(left.reshape(RING, -1, RING * rows), grads["upward"], (RING, rows, shards * unit))

    def side_of(grads):
        pieces = list(zip((0,) + edges, side_by_side(grads)))
        return placed(edges[2], pieces).reshape(RING, RING, rows, -1)

    grad_hidden, grads1 = backward_mlp(cotangent.reshape(-1, model), kept1, second_weights)
    c1, b1 = (down_of(grads1, kept1), up_of(grads1, kept1))
    cn, bn = (scatter_one(c1, "x"), scatter_one(b1, "y"))
    grad_resid, grad_packed = backward_attention(grad_hidden, grads1, kept1, second_weights)
    cn, bn, grad_packed = together(cn, bn, grad_packed)
    cf, bf = (scatter_two(c1, cn, "x"), scatter_two(b1, bn, "y"))
    grad_middle = backward_inputs(grad_resid, grad_packed, grads1, kept1, second_weights)
    a1 = side_of(grads1)
    a1, cf, bf, grad_middle = together(a1, cf, bf, grad_middle)
    c1, b1 = (scatter_end(c1, cn, cf, "x"), scatter_end(b1, bn, bf, "y"))
    a1 = slices(a1, 0)
    an1 = scatter_one(a1, "z")

    grad_hidden, grads0 = backward_mlp(grad_middle, kept0, first_weights)
    c0, b0 = (down_of(grads0, kept0), up_of(grads0, kept0))
    cn, bn = (scatter_one(c0, "x"), scatter_one(b0, "y"))
    grad_resid, grad_packed = backward_attention(grad_hidden, grads0, kept0, first_weights)
    an1, cn, bn, grad_packed = together(an1, cn, bn, grad_packed)
    af1 = scatter_two(a1, an1, "z")
    cf, bf = (scatter_two(c0, cn, "x"), scatter_two(b0, bn, "y"))
    grad_first = backward_inputs(grad_resid, grad_packed, grads0, kept0, first_weights)
    a0 = side_of(grads0)
    a0, af1, cf, bf = together(a0, af1, cf, bf)
    a1 = scatter_end(a1, an1, af1, "z")
    c0, b0 = (scatter_end(c0, cn, cf, "x"), scatter_end(b0, bn, bf, "y"))

    b = jnp.stack([b0, b1]).reshape(2, RING, RING, rows // RING, -1)
    c = jnp.stack([c0, c1]).reshape(2, RING, RING, quarter, model)
    a0, a1, b, c = (slices(a0, 0), slices(a1, 0), slices(b, 2), slices(c, 2))
    an, bn, cn, dn = together(
        scatter_one(a0, "z"), scatter_one(b, "x"), scatter_one(c, "y"), scatter_one(a1, "y")
    )
    af, bf, cf, df = together(
        scatter_two(a0, an, "z"), scatter_two(b, bn, "x"), scatter_two(c, cn, "y"), scatter_two(a1, dn, "y")
    )
    a0 = slices(scatter_end(a0, an, af, "z"), 0)
    a1 = slices(scatter_end(a1, dn, df, "y").reshape(RING, rows // RING, -1), 0)
    b, c = (slices(scatter_end(b, bn, bf, "x"), 1), slices(scatter_end(c, cn, cf, "y"), 1))
    an, bn, cn, dn = together(
        scatter_one(a0, "y"), scatter_one(b, "z"), scatter_one(c, "z"), scatter_one(a1, "x")
    )
    af, bf, cf, df = together(
        scatter_two(a0, an, "y"), scatter_two(b, bn, "z"), scatter_two(c, cn, "z"), scatter_two(a1, dn, "x")
    )
    a0 = scatter_end(a0, an, af, "y")
    a1 = scatter_end(a1, dn, df, "x")
    b, c = (scatter_end(b, bn, bf, "z"), scatter_end(c, cn, cf, "z"))
    wide = shards * unit
    rest = [b[0], c[0].reshape(-1, wide), b[1], c[1].reshape(-1, wide), a1]
    rest = placed(4 * wide + edges[2], [(n * wide, piece) for n, piece in enumerate(rest)])
    bn = gather_one(rest, "x")
    others = [hop(a0, n) for n in range(1, RING)]
    bn, others = together(bn, others)
    a0 = (a0.astype(F32) + sum(other.astype(F32) for other in others)).astype(BF)
    rest = gather_end(rest, bn, gather_two(rest, bn, "x"), "x", 0).reshape(rows, -1)
    b0, c0, b1, c1 = (rest[:, n * wide : (n + 1) * wide] for n in range(4))
    summed_first = (a0, b0, c0.reshape(unit, model))
    summed_second = (rest[:, 4 * wide :], b1, c1.reshape(unit, model))
    mine, sent = zip(*(mine_of(a, b) for a, b in zip(summed_first, summed_second)))
    both = [mine_of(a, swap(b)) for a, b in zip(mine, sent)]
    both = [[v.astype(F32) for v in pair] for pair in both]
    (side_a, side_b), (up_a, up_b), (down_a, down_b) = both

    def cut(block):
        flat = block[:vector_rows, :rows]
        return (flat, block[:, LANES : edges[1]].reshape(rows, 3, half), block[:, edges[1] :])

    (flat_a, qkv_a, out_a), (flat_b, qkv_b, out_b) = (cut(side_a), cut(side_b))
    up_a, up_b = (up_a.reshape(rows, shards, unit), up_b.reshape(rows, shards, unit))
    flat = flat_a + flat_b
    whole = [flat[n] for n in range(8)]
    grads = (
        jnp.stack([qkv_a, qkv_b], axis=2).reshape(rows, -1),
        whole[0],
        whole[1],
        jnp.concatenate([out_a, out_b], axis=1),
        whole[2],
        whole[3],
        whole[4],
        jnp.stack([up_a, up_b], axis=2).reshape(rows, -1),
        flat[8:].reshape(-1),
        jnp.concatenate([down_a, down_b], axis=0),
        whole[5],
        whole[6],
        whole[7],
    )
    shape = (1, count, 1, -1, model)
    activations = choose(middle, last).reshape(shape)
    input_grads = choose(grad_first, grad_middle).reshape(shape)
    return (activations, input_grads) + tuple(member[None] for member in grads)


def solution(mesh):
    rows = P(None, ("dp", "shard"), None, None)
    matrix = P("section", "shard", None)
    vector = P("section", "shard")
    weight_specs = (matrix, vector, vector, matrix, vector, vector, vector)
    weight_specs += (matrix, vector, matrix, vector, vector, vector)
    in_specs = (rows, P(None, ("dp", "shard")), rows) + weight_specs
    result = P("section", None, ("dp", "shard"), None, None)
    return jax.shard_map(
        per_device,
        mesh=mesh,
        in_specs=in_specs,
        out_specs=(result, result) + weight_specs,
        check_vma=False,
    )
```

```python
import jax
import jax.numpy as jnp
from jax import lax
from jax.experimental import pallas as pl
from jax.experimental.pallas import tpu as pltpu
from jax.sharding import PartitionSpec as P


HEAD_DIM = 64
EPSILON = 1e-06
TAU = 6.283185307179586
LANES = 128
RING = 4
BF = jnp.bfloat16
F32 = jnp.float32


def swap(value):
    return lax.ppermute(value, "section", [(0, 1), (1, 0)])


def pair_sum(part):
    low = part.astype(BF)
    other = swap(low)
    return low.astype(F32) + other.astype(F32)


def dot(left, right):
    return jnp.dot(left, right, preferred_element_type=F32)


def transpose_dot(left, right):
    return lax.dot_general(left, right, (((0,), (0,)), ((), ())), preferred_element_type=F32)


def dot_transposed(left, right):
    return lax.dot_general(left, right, (((1,), (1,)), ((), ())), preferred_element_type=F32)


def norm_rows(values):
    centered = values - jnp.mean(values, axis=-1, keepdims=True)
    inverse = lax.rsqrt(jnp.mean(centered * centered, axis=-1, keepdims=True) + EPSILON)
    return (centered * inverse, inverse)


def norm_back(grad_norm, normed, inverse):
    return inverse * (
        grad_norm
        - jnp.mean(grad_norm, axis=-1, keepdims=True)
        - normed * jnp.mean(grad_norm * normed, axis=-1, keepdims=True)
    )


def head_masks(rows):
    lane = lax.broadcasted_iota(jnp.int32, (rows, LANES), 1)
    return [lane < HEAD_DIM, lane >= HEAD_DIM]


def soft_weights_of(queries, keys, mask, seq_length):
    queries = jnp.where(mask, queries, 0.0).astype(BF)
    scores = dot_transposed(queries, keys) * HEAD_DIM ** (-0.5)
    positions = lax.broadcasted_iota(jnp.int32, scores.shape, 1)
    scores = jnp.where(positions < seq_length, scores, -1000000000.0)
    exponent = jnp.exp(scores - jnp.max(scores, axis=-1, keepdims=True))
    return exponent / jnp.sum(exponent, axis=-1, keepdims=True)


def pairs_of(packed_ref, count):
    rows, width = (packed_ref.shape[0] // count, packed_ref.shape[1] // 3)
    for n in range(count):
        for at in range(0, width, LANES):
            yield (n, pl.ds(n * rows, rows), [pl.ds(k * width + at, LANES) for k in range(3)])


def attention_kernel(lengths_ref, packed_ref, attended_ref):
    count = lengths_ref.shape[0]
    masks = head_masks(packed_ref.shape[0] // count)
    for n, rows, columns in pairs_of(packed_ref, count):
        queries, keys, values = (packed_ref[rows, at] for at in columns)
        queries = queries.astype(F32)
        parts = []
        for mask in masks:
            soft_weights = soft_weights_of(queries, keys, mask, lengths_ref[n])
            parts.append(dot(soft_weights.astype(BF), values))
        attended_ref[rows, columns[0]] = jnp.where(masks[0], *parts).astype(BF)


def attention_back_kernel(lengths_ref, packed_ref, grad_ref, out_ref):
    count = lengths_ref.shape[0]
    scaling = HEAD_DIM ** (-0.5)
    masks = head_masks(packed_ref.shape[0] // count)
    for n, rows, columns in pairs_of(packed_ref, count):
        queries, keys, values = (packed_ref[rows, at] for at in columns)
        grads = grad_ref[rows, columns[0]]
        wide_queries, wide_grads = (queries.astype(F32), grads.astype(F32))
        parts = []
        for mask in masks:
            soft_weights = soft_weights_of(wide_queries, keys, mask, lengths_ref[n])
            own = jnp.where(mask, wide_grads, 0.0).astype(BF)
            grad_soft = dot_transposed(own, values)
            mean = jnp.sum(grad_soft * soft_weights, axis=-1, keepdims=True)
            grad_scores = (soft_weights * (grad_soft - mean)).astype(BF)
            parts.append(
                (
                    dot(grad_scores, keys) * scaling,
                    transpose_dot(grad_scores, queries) * scaling,
                    transpose_dot(soft_weights.astype(BF), grads),
                )
            )
        for at, low, high in zip(columns, *parts):
            out_ref[rows, at] = jnp.where(masks[0], low, high).astype(BF)


def attention_call(kernel, width, seq_lengths, *arrays):
    rows = arrays[0].shape[0]
    vmem = pl.BlockSpec(memory_space=pltpu.VMEM)
    return pl.pallas_call(
        kernel,
        out_shape=jax.ShapeDtypeStruct((rows, width), BF),
        in_specs=[pl.BlockSpec(memory_space=pltpu.SMEM)] + [vmem] * len(arrays),
        out_specs=vmem,
        cost_estimate=pl.CostEstimate(
            flops=4 * rows * 128 * width, bytes_accessed=4 * rows * width, transcendentals=0
        ),
    )(seq_lengths, *arrays)


def forward_attention(inputs, weights, seq_lengths):
    packed = (dot(inputs, weights["qkv"]) + weights["bias_qkv"]).astype(BF)
    attended = attention_call(attention_kernel, packed.shape[1] // 3, seq_lengths, packed)
    return (attended, dict(inputs=inputs, packed=packed, seq_lengths=seq_lengths))


def forward_hidden(attended, kept, weights):
    branch = pair_sum(dot(attended, weights["out"])) + weights["bias_out"]
    normed, inverse = norm_rows(kept["inputs"].astype(F32) + branch)
    hidden = (normed * weights["gain_attn"] + weights["shift_attn"]).astype(BF)
    upward = dot(hidden, weights["up"]) + weights["bias_up"]
    share = 0.5 + 0.5 * lax.erf(upward * 0.5**0.5)
    activated = (upward * share).astype(BF)
    slope = share + upward * jnp.exp(-0.5 * upward * upward) * TAU ** (-0.5)
    kept.update(attended=attended, normed_attn=normed, inverse_attn=inverse)
    kept.update(hidden=hidden, slope=slope)
    return activated


def forward_output(activated, kept, weights):
    mixed = pair_sum(dot(activated, weights["down"])) + weights["bias_down"]
    normed, inverse = norm_rows(kept["hidden"].astype(F32) + mixed)
    kept.update(activated=activated, normed_mlp=normed, inverse_mlp=inverse)
    return (normed * weights["gain_mlp"] + weights["shift_mlp"]).astype(BF)


def backward_mlp(grad_result, kept, weights):
    grad_result = grad_result.astype(F32)
    normed = kept["normed_mlp"]
    grad_gain = jnp.sum(grad_result * normed, axis=0)
    grad_shift = jnp.sum(grad_result, axis=0)
    grad_resid = norm_back(grad_result * weights["gain_mlp"], normed, kept["inverse_mlp"])
    grad_mixed = grad_resid.astype(BF)
    grad_upward = (dot_transposed(grad_mixed, weights["down"]) * kept["slope"]).astype(BF)
    passed = dot_transposed(grad_upward, weights["up"])
    grads = dict(
        mixed=grad_mixed,
        upward=grad_upward,
        bias_up=jnp.sum(grad_upward.astype(F32), axis=0),
        bias_down=jnp.sum(grad_mixed.astype(F32), axis=0),
        gain_mlp=grad_gain,
        shift_mlp=grad_shift,
    )
    return (grad_resid + pair_sum(passed), grads)


def backward_attention(grad_hidden, grads, kept, weights):
    normed = kept["normed_attn"]
    grad_resid = norm_back(grad_hidden * weights["gain_attn"], normed, kept["inverse_attn"])
    grad_branch = grad_resid.astype(BF)
    grads.update(
        gain_attn=jnp.sum(grad_hidden * normed, axis=0),
        shift_attn=jnp.sum(grad_hidden, axis=0),
        bias_out=jnp.sum(grad_branch.astype(F32), axis=0),
        out=transpose_dot(kept["attended"], grad_branch).astype(BF),
    )
    packed = kept["packed"]
    grad_attended = dot_transposed(grad_branch, weights["out"]).astype(BF)
    grad_packed = attention_call(
        attention_back_kernel, packed.shape[1], kept["seq_lengths"], packed, grad_attended
    )
    return (grad_resid, grad_packed)


def backward_inputs(grad_resid, grad_packed, grads, kept, weights):
    columns = jnp.sum(grad_packed.astype(F32), axis=0)
    width = columns.shape[0] // 3
    grads.update(
        bias_q=columns[:width],
        bias_v=columns[2 * width :],
        qkv=transpose_dot(kept["inputs"], grad_packed).astype(BF),
    )
    passed = dot_transposed(grad_packed, weights["qkv"])
    return (grad_resid + pair_sum(passed)).astype(BF)


def per_device(
    tokens,
    lengths,
    cotangent,
    w_qkv,
    bias_q,
    bias_v,
    w_out,
    bias_out,
    gain_attn,
    shift_attn,
    w_up,
    bias_up,
    w_down,
    bias_down,
    gain_mlp,
    shift_mlp,
):
    first = lax.axis_index("section") == 0
    shards = lax.axis_size("shard")
    rows = w_qkv.shape[1]
    model = w_qkv.shape[2] // 3
    ff = w_up.shape[2]
    half = model // 2
    unit = ff // shards // 2

    def choose(low, high):
        return jnp.where(first, low, high)

    def mine_of(low, high):
        return (choose(low, high), choose(high, low))

    shard = lax.axis_index("shard")
    place = {"x": lax.axis_index("dp"), "y": shard % RING, "z": shard // RING}

    near = {axis: at ^ choose(1, 3) for axis, at in place.items()}
    far = {axis: at ^ choose(3, 1) for axis, at in place.items()}

    def trade(value, axis, masks):
        name = "dp" if axis == "x" else "shard"
        size = lax.axis_size(name)
        stride = RING if axis == "z" else 1
        route = []
        for core in range(2):
            for at in range(size):
                position = at // stride % RING
                target = at + ((position ^ masks[core]) - position) * stride
                route.append((core * size + at, core * size + target))
        return lax.ppermute(value, ("section", name), route)

    def after(value, earlier):
        return lax.optimization_barrier((value, earlier))[0]

    def hop(value, distance):
        route = [(at, (at + distance) % RING) for at in range(RING)]
        return lax.ppermute(value, "dp", route)

    def put(whole, piece, at, dim):
        start = [0] * whole.ndim
        start[dim] = at
        return lax.dynamic_update_slice(whole, jnp.expand_dims(piece, dim), start)

    def gather_one(block, axis):
        return trade(block, axis, (1, 3))

    def gather_two(block, beside, axis):
        return trade(jnp.stack([block, beside]), axis, (3, 1))

    def gather_end(block, beside, across, axis, dim):
        whole = jnp.zeros(block.shape[:dim] + (RING,) + block.shape[dim:], block.dtype)
        whole = put(whole, block, place[axis], dim)
        whole = put(whole, beside, near[axis], dim)
        whole = put(whole, across[0], far[axis], dim)
        return put(whole, across[1], place[axis] ^ 2, dim)

    def chunk(value, at, dim):
        return lax.dynamic_index_in_dim(value, at, dim, keepdims=False)

    def slices(value, dim):
        def two(at, other):
            return jnp.stack([chunk(value, at, dim), chunk(value, other, dim)])

        return (lambda at: chunk(value, at, dim).astype(F32), two)

    def products(left, right, shape):
        def one(at):
            return transpose_dot(chunk(left, at, 0), right).reshape(shape)

        def two(at, other):
            pair = jnp.stack([chunk(left, at, 0), chunk(left, other, 0)])
            both = lax.dot_general(pair, right, (((1,), (0,)), ((), ())), preferred_element_type=F32)
            return both.astype(BF).reshape((2,) + shape)

        return (one, two)

    def scatter_one(parts, axis):
        return trade(parts[1](near[axis], place[axis] ^ 2), axis, (1, 3))

    def scatter_two(parts, beside, axis):
        sent = parts[0](far[axis]) + beside[1].astype(F32)
        return trade(sent.astype(BF), axis, (3, 1))

    def scatter_end(parts, beside, across, axis):
        kept = parts[0](place[axis]) + beside[0].astype(F32)
        return (kept + across.astype(F32)).astype(BF)

    def together(*values):
        return lax.optimization_barrier(values)

    def placed(width, pieces):
        whole = jnp.zeros((pieces[0][1].shape[0], width), BF)
        for at, piece in pieces:
            whole = lax.dynamic_update_slice(whole, piece, (0, at))
        return whole

    def parts_of(part):
        qkv = w_qkv[0].reshape(rows, 3, 2, half)[:, :, part].reshape(rows, 3 * half)
        out = w_out[0][:, part * half : (part + 1) * half]
        up = w_up[0].reshape(rows, shards, 2, unit)[:, :, part].reshape(rows, shards * unit)
        return (qkv, out, up, w_down[0][part * unit : (part + 1) * unit])

    lines = [
        v.reshape(-1, rows)
        for v in (
            bias_q,
            bias_v,
            bias_out,
            gain_attn,
            shift_attn,
            bias_down,
            gain_mlp,
            shift_mlp,
            bias_up,
        )
    ]
    vectors, at = (jnp.zeros((rows, LANES), BF), 0)
    for line in lines:
        height = line.shape[0]
        vectors += jnp.pad(line, ((at, rows - at - height), (0, LANES - rows)))
        at += height
    vector_rows = at
    split = [mine_of(low, high) for low, high in zip(parts_of(0), parts_of(1))]
    kept_part = (vectors,) + tuple(low for low, high in split)
    sent_part = (vectors,) + tuple(high for low, high in split)
    got_part = tuple(swap(member) for member in sent_part)
    blocks = [mine_of(own, got) for own, got in zip(kept_part, got_part)]
    edges = (LANES, LANES + 3 * half, LANES + 4 * half, LANES + 4 * half + shards * unit)

    quarter = unit // RING

    def quarter_of(block):
        return chunk(block.reshape(RING, quarter, model), place["x"], 0)

    span = quarter * model // rows

    def gathered(layer, extra):
        pieces = list(zip((0,) + edges, [b[layer] for b in blocks[:4]]))
        pieces += [(edges[3] + n * span, piece) for n, piece in enumerate(extra)]
        return placed(edges[3] + len(extra) * span, pieces)

    def whole(block):
        return lax.all_gather(block, "shard", axis=0, tiled=True)

    side0 = whole(gathered(0, [quarter_of(block).reshape(rows, span) for block in blocks[4]]))
    side1 = whole(after(gathered(1, []), side0))
    c0, c1 = (
        side0[:, edges[3] + n * span : edges[3] + (n + 1) * span].reshape(shards, quarter, model)
        for n in range(2)
    )

    def arranged(attn, down):
        flat = attn[:, :LANES].reshape(shards, rows, LANES)[:, :vector_rows, :rows].astype(F32)
        whole = [flat[:, n].reshape(-1) for n in range(8)]
        bias_up_part = flat[:, 8:].reshape(shards, 2, unit)
        bias_up_part = choose(bias_up_part[:, 0], bias_up_part[:, 1]).reshape(-1)
        bias_q_part = choose(whole[0][:half], whole[0][half:])
        bias_v_part = choose(whole[1][:half], whole[1][half:])
        out = attn[:, edges[1] : edges[2]]
        held, handed = mine_of(out[:half], out[half:])
        arrived = swap(handed)
        return dict(
            qkv=attn[:, LANES : edges[1]],
            out=jnp.concatenate(mine_of(held, arrived), axis=1),
            up=attn[:, edges[2] :],
            down=down,
            bias_qkv=jnp.concatenate([bias_q_part, jnp.zeros_like(bias_q_part), bias_v_part]),
            bias_out=whole[2],
            gain_attn=whole[3],
            shift_attn=whole[4],
            bias_down=whole[5],
            gain_mlp=whole[6],
            shift_mlp=whole[7],
            bias_up=bias_up_part,
        )

    def side_by_side(grads):
        held, handed = mine_of(grads["out"][:, :half], grads["out"][:, half:])
        out = jnp.concatenate(mine_of(held, swap(handed)), axis=0)

        def widened(part):
            return jnp.concatenate([choose(part, 0.0), choose(0.0, part)])

        whole = [widened(grads["bias_q"]), widened(grads["bias_v"])]
        names = ("bias_out", "gain_attn", "shift_attn", "bias_down", "gain_mlp", "shift_mlp")
        whole += [0.5 * grads[name] for name in names]
        part = grads["bias_up"].reshape(shards, unit)
        spread = jnp.concatenate([choose(part, 0.0), choose(0.0, part)], axis=1)
        flat = [v.reshape(shards, 1, rows) for v in whole] + [spread.reshape(shards, -1, rows)]
        flat = jnp.concatenate(flat, axis=1).astype(BF)
        flat = jnp.pad(flat, ((0, 0), (0, rows - vector_rows), (0, LANES - rows)))
        return (flat.reshape(shards * rows, LANES), grads["qkv"], out)

    count = tokens.shape[0]
    seq_lengths = lengths[:, 0]

    first_weights = arranged(side0[:, : edges[3]], None)
    cn = gather_one(c0, "x")
    attended, kept0 = forward_attention(tokens.reshape(-1, model), first_weights, seq_lengths)
    cn, attended = together(cn, attended)
    cf = gather_two(c0, cn, "x")
    activated = forward_hidden(attended, kept0, first_weights)
    cf, activated = together(cf, activated)
    first_weights["down"] = gather_end(c0, cn, cf, "x", 1).reshape(-1, model)
    cn = gather_one(after(c1, cf), "x")
    middle = forward_output(activated, kept0, first_weights)
    cn, middle, side1 = together(cn, middle, side1)
    cf = gather_two(c1, cn, "x")
    second_weights = arranged(side1, None)
    attended, kept1 = forward_attention(middle, second_weights, seq_lengths)
    activated = forward_hidden(attended, kept1, second_weights)
    cf, activated = together(cf, activated)
    second_weights["down"] = gather_end(c1, cn, cf, "x", 1).reshape(-1, model)
    last = forward_output(activated, kept1, second_weights)

    def down_of(grads, kept):
        left = kept["activated"].reshape(-1, shards, RING, quarter).transpose(2, 0, 1, 3)
        left = left.reshape(RING, -1, shards * quarter)
        return products(left, grads["mixed"], (shards, quarter, model))

    def up_of(grads, kept):
        left = kept["hidden"].reshape(-1, RING, RING, rows).transpose(2, 0, 1, 3)
        return products(left.reshape(RING, -1, RING * rows), grads["upward"], (RING, rows, shards * unit))

    def side_of(grads):
        pieces = list(zip((0,) + edges, side_by_side(grads)))
        return placed(edges[2], pieces).reshape(RING, RING, rows, -1)

    grad_hidden, grads1 = backward_mlp(cotangent.reshape(-1, model), kept1, second_weights)
    c1, b1 = (down_of(grads1, kept1), up_of(grads1, kept1))
    cn, bn = (scatter_one(c1, "x"), scatter_one(b1, "y"))
    grad_resid, grad_packed = backward_attention(grad_hidden, grads1, kept1, second_weights)
    cn, bn, grad_packed = together(cn, bn, grad_packed)
    cf, bf = (scatter_two(c1, cn, "x"), scatter_two(b1, bn, "y"))
    grad_middle = backward_inputs(grad_resid, grad_packed, grads1, kept1, second_weights)
    a1 = side_of(grads1)
    a1, cf, bf, grad_middle = together(a1, cf, bf, grad_middle)
    c1, b1 = (scatter_end(c1, cn, cf, "x"), scatter_end(b1, bn, bf, "y"))
    a1 = slices(a1, 0)
    an1 = scatter_one(a1, "z")

    grad_hidden, grads0 = backward_mlp(grad_middle, kept0, first_weights)
    c0, b0 = (down_of(grads0, kept0), up_of(grads0, kept0))
    cn, bn = (scatter_one(c0, "x"), scatter_one(b0, "y"))
    grad_resid, grad_packed = backward_attention(grad_hidden, grads0, kept0, first_weights)
    an1, cn, bn, grad_packed = together(an1, cn, bn, grad_packed)
    af1 = scatter_two(a1, an1, "z")
    cf, bf = (scatter_two(c0, cn, "x"), scatter_two(b0, bn, "y"))
    grad_first = backward_inputs(grad_resid, grad_packed, grads0, kept0, first_weights)
    a0 = side_of(grads0)
    a0, af1, cf, bf = together(a0, af1, cf, bf)
    a1 = scatter_end(a1, an1, af1, "z")
    c0, b0 = (scatter_end(c0, cn, cf, "x"), scatter_end(b0, bn, bf, "y"))

    b = jnp.stack([b0, b1]).reshape(2, RING, RING, rows // RING, -1)
    c = jnp.stack([c0, c1]).reshape(2, RING, RING, quarter, model)
    a0, a1, b, c = (slices(a0, 0), slices(a1, 0), slices(b, 2), slices(c, 2))
    an, bn, cn, dn = together(
        scatter_one(a0, "z"), scatter_one(b, "x"), scatter_one(c, "y"), scatter_one(a1, "y")
    )
    af, bf, cf, df = together(
        scatter_two(a0, an, "z"), scatter_two(b, bn, "x"), scatter_two(c, cn, "y"), scatter_two(a1, dn, "y")
    )
    a0 = slices(scatter_end(a0, an, af, "z"), 0)
    a1 = slices(scatter_end(a1, dn, df, "y").reshape(RING, rows // RING, -1), 0)
    b, c = (slices(scatter_end(b, bn, bf, "x"), 1), slices(scatter_end(c, cn, cf, "y"), 1))
    an, bn, cn, dn = together(
        scatter_one(a0, "y"), scatter_one(b, "z"), scatter_one(c, "z"), scatter_one(a1, "x")
    )
    af, bf, cf, df = together(
        scatter_two(a0, an, "y"), scatter_two(b, bn, "z"), scatter_two(c, cn, "z"), scatter_two(a1, dn, "x")
    )
    a0 = scatter_end(a0, an, af, "y")
    a1 = scatter_end(a1, dn, df, "x")
    b, c = (scatter_end(b, bn, bf, "z"), scatter_end(c, cn, cf, "z"))
    wide = shards * unit
    rest = [b[0], c[0].reshape(-1, wide), b[1], c[1].reshape(-1, wide), a1]
    rest = placed(4 * wide + edges[2], [(n * wide, piece) for n, piece in enumerate(rest)])
    bn = gather_one(rest, "x")
    others = [hop(a0, n) for n in range(1, RING)]
    bn, others = together(bn, others)
    a0 = (a0.astype(F32) + sum(other.astype(F32) for other in others)).astype(BF)
    rest = gather_end(rest, bn, gather_two(rest, bn, "x"), "x", 0).reshape(rows, -1)
    b0, c0, b1, c1 = (rest[:, n * wide : (n + 1) * wide] for n in range(4))
    summed_first = (a0, b0, c0.reshape(unit, model))
    summed_second = (rest[:, 4 * wide :], b1, c1.reshape(unit, model))
    mine, sent = zip(*(mine_of(a, b) for a, b in zip(summed_first, summed_second)))
    both = [mine_of(a, swap(b)) for a, b in zip(mine, sent)]
    both = [[v.astype(F32) for v in pair] for pair in both]
    (side_a, side_b), (up_a, up_b), (down_a, down_b) = both

    def cut(block):
        flat = block[:vector_rows, :rows]
        return (flat, block[:, LANES : edges[1]].reshape(rows, 3, half), block[:, edges[1] :])

    (flat_a, qkv_a, out_a), (flat_b, qkv_b, out_b) = (cut(side_a), cut(side_b))
    up_a, up_b = (up_a.reshape(rows, shards, unit), up_b.reshape(rows, shards, unit))
    flat = flat_a + flat_b
    whole = [flat[n] for n in range(8)]
    grads = (
        jnp.stack([qkv_a, qkv_b], axis=2).reshape(rows, -1),
        whole[0],
        whole[1],
        jnp.concatenate([out_a, out_b], axis=1),
        whole[2],
        whole[3],
        whole[4],
        jnp.stack([up_a, up_b], axis=2).reshape(rows, -1),
        flat[8:].reshape(-1),
        jnp.concatenate([down_a, down_b], axis=0),
        whole[5],
        whole[6],
        whole[7],
    )
    shape = (1, count, 1, -1, model)
    activations = choose(middle, last).reshape(shape)
    input_grads = choose(grad_first, grad_middle).reshape(shape)
    return (activations, input_grads) + tuple(member[None] for member in grads)


def solution(mesh):
    rows = P(None, ("dp", "shard"), None, None)
    matrix = P("section", "shard", None)
    vector = P("section", "shard")
    weight_specs = (matrix, vector, vector, matrix, vector, vector, vector)
    weight_specs += (matrix, vector, matrix, vector, vector, vector)
    in_specs = (rows, P(None, ("dp", "shard")), rows) + weight_specs
    result = P("section", None, ("dp", "shard"), None, None)
    return jax.shard_map(
        per_device,
        mesh=mesh,
        in_specs=in_specs,
        out_specs=(result, result) + weight_specs,
        check_vma=False,
    )
```

```python
import jax
import jax.numpy as jnp
from jax import lax
from jax.experimental import pallas as pl
from jax.experimental.pallas import tpu as pltpu
from jax.sharding import PartitionSpec as P


HEAD_DIM = 64
EPSILON = 1e-06
TAU = 6.283185307179586
LANES = 128
RING = 4
BF = jnp.bfloat16
F32 = jnp.float32


def swap(value):
    return lax.ppermute(value, "section", [(0, 1), (1, 0)])


def pair_sum(part):
    low = part.astype(BF)
    other = swap(low)
    return low.astype(F32) + other.astype(F32)


def dot(left, right):
    return jnp.dot(left, right, preferred_element_type=F32)


def transpose_dot(left, right):
    return lax.dot_general(left, right, (((0,), (0,)), ((), ())), preferred_element_type=F32)


def dot_transposed(left, right):
    return lax.dot_general(left, right, (((1,), (1,)), ((), ())), preferred_element_type=F32)


def sum_rows(values):
    return jnp.sum(values, axis=0, keepdims=True)


def norm_rows(values):
    centered = values - jnp.mean(values, axis=-1, keepdims=True)
    inverse = lax.rsqrt(jnp.mean(centered * centered, axis=-1, keepdims=True) + EPSILON)
    return (centered * inverse, inverse)


def norm_back(grad_norm, normed, inverse):
    return inverse * (
        grad_norm
        - jnp.mean(grad_norm, axis=-1, keepdims=True)
        - normed * jnp.mean(grad_norm * normed, axis=-1, keepdims=True)
    )


def head_masks(rows):
    lane = lax.broadcasted_iota(jnp.int32, (rows, LANES), 1)
    return [lane < HEAD_DIM, lane >= HEAD_DIM]


def soft_weights_of(queries, keys, mask, seq_length):
    queries = jnp.where(mask, queries, 0.0).astype(BF)
    scores = dot_transposed(queries, keys) * HEAD_DIM ** (-0.5)
    positions = lax.broadcasted_iota(jnp.int32, scores.shape, 1)
    scores = jnp.where(positions < seq_length, scores, -1000000000.0)
    exponent = jnp.exp(scores - jnp.max(scores, axis=-1, keepdims=True))
    return exponent / jnp.sum(exponent, axis=-1, keepdims=True)


def pairs_of(packed_ref, count):
    rows, width = (packed_ref.shape[0] // count, packed_ref.shape[1] // 3)
    for n in range(count):
        for at in range(0, width, LANES):
            yield (n, pl.ds(n * rows, rows), [pl.ds(k * width + at, LANES) for k in range(3)])


def attention_kernel(lengths_ref, packed_ref, attended_ref):
    count = lengths_ref.shape[0]
    masks = head_masks(packed_ref.shape[0] // count)
    for n, rows, columns in pairs_of(packed_ref, count):
        queries, keys, values = (packed_ref[rows, at] for at in columns)
        queries = queries.astype(F32)
        parts = []
        for mask in masks:
            soft_weights = soft_weights_of(queries, keys, mask, lengths_ref[n])
            parts.append(dot(soft_weights.astype(BF), values))
        attended_ref[rows, columns[0]] = jnp.where(masks[0], *parts).astype(BF)


def attention_back_kernel(lengths_ref, packed_ref, grad_ref, out_ref):
    count = lengths_ref.shape[0]
    scaling = HEAD_DIM ** (-0.5)
    masks = head_masks(packed_ref.shape[0] // count)
    for n, rows, columns in pairs_of(packed_ref, count):
        queries, keys, values = (packed_ref[rows, at] for at in columns)
        grads = grad_ref[rows, columns[0]]
        wide_queries, wide_grads = (queries.astype(F32), grads.astype(F32))
        parts = []
        for mask in masks:
            soft_weights = soft_weights_of(wide_queries, keys, mask, lengths_ref[n])
            own = jnp.where(mask, wide_grads, 0.0).astype(BF)
            grad_soft = dot_transposed(own, values)
            mean = jnp.sum(grad_soft * soft_weights, axis=-1, keepdims=True)
            grad_scores = (soft_weights * (grad_soft - mean)).astype(BF)
            parts.append(
                (
                    dot(grad_scores, keys) * scaling,
                    transpose_dot(grad_scores, queries) * scaling,
                    transpose_dot(soft_weights.astype(BF), grads),
                )
            )
        for at, low, high in zip(columns, *parts):
            out_ref[rows, at] = jnp.where(masks[0], low, high).astype(BF)


def attention_call(kernel, width, seq_lengths, *arrays):
    rows = arrays[0].shape[0]
    vmem = pl.BlockSpec(memory_space=pltpu.VMEM)
    return pl.pallas_call(
        kernel,
        out_shape=jax.ShapeDtypeStruct((rows, width), BF),
        in_specs=[pl.BlockSpec(memory_space=pltpu.SMEM)] + [vmem] * len(arrays),
        out_specs=vmem,
        cost_estimate=pl.CostEstimate(
            flops=4 * rows * 128 * width, bytes_accessed=4 * rows * width, transcendentals=0
        ),
    )(seq_lengths, *arrays)


def forward_packed(inputs, weights):
    return (dot(inputs, weights["qkv"]) + weights["bias_qkv"]).astype(BF)


def forward_attention(inputs, packed, seq_lengths):
    attended = attention_call(attention_kernel, packed.shape[1] // 3, seq_lengths, packed)
    return (attended, dict(inputs=inputs, packed=packed, seq_lengths=seq_lengths))


def forward_hidden(attended, kept, weights):
    branch = pair_sum(dot(attended, weights["out"])) + weights["bias_out"]
    normed, inverse = norm_rows(kept["inputs"].astype(F32) + branch)
    hidden = (normed * weights["gain_attn"] + weights["shift_attn"]).astype(BF)
    upward = dot(hidden, weights["up"]) + weights["bias_up"]
    share = 0.5 + 0.5 * lax.erf(upward * 0.5**0.5)
    activated = (upward * share).astype(BF)
    slope = share + upward * jnp.exp(-0.5 * upward * upward) * TAU ** (-0.5)
    kept.update(attended=attended, normed_attn=normed, inverse_attn=inverse)
    kept.update(hidden=hidden, slope=slope)
    return activated


def forward_output(activated, kept, weights):
    mixed = pair_sum(dot(activated, weights["down"])) + weights["bias_down"]
    normed, inverse = norm_rows(kept["hidden"].astype(F32) + mixed)
    kept.update(activated=activated, normed_mlp=normed, inverse_mlp=inverse)
    return (normed * weights["gain_mlp"] + weights["shift_mlp"]).astype(BF)


def backward_mlp(grad_result, kept, weights):
    grad_result = grad_result.astype(F32)
    normed = kept["normed_mlp"]
    grad_gain = sum_rows(grad_result * normed)
    grad_shift = sum_rows(grad_result)
    grad_resid = norm_back(grad_result * weights["gain_mlp"], normed, kept["inverse_mlp"])
    grad_mixed = grad_resid.astype(BF)
    grad_upward = (dot_transposed(grad_mixed, weights["down"]) * kept["slope"]).astype(BF)
    passed = dot_transposed(grad_upward, weights["up"])
    grads = dict(
        mixed=grad_mixed,
        upward=grad_upward,
        bias_up=sum_rows(grad_upward.astype(F32)),
        bias_down=sum_rows(grad_mixed.astype(F32)),
        gain_mlp=grad_gain,
        shift_mlp=grad_shift,
    )
    return (grad_resid + pair_sum(passed), grads)


def backward_attention(grad_hidden, grads, kept, weights):
    normed = kept["normed_attn"]
    grad_resid = norm_back(grad_hidden * weights["gain_attn"], normed, kept["inverse_attn"])
    grad_branch = grad_resid.astype(BF)
    grads.update(
        gain_attn=sum_rows(grad_hidden * normed),
        shift_attn=sum_rows(grad_hidden),
        bias_out=sum_rows(grad_branch.astype(F32)),
        out=transpose_dot(kept["attended"], grad_branch).astype(BF),
    )
    packed = kept["packed"]
    grad_attended = dot_transposed(grad_branch, weights["out"]).astype(BF)
    grad_packed = attention_call(
        attention_back_kernel, packed.shape[1], kept["seq_lengths"], packed, grad_attended
    )
    return (grad_resid, grad_packed)


def backward_inputs(grad_resid, grad_packed, grads, kept, weights):
    columns = sum_rows(grad_packed.astype(F32))
    width = columns.shape[1] // 3
    grads.update(
        bias_q=columns[:, :width],
        bias_v=columns[:, 2 * width :],
        qkv=transpose_dot(kept["inputs"], grad_packed).astype(BF),
    )
    passed = dot_transposed(grad_packed, weights["qkv"])
    return (grad_resid + pair_sum(passed)).astype(BF)


def per_device(
    tokens,
    lengths,
    cotangent,
    w_qkv,
    bias_q,
    bias_v,
    w_out,
    bias_out,
    gain_attn,
    shift_attn,
    w_up,
    bias_up,
    w_down,
    bias_down,
    gain_mlp,
    shift_mlp,
):
    first = lax.axis_index("section") == 0
    shards = lax.axis_size("shard")
    rows = w_qkv.shape[1]
    model = w_qkv.shape[2] // 3
    ff = w_up.shape[2]
    half = model // 2
    unit = ff // shards // 2

    def choose(low, high):
        return jnp.where(first, low, high)

    def mine_of(low, high):
        return (choose(low, high), choose(high, low))

    shard = lax.axis_index("shard")
    place = {"x": lax.axis_index("dp"), "y": shard % RING, "z": shard // RING}

    near = {axis: at ^ choose(1, 3) for axis, at in place.items()}
    far = {axis: at ^ choose(3, 1) for axis, at in place.items()}

    def trade(value, axis, masks):
        name = "dp" if axis == "x" else "shard"
        size = lax.axis_size(name)
        stride = RING if axis == "z" else 1
        route = []
        for core in range(2):
            for at in range(size):
                position = at // stride % RING
                target = at + ((position ^ masks[core]) - position) * stride
                route.append((core * size + at, core * size + target))
        return lax.ppermute(value, ("section", name), route)

    def after(value, earlier):
        return lax.optimization_barrier((value, earlier))[0]

    def hop(value, distance):
        route = [(at, (at + distance) % RING) for at in range(RING)]
        return lax.ppermute(value, "dp", route)

    def put(whole, piece, at, dim):
        start = [0] * whole.ndim
        start[dim] = at
        return lax.dynamic_update_slice(whole, jnp.expand_dims(piece, dim), start)

    def gather_one(block, axis):
        return trade(block, axis, (1, 3))

    def gather_two(block, beside, axis):
        return trade(jnp.stack([block, beside]), axis, (3, 1))

    def gather_end(block, beside, across, axis, dim):
        whole = jnp.zeros(block.shape[:dim] + (RING,) + block.shape[dim:], block.dtype)
        whole = put(whole, block, place[axis], dim)
        whole = put(whole, beside, near[axis], dim)
        whole = put(whole, across[0], far[axis], dim)
        return put(whole, across[1], place[axis] ^ 2, dim)

    def chunk(value, at, dim):
        return lax.dynamic_index_in_dim(value, at, dim, keepdims=False)

    def slices(value, dim):
        def two(at, other):
            return jnp.stack([chunk(value, at, dim), chunk(value, other, dim)])

        return (lambda at: chunk(value, at, dim).astype(F32), two)

    def products(left, right, shape):
        def one(at):
            return transpose_dot(chunk(left, at, 0), right).reshape(shape)

        def two(at, other):
            pair = jnp.stack([chunk(left, at, 0), chunk(left, other, 0)])
            both = lax.dot_general(pair, right, (((1,), (0,)), ((), ())), preferred_element_type=F32)
            return both.astype(BF).reshape((2,) + shape)

        return (one, two)

    def scatter_one(parts, axis):
        return trade(parts[1](near[axis], place[axis] ^ 2), axis, (1, 3))

    def scatter_two(parts, beside, axis):
        sent = parts[0](far[axis]) + beside[1].astype(F32)
        return trade(sent.astype(BF), axis, (3, 1))

    def scatter_end(parts, beside, across, axis):
        kept = parts[0](place[axis]) + beside[0].astype(F32)
        return (kept + across.astype(F32)).astype(BF)

    def together(*values):
        return lax.optimization_barrier(values)

    def placed(width, pieces):
        whole = jnp.zeros((pieces[0][1].shape[0], width), BF)
        for at, piece in pieces:
            whole = lax.dynamic_update_slice(whole, piece, (0, at))
        return whole

    def parts_of(part):
        qkv = w_qkv[0].reshape(rows, 3, 2, half)[:, :, part].reshape(rows, 3 * half)
        out = w_out[0][:, part * half : (part + 1) * half]
        up = w_up[0].reshape(rows, shards, 2, unit)[:, :, part].reshape(rows, shards * unit)
        return (qkv, out, up, w_down[0][part * unit : (part + 1) * unit])

    lines = [
        v.reshape(-1, rows)
        for v in (
            bias_q,
            bias_v,
            bias_out,
            gain_attn,
            shift_attn,
            bias_down,
            gain_mlp,
            shift_mlp,
            bias_up,
        )
    ]
    vectors, at = (jnp.zeros((rows, LANES), BF), 0)
    for line in lines:
        height = line.shape[0]
        vectors += jnp.pad(line, ((at, rows - at - height), (0, LANES - rows)))
        at += height
    vector_rows = at
    split = [mine_of(low, high) for low, high in zip(parts_of(0), parts_of(1))]
    kept_part = (vectors,) + tuple(low for low, high in split)
    sent_part = (vectors,) + tuple(high for low, high in split)
    got_part = tuple(swap(member) for member in sent_part)
    blocks = [mine_of(own, got) for own, got in zip(kept_part, got_part)]
    edges = (LANES, LANES + 3 * half, LANES + 4 * half, LANES + 4 * half + shards * unit)

    quarter = unit // RING

    def quarter_of(block):
        return chunk(block.reshape(RING, quarter, model), place["x"], 0)

    span = quarter * model // rows

    def gathered(layer, extra):
        pieces = list(zip((0,) + edges, [b[layer] for b in blocks[:4]]))
        pieces += [(edges[3] + n * span, piece) for n, piece in enumerate(extra)]
        return placed(edges[3] + len(extra) * span, pieces)

    def whole(block):
        return lax.all_gather(block, "shard", axis=0, tiled=True)

    side0 = whole(gathered(0, [quarter_of(block).reshape(rows, span) for block in blocks[4]]))
    side1 = whole(after(gathered(1, []), side0))
    c0, c1 = (
        side0[:, edges[3] + n * span : edges[3] + (n + 1) * span].reshape(shards, quarter, model)
        for n in range(2)
    )

    def arranged(attn, down):
        flat = attn[:, :LANES].reshape(shards, rows, LANES)[:, :vector_rows, :rows].astype(F32)
        lines = flat[:, :8].transpose(1, 0, 2).reshape(8, model)
        whole = [lines[n : n + 1] for n in range(8)]
        bias_up_part = flat[:, 8:].reshape(shards, 2, unit)
        bias_up_part = choose(bias_up_part[:, 0], bias_up_part[:, 1]).reshape(1, -1)
        bias_q_part = choose(whole[0][:, :half], whole[0][:, half:])
        bias_v_part = choose(whole[1][:, :half], whole[1][:, half:])
        out = attn[:, edges[1] : edges[2]]
        held, handed = mine_of(out[:half], out[half:])
        arrived = swap(handed)
        return dict(
            qkv=attn[:, LANES : edges[1]],
            out=jnp.concatenate(mine_of(held, arrived), axis=1),
            up=attn[:, edges[2] :],
            down=down,
            bias_qkv=jnp.concatenate([bias_q_part, 0.0 * bias_q_part, bias_v_part], axis=1),
            bias_out=whole[2],
            gain_attn=whole[3],
            shift_attn=whole[4],
            bias_down=whole[5],
            gain_mlp=whole[6],
            shift_mlp=whole[7],
            bias_up=bias_up_part,
        )

    def vectors_of(grads):
        def widened(part):
            return jnp.concatenate([choose(part, 0.0), choose(0.0, part)], axis=1)

        names = ("bias_out", "gain_attn", "shift_attn", "bias_down", "gain_mlp", "shift_mlp")
        lines = [widened(grads["bias_q"]), widened(grads["bias_v"])]
        lines = jnp.concatenate(lines + [0.5 * grads[name] for name in names], axis=0)
        lines = lines.reshape(8, shards, rows).transpose(1, 0, 2)
        spread = widened(grads["bias_up"].reshape(shards, unit)).reshape(shards, -1, rows)
        return jnp.concatenate([lines, spread], axis=1)

    def sides_of(grads):
        held, handed = mine_of(grads["out"][:, :half], grads["out"][:, half:])
        return [grads["qkv"], jnp.concatenate(mine_of(held, swap(handed)), axis=0)]

    count = tokens.shape[0]
    seq_lengths = lengths[:, 0]

    first_weights = arranged(side0[:, : edges[3]], None)
    cn = gather_one(c0, "x")
    packed = forward_packed(tokens.reshape(-1, model), first_weights)
    cn, packed = together(cn, packed)
    cf = gather_two(c0, cn, "x")
    attended, kept0 = forward_attention(tokens.reshape(-1, model), packed, seq_lengths)
    activated = forward_hidden(attended, kept0, first_weights)
    cf, activated = together(cf, activated)
    first_weights["down"] = gather_end(c0, cn, cf, "x", 1).reshape(-1, model)
    cn = gather_one(after(c1, cf), "x")
    middle = forward_output(activated, kept0, first_weights)
    cn, middle, side1 = together(cn, middle, side1)
    cf = gather_two(c1, cn, "x")
    second_weights = arranged(side1, None)
    packed = forward_packed(middle, second_weights)
    attended, kept1 = forward_attention(middle, packed, seq_lengths)
    cf, attended = together(cf, attended)
    activated = forward_hidden(attended, kept1, second_weights)
    second_weights["down"] = gather_end(c1, cn, cf, "x", 1).reshape(-1, model)
    last = forward_output(activated, kept1, second_weights)

    def down_of(grads, kept):
        left = kept["activated"].reshape(-1, shards, RING, quarter).transpose(2, 0, 1, 3)
        left = left.reshape(RING, -1, shards * quarter)
        return products(left, grads["mixed"], (shards, quarter, model))

    def up_of(grads, kept):
        left = kept["hidden"].reshape(-1, RING, RING, rows).transpose(2, 0, 1, 3)
        return products(left.reshape(RING, -1, RING * rows), grads["upward"], (RING, rows, shards * unit))

    def side_by_side(pieces, ends):
        joined = placed(ends[-1], list(zip((0,) + ends, pieces)))
        return joined.reshape(RING, RING, rows, -1)

    grad_hidden, grads1 = backward_mlp(cotangent.reshape(-1, model), kept1, second_weights)
    c1, b1 = (down_of(grads1, kept1), up_of(grads1, kept1))
    cn, bn = (scatter_one(c1, "x"), scatter_one(b1, "y"))
    grad_resid, grad_packed = backward_attention(grad_hidden, grads1, kept1, second_weights)
    cn, bn, grad_packed = together(cn, bn, grad_packed)
    cf, bf = (scatter_two(c1, cn, "x"), scatter_two(b1, bn, "y"))
    grad_middle = backward_inputs(grad_resid, grad_packed, grads1, kept1, second_weights)
    a1 = side_by_side(sides_of(grads1), (3 * half, 4 * half))
    a1, cf, bf, grad_middle = together(a1, cf, bf, grad_middle)
    c1, b1 = (scatter_end(c1, cn, cf, "x"), scatter_end(b1, bn, bf, "y"))
    a1 = slices(a1, 0)
    an1 = scatter_one(a1, "z")

    grad_hidden, grads0 = backward_mlp(grad_middle, kept0, first_weights)
    c0, b0 = (down_of(grads0, kept0), up_of(grads0, kept0))
    cn, bn = (scatter_one(c0, "x"), scatter_one(b0, "y"))
    grad_resid, grad_packed = backward_attention(grad_hidden, grads0, kept0, first_weights)
    an1, cn, bn, grad_packed = together(an1, cn, bn, grad_packed)
    af1 = scatter_two(a1, an1, "z")
    cf, bf = (scatter_two(c0, cn, "x"), scatter_two(b0, bn, "y"))
    grad_first = backward_inputs(grad_resid, grad_packed, grads0, kept0, first_weights)
    flat = jnp.concatenate([vectors_of(grads0), vectors_of(grads1)], axis=2).astype(BF)
    flat = jnp.pad(flat, ((0, 0), (0, rows - vector_rows), (0, LANES - 2 * rows)))
    a0 = side_by_side([flat.reshape(-1, LANES)] + sides_of(grads0), edges[:3])
    a0, af1, cf, bf = together(a0, af1, cf, bf)
    a1 = scatter_end(a1, an1, af1, "z")
    c0, b0 = (scatter_end(c0, cn, cf, "x"), scatter_end(b0, bn, bf, "y"))

    b = jnp.stack([b0, b1]).reshape(2, RING, RING, rows // RING, -1)
    c = jnp.stack([c0, c1]).reshape(2, RING, RING, quarter, model)
    a0, a1, b, c = (slices(a0, 0), slices(a1, 0), slices(b, 2), slices(c, 2))
    an, bn, cn, dn = together(
        scatter_one(a0, "z"), scatter_one(b, "x"), scatter_one(c, "y"), scatter_one(a1, "y")
    )
    af, bf, cf, df = together(
        scatter_two(a0, an, "z"), scatter_two(b, bn, "x"), scatter_two(c, cn, "y"), scatter_two(a1, dn, "y")
    )
    a0 = slices(scatter_end(a0, an, af, "z"), 0)
    a1 = slices(scatter_end(a1, dn, df, "y").reshape(RING, rows // RING, -1), 0)
    b, c = (slices(scatter_end(b, bn, bf, "x"), 1), slices(scatter_end(c, cn, cf, "y"), 1))
    an, bn, cn, dn = together(
        scatter_one(a0, "y"), scatter_one(b, "z"), scatter_one(c, "z"), scatter_one(a1, "x")
    )
    af, bf, cf, df = together(
        scatter_two(a0, an, "y"), scatter_two(b, bn, "z"), scatter_two(c, cn, "z"), scatter_two(a1, dn, "x")
    )
    a0 = scatter_end(a0, an, af, "y")
    a1 = scatter_end(a1, dn, df, "x")
    b, c = (scatter_end(b, bn, bf, "z"), scatter_end(c, cn, cf, "z"))
    wide = shards * unit
    rest = [b[0], c[0].reshape(-1, wide), b[1], c[1].reshape(-1, wide), a1]
    rest = placed(4 * wide + 4 * half, [(n * wide, piece) for n, piece in enumerate(rest)])
    others = [hop(a0, n) for n in range(1, RING)]
    spread = [hop(rest, n) for n in range(1, RING)]
    others, spread = together(others, spread)
    a0 = (a0.astype(F32) + sum(other.astype(F32) for other in others)).astype(BF)
    whole = put(jnp.zeros((RING,) + rest.shape, BF), rest, place["x"], 0)
    for n, piece in enumerate(spread):
        whole = put(whole, piece, (place["x"] - n - 1) % RING, 0)
    rest = whole.reshape(rows, -1)
    b0, c0, b1, c1 = (rest[:, n * wide : (n + 1) * wide] for n in range(4))
    summed_first = (a0[:, LANES:], b0, c0.reshape(unit, model))
    summed_second = (rest[:, 4 * wide :], b1, c1.reshape(unit, model))
    mine, sent = zip(*(mine_of(a, b) for a, b in zip(summed_first, summed_second)))
    both = [mine_of(a, swap(b)) for a, b in zip(mine, sent)]
    both = [[v.astype(F32) for v in pair] for pair in both]
    (side_a, side_b), (up_a, up_b), (down_a, down_b) = both
    flat = a0[:vector_rows, :LANES]
    flat = flat.astype(F32) + swap(flat).astype(F32)
    flat = choose(flat[:, :rows], flat[:, rows : 2 * rows])
    qkv_a, qkv_b = (side[:, : 3 * half].reshape(rows, 3, half) for side in (side_a, side_b))
    out_a, out_b = (side[:, 3 * half :] for side in (side_a, side_b))
    up_a, up_b = (up_a.reshape(rows, shards, unit), up_b.reshape(rows, shards, unit))
    whole = [flat[n] for n in range(8)]
    grads = (
        jnp.stack([qkv_a, qkv_b], axis=2).reshape(rows, -1),
        whole[0],
        whole[1],
        jnp.concatenate([out_a, out_b], axis=1),
        whole[2],
        whole[3],
        whole[4],
        jnp.stack([up_a, up_b], axis=2).reshape(rows, -1),
        flat[8:].reshape(-1),
        jnp.concatenate([down_a, down_b], axis=0),
        whole[5],
        whole[6],
        whole[7],
    )
    shape = (1, count, 1, -1, model)
    activations = choose(middle, last).reshape(shape)
    input_grads = choose(grad_first, grad_middle).reshape(shape)
    return (activations, input_grads) + tuple(member[None] for member in grads)


def solution(mesh):
    rows = P(None, ("dp", "shard"), None, None)
    matrix = P("section", "shard", None)
    vector = P("section", "shard")
    weight_specs = (matrix, vector, vector, matrix, vector, vector, vector)
    weight_specs += (matrix, vector, matrix, vector, vector, vector)
    in_specs = (rows, P(None, ("dp", "shard")), rows) + weight_specs
    result = P("section", None, ("dp", "shard"), None, None)
    return jax.shard_map(
        per_device,
        mesh=mesh,
        in_specs=in_specs,
        out_specs=(result, result) + weight_specs,
        check_vma=False,
    )
```

```python
import jax
import jax.numpy as jnp
from jax import lax
from jax.experimental import pallas as pl
from jax.experimental.pallas import tpu as pltpu
from jax.sharding import PartitionSpec as P


HEAD_DIM = 64
EPSILON = 1e-06
TAU = 6.283185307179586
LANES = 128
RING = 4
BF = jnp.bfloat16
F32 = jnp.float32


def swap(value):
    return lax.ppermute(value, "section", [(0, 1), (1, 0)])


def pair_sum(part):
    low = part.astype(BF)
    other = swap(low)
    return low.astype(F32) + other.astype(F32)


def dot(left, right):
    return jnp.dot(left, right, preferred_element_type=F32)


def transpose_dot(left, right):
    return lax.dot_general(left, right, (((0,), (0,)), ((), ())), preferred_element_type=F32)


def dot_transposed(left, right):
    return lax.dot_general(left, right, (((1,), (1,)), ((), ())), preferred_element_type=F32)


def sum_rows(values):
    return jnp.sum(values, axis=0, keepdims=True)


def norm_rows(values):
    centered = values - jnp.mean(values, axis=-1, keepdims=True)
    inverse = lax.rsqrt(jnp.mean(centered * centered, axis=-1, keepdims=True) + EPSILON)
    return (centered * inverse, inverse)


def norm_back(grad_norm, normed, inverse):
    return inverse * (
        grad_norm
        - jnp.mean(grad_norm, axis=-1, keepdims=True)
        - normed * jnp.mean(grad_norm * normed, axis=-1, keepdims=True)
    )


def head_masks(rows):
    lane = lax.broadcasted_iota(jnp.int32, (rows, LANES), 1)
    return [lane < HEAD_DIM, lane >= HEAD_DIM]


def soft_weights_of(queries, keys, mask, seq_length):
    queries = jnp.where(mask, queries, 0.0).astype(BF)
    scores = dot_transposed(queries, keys) * HEAD_DIM ** (-0.5)
    positions = lax.broadcasted_iota(jnp.int32, scores.shape, 1)
    scores = jnp.where(positions < seq_length, scores, -1000000000.0)
    exponent = jnp.exp(scores - jnp.max(scores, axis=-1, keepdims=True))
    return exponent / jnp.sum(exponent, axis=-1, keepdims=True)


def pairs_of(packed_ref, count):
    rows, width = (packed_ref.shape[0] // count, packed_ref.shape[1] // 3)
    for n in range(count):
        for at in range(0, width, LANES):
            yield (n, pl.ds(n * rows, rows), [pl.ds(k * width + at, LANES) for k in range(3)])


def attention_kernel(lengths_ref, packed_ref, attended_ref):
    count = lengths_ref.shape[0]
    masks = head_masks(packed_ref.shape[0] // count)
    for n, rows, columns in pairs_of(packed_ref, count):
        queries, keys, values = (packed_ref[rows, at] for at in columns)
        queries = queries.astype(F32)
        parts = []
        for mask in masks:
            soft_weights = soft_weights_of(queries, keys, mask, lengths_ref[n])
            parts.append(dot(soft_weights.astype(BF), values))
        attended_ref[rows, columns[0]] = jnp.where(masks[0], *parts).astype(BF)


def attention_back_kernel(lengths_ref, packed_ref, grad_ref, out_ref):
    count = lengths_ref.shape[0]
    scaling = HEAD_DIM ** (-0.5)
    masks = head_masks(packed_ref.shape[0] // count)
    for n, rows, columns in pairs_of(packed_ref, count):
        queries, keys, values = (packed_ref[rows, at] for at in columns)
        grads = grad_ref[rows, columns[0]]
        wide_queries, wide_grads = (queries.astype(F32), grads.astype(F32))
        parts = []
        for mask in masks:
            soft_weights = soft_weights_of(wide_queries, keys, mask, lengths_ref[n])
            own = jnp.where(mask, wide_grads, 0.0).astype(BF)
            grad_soft = dot_transposed(own, values)
            mean = jnp.sum(grad_soft * soft_weights, axis=-1, keepdims=True)
            grad_scores = (soft_weights * (grad_soft - mean)).astype(BF)
            parts.append(
                (
                    dot(grad_scores, keys) * scaling,
                    transpose_dot(grad_scores, queries) * scaling,
                    transpose_dot(soft_weights.astype(BF), grads),
                )
            )
        for at, low, high in zip(columns, *parts):
            out_ref[rows, at] = jnp.where(masks[0], low, high).astype(BF)


def attention_call(kernel, width, seq_lengths, *arrays):
    rows = arrays[0].shape[0]
    vmem = pl.BlockSpec(memory_space=pltpu.VMEM)
    return pl.pallas_call(
        kernel,
        out_shape=jax.ShapeDtypeStruct((rows, width), BF),
        in_specs=[pl.BlockSpec(memory_space=pltpu.SMEM)] + [vmem] * len(arrays),
        out_specs=vmem,
        cost_estimate=pl.CostEstimate(
            flops=4 * rows * 128 * width, bytes_accessed=4 * rows * width, transcendentals=0
        ),
    )(seq_lengths, *arrays)


def forward_packed(inputs, weights):
    return (dot(inputs, weights["qkv"]) + weights["bias_qkv"]).astype(BF)


def forward_attention(inputs, packed, seq_lengths):
    attended = attention_call(attention_kernel, packed.shape[1] // 3, seq_lengths, packed)
    return (attended, dict(inputs=inputs, packed=packed, seq_lengths=seq_lengths))


def forward_hidden(attended, kept, weights):
    branch = pair_sum(dot(attended, weights["out"])) + weights["bias_out"]
    normed, inverse = norm_rows(kept["inputs"].astype(F32) + branch)
    hidden = (normed * weights["gain_attn"] + weights["shift_attn"]).astype(BF)
    upward = dot(hidden, weights["up"]) + weights["bias_up"]
    share = 0.5 + 0.5 * lax.erf(upward * 0.5**0.5)
    activated = (upward * share).astype(BF)
    slope = share + upward * jnp.exp(-0.5 * upward * upward) * TAU ** (-0.5)
    kept.update(attended=attended, normed_attn=normed, inverse_attn=inverse)
    kept.update(hidden=hidden, slope=slope)
    return activated


def forward_output(activated, kept, weights):
    mixed = pair_sum(dot(activated, weights["down"])) + weights["bias_down"]
    normed, inverse = norm_rows(kept["hidden"].astype(F32) + mixed)
    kept.update(activated=activated, normed_mlp=normed, inverse_mlp=inverse)
    return (normed * weights["gain_mlp"] + weights["shift_mlp"]).astype(BF)


def backward_mlp(grad_result, kept, weights):
    grad_result = grad_result.astype(F32)
    normed = kept["normed_mlp"]
    grad_gain = sum_rows(grad_result * normed)
    grad_shift = sum_rows(grad_result)
    grad_resid = norm_back(grad_result * weights["gain_mlp"], normed, kept["inverse_mlp"])
    grad_mixed = grad_resid.astype(BF)
    grad_upward = (dot_transposed(grad_mixed, weights["down"]) * kept["slope"]).astype(BF)
    passed = dot_transposed(grad_upward, weights["up"])
    grads = dict(
        mixed=grad_mixed,
        upward=grad_upward,
        bias_up=sum_rows(grad_upward.astype(F32)),
        bias_down=sum_rows(grad_mixed.astype(F32)),
        gain_mlp=grad_gain,
        shift_mlp=grad_shift,
    )
    return (grad_resid + pair_sum(passed), grads)


def backward_attention(grad_hidden, grads, kept, weights):
    normed = kept["normed_attn"]
    grad_resid = norm_back(grad_hidden * weights["gain_attn"], normed, kept["inverse_attn"])
    grad_branch = grad_resid.astype(BF)
    grads.update(
        gain_attn=sum_rows(grad_hidden * normed),
        shift_attn=sum_rows(grad_hidden),
        bias_out=sum_rows(grad_branch.astype(F32)),
        out=transpose_dot(kept["attended"], grad_branch).astype(BF),
    )
    packed = kept["packed"]
    grad_attended = dot_transposed(grad_branch, weights["out"]).astype(BF)
    grad_packed = attention_call(
        attention_back_kernel, packed.shape[1], kept["seq_lengths"], packed, grad_attended
    )
    return (grad_resid, grad_packed)


def backward_inputs(grad_resid, grad_packed, grads, kept, weights):
    columns = sum_rows(grad_packed.astype(F32))
    width = columns.shape[1] // 3
    grads.update(
        bias_q=columns[:, :width],
        bias_v=columns[:, 2 * width :],
        qkv=transpose_dot(kept["inputs"], grad_packed).astype(BF),
    )
    passed = dot_transposed(grad_packed, weights["qkv"])
    return (grad_resid + pair_sum(passed)).astype(BF)


def per_device(
    tokens,
    lengths,
    cotangent,
    w_qkv,
    bias_q,
    bias_v,
    w_out,
    bias_out,
    gain_attn,
    shift_attn,
    w_up,
    bias_up,
    w_down,
    bias_down,
    gain_mlp,
    shift_mlp,
):
    first = lax.axis_index("section") == 0
    shards = lax.axis_size("shard")
    rows = w_qkv.shape[1]
    model = w_qkv.shape[2] // 3
    ff = w_up.shape[2]
    half = model // 2
    unit = ff // shards // 2

    def choose(low, high):
        return jnp.where(first, low, high)

    def mine_of(low, high):
        return (choose(low, high), choose(high, low))

    shard = lax.axis_index("shard")
    place = {"x": lax.axis_index("dp"), "y": shard % RING, "z": shard // RING}

    near = {axis: at ^ choose(1, 3) for axis, at in place.items()}
    far = {axis: at ^ choose(3, 1) for axis, at in place.items()}

    def trade(value, axis, masks):
        name = "dp" if axis == "x" else "shard"
        size = lax.axis_size(name)
        stride = RING if axis == "z" else 1
        route = []
        for core in range(2):
            for at in range(size):
                position = at // stride % RING
                target = at + ((position ^ masks[core]) - position) * stride
                route.append((core * size + at, core * size + target))
        return lax.ppermute(value, ("section", name), route)

    def after(value, earlier):
        return lax.optimization_barrier((value, earlier))[0]

    def hop(value, distance):
        route = [(at, (at + distance) % RING) for at in range(RING)]
        return lax.ppermute(value, "dp", route)

    def put(whole, piece, at, dim):
        start = [0] * whole.ndim
        start[dim] = at
        return lax.dynamic_update_slice(whole, jnp.expand_dims(piece, dim), start)

    def gather_one(block, axis):
        return trade(block, axis, (1, 3))

    def gather_two(block, beside, axis):
        return trade(jnp.stack([block, beside]), axis, (3, 1))

    def gather_end(block, beside, across, axis, dim):
        whole = jnp.zeros(block.shape[:dim] + (RING,) + block.shape[dim:], block.dtype)
        whole = put(whole, block, place[axis], dim)
        whole = put(whole, beside, near[axis], dim)
        whole = put(whole, across[0], far[axis], dim)
        return put(whole, across[1], place[axis] ^ 2, dim)

    def chunk(value, at, dim):
        return lax.dynamic_index_in_dim(value, at, dim, keepdims=False)

    def slices(value, dim):
        def two(at, other):
            return jnp.stack([chunk(value, at, dim), chunk(value, other, dim)])

        return (lambda at: chunk(value, at, dim).astype(F32), two)

    def products(left, right, shape):
        def one(at):
            return transpose_dot(chunk(left, at, 0), right).reshape(shape)

        def two(at, other):
            pair = jnp.stack([chunk(left, at, 0), chunk(left, other, 0)])
            both = lax.dot_general(pair, right, (((1,), (0,)), ((), ())), preferred_element_type=F32)
            return both.astype(BF).reshape((2,) + shape)

        return (one, two)

    def scatter_one(parts, axis):
        return trade(parts[1](near[axis], place[axis] ^ 2), axis, (1, 3))

    def scatter_two(parts, beside, axis):
        sent = parts[0](far[axis]) + beside[1].astype(F32)
        return trade(sent.astype(BF), axis, (3, 1))

    def scatter_end(parts, beside, across, axis):
        kept = parts[0](place[axis]) + beside[0].astype(F32)
        return (kept + across.astype(F32)).astype(BF)

    def together(*values):
        return lax.optimization_barrier(values)

    def placed(width, pieces):
        whole = jnp.zeros((pieces[0][1].shape[0], width), BF)
        for at, piece in pieces:
            whole = lax.dynamic_update_slice(whole, piece, (0, at))
        return whole

    def parts_of(part):
        qkv = w_qkv[0].reshape(rows, 3, 2, half)[:, :, part].reshape(rows, 3 * half)
        out = w_out[0][:, part * half : (part + 1) * half]
        up = w_up[0].reshape(rows, shards, 2, unit)[:, :, part].reshape(rows, shards * unit)
        return (qkv, out, up, w_down[0][part * unit : (part + 1) * unit])

    lines = [
        v.reshape(-1, rows)
        for v in (
            bias_q,
            bias_v,
            bias_out,
            gain_attn,
            shift_attn,
            bias_down,
            gain_mlp,
            shift_mlp,
            bias_up,
        )
    ]
    vectors, at = (jnp.zeros((rows, LANES), BF), 0)
    for line in lines:
        height = line.shape[0]
        vectors += jnp.pad(line, ((at, rows - at - height), (0, LANES - rows)))
        at += height
    vector_rows = at
    split = [mine_of(low, high) for low, high in zip(parts_of(0), parts_of(1))]
    kept_part = (vectors,) + tuple(low for low, high in split)
    sent_part = (vectors,) + tuple(high for low, high in split)
    got_part = tuple(swap(member) for member in sent_part)
    blocks = [mine_of(own, got) for own, got in zip(kept_part, got_part)]
    edges = (LANES, LANES + 3 * half, LANES + 4 * half, LANES + 4 * half + shards * unit)

    quarter = unit // RING

    def quarter_of(block):
        return chunk(block.reshape(RING, quarter, model), place["x"], 0)

    span = quarter * model // rows

    def gathered(layer, extra):
        pieces = list(zip((0,) + edges, [b[layer] for b in blocks[:4]]))
        pieces += [(edges[3] + n * span, piece) for n, piece in enumerate(extra)]
        return placed(edges[3] + len(extra) * span, pieces)

    def whole(block):
        return lax.all_gather(block, "shard", axis=0, tiled=True)

    side0 = whole(gathered(0, [quarter_of(block).reshape(rows, span) for block in blocks[4]]))
    side1 = whole(after(gathered(1, []), side0))
    c0, c1 = (
        side0[:, edges[3] + n * span : edges[3] + (n + 1) * span].reshape(shards, quarter, model)
        for n in range(2)
    )

    def arranged(attn, down):
        flat = attn[:, :LANES].reshape(shards, rows, LANES)[:, :vector_rows, :rows].astype(F32)
        lines = lax.optimization_barrier(flat[:, :8].transpose(1, 0, 2).reshape(8, model))
        whole = [lines[n : n + 1] for n in range(8)]
        bias_up_part = flat[:, 8:].reshape(shards, 2, unit)
        bias_up_part = choose(bias_up_part[:, 0], bias_up_part[:, 1]).reshape(1, -1)
        bias_q_part = choose(whole[0][:, :half], whole[0][:, half:])
        bias_v_part = choose(whole[1][:, :half], whole[1][:, half:])
        out = attn[:, edges[1] : edges[2]]
        held, handed = mine_of(out[:half], out[half:])
        arrived = swap(handed)
        return dict(
            qkv=attn[:, LANES : edges[1]],
            out=jnp.concatenate(mine_of(held, arrived), axis=1),
            up=attn[:, edges[2] :],
            down=down,
            bias_qkv=jnp.concatenate([bias_q_part, 0.0 * bias_q_part, bias_v_part], axis=1),
            bias_out=whole[2],
            gain_attn=whole[3],
            shift_attn=whole[4],
            bias_down=whole[5],
            gain_mlp=whole[6],
            shift_mlp=whole[7],
            bias_up=bias_up_part,
        )

    def vectors_of(grads):
        def widened(part):
            return jnp.concatenate([choose(part, 0.0), choose(0.0, part)], axis=1)

        names = ("bias_out", "gain_attn", "shift_attn", "bias_down", "gain_mlp", "shift_mlp")
        lines = [widened(grads["bias_q"]), widened(grads["bias_v"])]
        lines = jnp.concatenate(lines + [0.5 * grads[name] for name in names], axis=0)
        lines, spread = lax.optimization_barrier((lines, grads["bias_up"]))
        lines = lines.reshape(8, shards, rows).transpose(1, 0, 2)
        spread = widened(spread.reshape(shards, unit)).reshape(shards, -1, rows)
        return jnp.concatenate([lines, spread], axis=1)

    def sides_of(grads):
        held, handed = mine_of(grads["out"][:, :half], grads["out"][:, half:])
        return [grads["qkv"], jnp.concatenate(mine_of(held, swap(handed)), axis=0)]

    count = tokens.shape[0]
    seq_lengths = lengths[:, 0]

    first_weights = arranged(side0[:, : edges[3]], None)
    cn = gather_one(c0, "x")
    packed = forward_packed(tokens.reshape(-1, model), first_weights)
    cn, packed = together(cn, packed)
    cf = gather_two(c0, cn, "x")
    attended, kept0 = forward_attention(tokens.reshape(-1, model), packed, seq_lengths)
    activated = forward_hidden(attended, kept0, first_weights)
    cf, activated = together(cf, activated)
    first_weights["down"] = gather_end(c0, cn, cf, "x", 1).reshape(-1, model)
    cn = gather_one(after(c1, cf), "x")
    middle = forward_output(activated, kept0, first_weights)
    middle, side1 = together(middle, side1)
    second_weights = arranged(side1, None)
    packed = forward_packed(middle, second_weights)
    cn, packed = together(cn, packed)
    cf = gather_two(c1, cn, "x")
    attended, kept1 = forward_attention(middle, packed, seq_lengths)
    activated = forward_hidden(attended, kept1, second_weights)
    cf, activated = together(cf, activated)
    second_weights["down"] = gather_end(c1, cn, cf, "x", 1).reshape(-1, model)
    last = forward_output(activated, kept1, second_weights)

    def down_of(grads, kept):
        left = kept["activated"].reshape(-1, shards, RING, quarter).transpose(2, 0, 1, 3)
        left = left.reshape(RING, -1, shards * quarter)
        return products(left, grads["mixed"], (shards, quarter, model))

    def up_of(grads, kept):
        left = kept["hidden"].reshape(-1, RING, RING, rows).transpose(2, 0, 1, 3)
        return products(left.reshape(RING, -1, RING * rows), grads["upward"], (RING, rows, shards * unit))

    def side_by_side(pieces, ends):
        joined = placed(ends[-1], list(zip((0,) + ends, pieces)))
        return joined.reshape(RING, RING, rows, -1)

    grad_hidden, grads1 = backward_mlp(cotangent.reshape(-1, model), kept1, second_weights)
    c1, b1 = (down_of(grads1, kept1), up_of(grads1, kept1))
    cn, bn = (scatter_one(c1, "x"), scatter_one(b1, "y"))
    grad_resid, grad_packed = backward_attention(grad_hidden, grads1, kept1, second_weights)
    cn, bn, grad_packed = together(cn, bn, grad_packed)
    cf, bf = (scatter_two(c1, cn, "x"), scatter_two(b1, bn, "y"))
    grad_middle = backward_inputs(grad_resid, grad_packed, grads1, kept1, second_weights)
    a1 = side_by_side(sides_of(grads1), (3 * half, 4 * half))
    a1, cf, bf, grad_middle = together(a1, cf, bf, grad_middle)
    c1, b1 = (scatter_end(c1, cn, cf, "x"), scatter_end(b1, bn, bf, "y"))
    a1 = slices(a1, 0)
    an1 = scatter_one(a1, "z")

    grad_hidden, grads0 = backward_mlp(grad_middle, kept0, first_weights)
    c0, b0 = (down_of(grads0, kept0), up_of(grads0, kept0))
    cn, bn = (scatter_one(c0, "x"), scatter_one(b0, "y"))
    grad_resid, grad_packed = backward_attention(grad_hidden, grads0, kept0, first_weights)
    an1, cn, bn, grad_packed = together(an1, cn, bn, grad_packed)
    af1 = scatter_two(a1, an1, "z")
    cf, bf = (scatter_two(c0, cn, "x"), scatter_two(b0, bn, "y"))
    grad_first = backward_inputs(grad_resid, grad_packed, grads0, kept0, first_weights)
    flat = jnp.concatenate([vectors_of(grads0), vectors_of(grads1)], axis=2).astype(BF)
    flat = jnp.pad(flat, ((0, 0), (0, rows - vector_rows), (0, LANES - 2 * rows)))
    a0 = side_by_side([flat.reshape(-1, LANES)] + sides_of(grads0), edges[:3])
    a0, af1, cf, bf = together(a0, af1, cf, bf)
    a1 = scatter_end(a1, an1, af1, "z")
    c0, b0 = (scatter_end(c0, cn, cf, "x"), scatter_end(b0, bn, bf, "y"))

    b = jnp.stack([b0, b1]).reshape(2, RING, RING, rows // RING, -1)
    c = jnp.stack([c0, c1]).reshape(2, RING, RING, quarter, model)
    a0, a1, b, c = (slices(a0, 0), slices(a1, 0), slices(b, 2), slices(c, 2))
    an, bn, cn, dn = together(
        scatter_one(a0, "z"), scatter_one(b, "x"), scatter_one(c, "y"), scatter_one(a1, "y")
    )
    af, bf, cf, df = together(
        scatter_two(a0, an, "z"), scatter_two(b, bn, "x"), scatter_two(c, cn, "y"), scatter_two(a1, dn, "y")
    )
    a0 = slices(scatter_end(a0, an, af, "z"), 0)
    a1 = slices(scatter_end(a1, dn, df, "y").reshape(RING, rows // RING, -1), 0)
    b, c = (slices(scatter_end(b, bn, bf, "x"), 1), slices(scatter_end(c, cn, cf, "y"), 1))
    an, bn, cn, dn = together(
        scatter_one(a0, "y"), scatter_one(b, "z"), scatter_one(c, "z"), scatter_one(a1, "x")
    )
    af, bf, cf, df = together(
        scatter_two(a0, an, "y"), scatter_two(b, bn, "z"), scatter_two(c, cn, "z"), scatter_two(a1, dn, "x")
    )
    a0 = scatter_end(a0, an, af, "y")
    a1 = scatter_end(a1, dn, df, "x")
    b, c = (scatter_end(b, bn, bf, "z"), scatter_end(c, cn, cf, "z"))
    wide = shards * unit
    rest = [b[0], c[0].reshape(-1, wide), b[1], c[1].reshape(-1, wide), a1]
    rest = placed(4 * wide + 4 * half, [(n * wide, piece) for n, piece in enumerate(rest)])
    others = [hop(a0, n) for n in range(1, RING)]
    spread = [hop(rest, n) for n in range(1, RING)]
    others, spread = together(others, spread)
    a0 = (a0.astype(F32) + sum(other.astype(F32) for other in others)).astype(BF)
    whole = put(jnp.zeros((RING,) + rest.shape, BF), rest, place["x"], 0)
    for n, piece in enumerate(spread):
        whole = put(whole, piece, (place["x"] - n - 1) % RING, 0)
    rest = whole.reshape(rows, -1)
    b0, c0, b1, c1 = (rest[:, n * wide : (n + 1) * wide] for n in range(4))
    summed_first = (a0[:, LANES:], b0, c0.reshape(unit, model))
    summed_second = (rest[:, 4 * wide :], b1, c1.reshape(unit, model))
    mine, sent = zip(*(mine_of(a, b) for a, b in zip(summed_first, summed_second)))
    both = [mine_of(a, swap(b)) for a, b in zip(mine, sent)]
    both = [[v.astype(F32) for v in pair] for pair in both]
    (side_a, side_b), (up_a, up_b), (down_a, down_b) = both
    flat = a0[:vector_rows, :LANES]
    flat = flat.astype(F32) + swap(flat).astype(F32)
    flat = choose(flat[:, :rows], flat[:, rows : 2 * rows])
    qkv_a, qkv_b = (side[:, : 3 * half].reshape(rows, 3, half) for side in (side_a, side_b))
    out_a, out_b = (side[:, 3 * half :] for side in (side_a, side_b))
    up_a, up_b = (up_a.reshape(rows, shards, unit), up_b.reshape(rows, shards, unit))
    whole = [flat[n] for n in range(8)]
    grads = (
        jnp.stack([qkv_a, qkv_b], axis=2).reshape(rows, -1),
        whole[0],
        whole[1],
        jnp.concatenate([out_a, out_b], axis=1),
        whole[2],
        whole[3],
        whole[4],
        jnp.stack([up_a, up_b], axis=2).reshape(rows, -1),
        flat[8:].reshape(-1),
        jnp.concatenate([down_a, down_b], axis=0),
        whole[5],
        whole[6],
        whole[7],
    )
    shape = (1, count, 1, -1, model)
    activations = choose(middle, last).reshape(shape)
    input_grads = choose(grad_first, grad_middle).reshape(shape)
    return (activations, input_grads) + tuple(member[None] for member in grads)


def solution(mesh):
    rows = P(None, ("dp", "shard"), None, None)
    matrix = P("section", "shard", None)
    vector = P("section", "shard")
    weight_specs = (matrix, vector, vector, matrix, vector, vector, vector)
    weight_specs += (matrix, vector, matrix, vector, vector, vector)
    in_specs = (rows, P(None, ("dp", "shard")), rows) + weight_specs
    result = P("section", None, ("dp", "shard"), None, None)
    return jax.shard_map(
        per_device,
        mesh=mesh,
        in_specs=in_specs,
        out_specs=(result, result) + weight_specs,
        check_vma=False,
    )
```

```python
import jax
import jax.numpy as jnp
from jax import lax
from jax.experimental import pallas as pl
from jax.experimental.pallas import tpu as pltpu
from jax.sharding import PartitionSpec as P


HEAD_DIM = 64
EPSILON = 1e-06
TAU = 6.283185307179586
LANES = 128
RING = 4
BF = jnp.bfloat16
F32 = jnp.float32


def swap(value):
    return lax.ppermute(value, "section", [(0, 1), (1, 0)])


def pair_sum(part):
    low = part.astype(BF)
    other = swap(low)
    return low.astype(F32) + other.astype(F32)


def dot(left, right):
    return jnp.dot(left, right, preferred_element_type=F32)


def transpose_dot(left, right):
    return lax.dot_general(left, right, (((0,), (0,)), ((), ())), preferred_element_type=F32)


def dot_transposed(left, right):
    return lax.dot_general(left, right, (((1,), (1,)), ((), ())), preferred_element_type=F32)


def sum_rows(values):
    return jnp.sum(values, axis=0, keepdims=True)


def norm_rows(values):
    centered = values - jnp.mean(values, axis=-1, keepdims=True)
    inverse = lax.rsqrt(jnp.mean(centered * centered, axis=-1, keepdims=True) + EPSILON)
    return (centered * inverse, inverse)


def norm_back(grad_norm, normed, inverse):
    return inverse * (
        grad_norm
        - jnp.mean(grad_norm, axis=-1, keepdims=True)
        - normed * jnp.mean(grad_norm * normed, axis=-1, keepdims=True)
    )


def head_masks(rows):
    lane = lax.broadcasted_iota(jnp.int32, (rows, LANES), 1)
    return [lane < HEAD_DIM, lane >= HEAD_DIM]


def soft_weights_of(queries, keys, mask, seq_length):
    queries = jnp.where(mask, queries, 0.0).astype(BF)
    scores = dot_transposed(queries, keys) * HEAD_DIM ** (-0.5)
    positions = lax.broadcasted_iota(jnp.int32, scores.shape, 1)
    scores = jnp.where(positions < seq_length, scores, -1000000000.0)
    exponent = jnp.exp(scores - jnp.max(scores, axis=-1, keepdims=True))
    return exponent / jnp.sum(exponent, axis=-1, keepdims=True)


def pairs_of(packed_ref, count):
    rows, width = (packed_ref.shape[0] // count, packed_ref.shape[1] // 3)
    for n in range(count):
        for at in range(0, width, LANES):
            yield (n, pl.ds(n * rows, rows), [pl.ds(k * width + at, LANES) for k in range(3)])


def attention_kernel(lengths_ref, packed_ref, attended_ref):
    count = lengths_ref.shape[0]
    masks = head_masks(packed_ref.shape[0] // count)
    for n, rows, columns in pairs_of(packed_ref, count):
        queries, keys, values = (packed_ref[rows, at] for at in columns)
        queries = queries.astype(F32)
        parts = []
        for mask in masks:
            soft_weights = soft_weights_of(queries, keys, mask, lengths_ref[n])
            parts.append(dot(soft_weights.astype(BF), values))
        attended_ref[rows, columns[0]] = jnp.where(masks[0], *parts).astype(BF)


def attention_back_kernel(lengths_ref, packed_ref, grad_ref, out_ref):
    count = lengths_ref.shape[0]
    scaling = HEAD_DIM ** (-0.5)
    masks = head_masks(packed_ref.shape[0] // count)
    for n, rows, columns in pairs_of(packed_ref, count):
        queries, keys, values = (packed_ref[rows, at] for at in columns)
        grads = grad_ref[rows, columns[0]]
        wide_queries, wide_grads = (queries.astype(F32), grads.astype(F32))
        parts = []
        for mask in masks:
            soft_weights = soft_weights_of(wide_queries, keys, mask, lengths_ref[n])
            own = jnp.where(mask, wide_grads, 0.0).astype(BF)
            grad_soft = dot_transposed(own, values)
            mean = jnp.sum(grad_soft * soft_weights, axis=-1, keepdims=True)
            grad_scores = (soft_weights * (grad_soft - mean)).astype(BF)
            parts.append(
                (
                    dot(grad_scores, keys) * scaling,
                    transpose_dot(grad_scores, queries) * scaling,
                    transpose_dot(soft_weights.astype(BF), grads),
                )
            )
        for at, low, high in zip(columns, *parts):
            out_ref[rows, at] = jnp.where(masks[0], low, high).astype(BF)


def attention_call(kernel, width, seq_lengths, *arrays):
    rows = arrays[0].shape[0]
    vmem = pl.BlockSpec(memory_space=pltpu.VMEM)
    return pl.pallas_call(
        kernel,
        out_shape=jax.ShapeDtypeStruct((rows, width), BF),
        in_specs=[pl.BlockSpec(memory_space=pltpu.SMEM)] + [vmem] * len(arrays),
        out_specs=vmem,
        cost_estimate=pl.CostEstimate(
            flops=4 * rows * 128 * width, bytes_accessed=4 * rows * width, transcendentals=0
        ),
    )(seq_lengths, *arrays)


def forward_packed(inputs, weights):
    return (dot(inputs, weights["qkv"]) + weights["bias_qkv"]).astype(BF)


def forward_attention(inputs, packed, seq_lengths):
    attended = attention_call(attention_kernel, packed.shape[1] // 3, seq_lengths, packed)
    return (attended, dict(inputs=inputs, packed=packed, seq_lengths=seq_lengths))


def forward_hidden(attended, kept, weights):
    branch = pair_sum(dot(attended, weights["out"])) + weights["bias_out"]
    normed, inverse = norm_rows(kept["inputs"].astype(F32) + branch)
    hidden = (normed * weights["gain_attn"] + weights["shift_attn"]).astype(BF)
    upward = dot(hidden, weights["up"]) + weights["bias_up"]
    share = 0.5 + 0.5 * lax.erf(upward * 0.5**0.5)
    activated = (upward * share).astype(BF)
    slope = share + upward * jnp.exp(-0.5 * upward * upward) * TAU ** (-0.5)
    kept.update(attended=attended, normed_attn=normed, inverse_attn=inverse)
    kept.update(hidden=hidden, slope=slope)
    return activated


def forward_output(activated, kept, weights):
    mixed = pair_sum(dot(activated, weights["down"])) + weights["bias_down"]
    normed, inverse = norm_rows(kept["hidden"].astype(F32) + mixed)
    kept.update(activated=activated, normed_mlp=normed, inverse_mlp=inverse)
    return (normed * weights["gain_mlp"] + weights["shift_mlp"]).astype(BF)


def backward_mlp(grad_result, kept, weights):
    grad_result = grad_result.astype(F32)
    normed = kept["normed_mlp"]
    grad_gain = sum_rows(grad_result * normed)
    grad_shift = sum_rows(grad_result)
    grad_resid = norm_back(grad_result * weights["gain_mlp"], normed, kept["inverse_mlp"])
    grad_mixed = grad_resid.astype(BF)
    grad_upward = (dot_transposed(grad_mixed, weights["down"]) * kept["slope"]).astype(BF)
    passed = dot_transposed(grad_upward, weights["up"])
    grads = dict(
        mixed=grad_mixed,
        upward=grad_upward,
        bias_up=sum_rows(grad_upward.astype(F32)),
        bias_down=sum_rows(grad_mixed.astype(F32)),
        gain_mlp=grad_gain,
        shift_mlp=grad_shift,
    )
    return (grad_resid + pair_sum(passed), grads)


def backward_attention(grad_hidden, grads, kept, weights):
    normed = kept["normed_attn"]
    grad_resid = norm_back(grad_hidden * weights["gain_attn"], normed, kept["inverse_attn"])
    grad_branch = grad_resid.astype(BF)
    grads.update(
        gain_attn=sum_rows(grad_hidden * normed),
        shift_attn=sum_rows(grad_hidden),
        bias_out=sum_rows(grad_branch.astype(F32)),
        out=transpose_dot(kept["attended"], grad_branch).astype(BF),
    )
    packed = kept["packed"]
    grad_attended = dot_transposed(grad_branch, weights["out"]).astype(BF)
    grad_packed = attention_call(
        attention_back_kernel, packed.shape[1], kept["seq_lengths"], packed, grad_attended
    )
    return (grad_resid, grad_packed)


def backward_inputs(grad_resid, grad_packed, grads, kept, weights):
    columns = sum_rows(grad_packed.astype(F32))
    width = columns.shape[1] // 3
    grads.update(
        bias_q=columns[:, :width],
        bias_v=columns[:, 2 * width :],
        qkv=transpose_dot(kept["inputs"], grad_packed).astype(BF),
    )
    passed = dot_transposed(grad_packed, weights["qkv"])
    return (grad_resid + pair_sum(passed)).astype(BF)


def per_device(
    tokens,
    lengths,
    cotangent,
    w_qkv,
    bias_q,
    bias_v,
    w_out,
    bias_out,
    gain_attn,
    shift_attn,
    w_up,
    bias_up,
    w_down,
    bias_down,
    gain_mlp,
    shift_mlp,
):
    first = lax.axis_index("section") == 0
    shards = lax.axis_size("shard")
    rows = w_qkv.shape[1]
    model = w_qkv.shape[2] // 3
    ff = w_up.shape[2]
    half = model // 2
    unit = ff // shards // 2

    def choose(low, high):
        return jnp.where(first, low, high)

    def mine_of(low, high):
        return (choose(low, high), choose(high, low))

    shard = lax.axis_index("shard")
    place = {"x": lax.axis_index("dp"), "y": shard % RING, "z": shard // RING}

    near = {axis: at ^ choose(1, 3) for axis, at in place.items()}
    far = {axis: at ^ choose(3, 1) for axis, at in place.items()}

    def trade(value, axis, masks):
        name = "dp" if axis == "x" else "shard"
        size = lax.axis_size(name)
        stride = RING if axis == "z" else 1
        route = []
        for core in range(2):
            for at in range(size):
                position = at // stride % RING
                target = at + ((position ^ masks[core]) - position) * stride
                route.append((core * size + at, core * size + target))
        return lax.ppermute(value, ("section", name), route)

    def after(value, earlier):
        return lax.optimization_barrier((value, earlier))[0]

    def hop(value, distance):
        route = [(at, (at + distance) % RING) for at in range(RING)]
        return lax.ppermute(value, "dp", route)

    def put(whole, piece, at, dim):
        start = [0] * whole.ndim
        start[dim] = at
        return lax.dynamic_update_slice(whole, jnp.expand_dims(piece, dim), start)

    def gather_one(block, axis):
        return trade(block, axis, (1, 3))

    def gather_two(block, beside, axis):
        return trade(jnp.stack([block, beside]), axis, (3, 1))

    def gather_end(block, beside, across, axis, dim):
        whole = jnp.zeros(block.shape[:dim] + (RING,) + block.shape[dim:], block.dtype)
        whole = put(whole, block, place[axis], dim)
        whole = put(whole, beside, near[axis], dim)
        whole = put(whole, across[0], far[axis], dim)
        return put(whole, across[1], place[axis] ^ 2, dim)

    def chunk(value, at, dim):
        return lax.dynamic_index_in_dim(value, at, dim, keepdims=False)

    def slices(value, dim):
        def two(at, other):
            return jnp.stack([chunk(value, at, dim), chunk(value, other, dim)])

        return (lambda at: chunk(value, at, dim).astype(F32), two)

    def products(left, right, shape):
        def one(at):
            return transpose_dot(chunk(left, at, 0), right).reshape(shape)

        def two(at, other):
            pair = jnp.stack([chunk(left, at, 0), chunk(left, other, 0)])
            both = lax.dot_general(pair, right, (((1,), (0,)), ((), ())), preferred_element_type=F32)
            return both.astype(BF).reshape((2,) + shape)

        return (one, two)

    def scatter_one(parts, axis):
        return trade(parts[1](near[axis], place[axis] ^ 2), axis, (1, 3))

    def scatter_two(parts, beside, axis):
        sent = parts[0](far[axis]) + beside[1].astype(F32)
        return trade(sent.astype(BF), axis, (3, 1))

    def scatter_end(parts, beside, across, axis):
        kept = parts[0](place[axis]) + beside[0].astype(F32)
        return (kept + across.astype(F32)).astype(BF)

    def together(*values):
        return lax.optimization_barrier(values)

    def placed(width, pieces):
        whole = jnp.zeros((pieces[0][1].shape[0], width), BF)
        for at, piece in pieces:
            whole = lax.dynamic_update_slice(whole, piece, (0, at))
        return whole

    def parts_of(part):
        qkv = w_qkv[0].reshape(rows, 3, 2, half)[:, :, part].reshape(rows, 3 * half)
        out = w_out[0][:, part * half : (part + 1) * half]
        up = w_up[0].reshape(rows, shards, 2, unit)[:, :, part].reshape(rows, shards * unit)
        return (qkv, out, up, w_down[0][part * unit : (part + 1) * unit])

    lines = [
        v.reshape(-1, rows)
        for v in (
            bias_q,
            bias_v,
            bias_out,
            gain_attn,
            shift_attn,
            bias_down,
            gain_mlp,
            shift_mlp,
            bias_up,
        )
    ]
    vectors, at = (jnp.zeros((rows, LANES), BF), 0)
    for line in lines:
        height = line.shape[0]
        vectors += jnp.pad(line, ((at, rows - at - height), (0, LANES - rows)))
        at += height
    vector_rows = at
    split = [mine_of(low, high) for low, high in zip(parts_of(0), parts_of(1))]
    kept_part = (vectors,) + tuple(low for low, high in split)
    sent_part = (vectors,) + tuple(high for low, high in split)
    got_part = tuple(swap(member) for member in sent_part)
    blocks = [mine_of(own, got) for own, got in zip(kept_part, got_part)]
    edges = (LANES, LANES + 3 * half, LANES + 4 * half, LANES + 4 * half + shards * unit)

    quarter = unit // RING

    def quarter_of(block):
        return chunk(block.reshape(RING, quarter, model), place["x"], 0)

    span = quarter * model // rows

    def gathered(layer, extra):
        pieces = list(zip((0,) + edges, [b[layer] for b in blocks[:4]]))
        pieces += [(edges[3] + n * span, piece) for n, piece in enumerate(extra)]
        return placed(edges[3] + len(extra) * span, pieces)

    def whole(block):
        return lax.all_gather(block, "shard", axis=0, tiled=True)

    side0 = whole(gathered(0, [quarter_of(block).reshape(rows, span) for block in blocks[4]]))
    side1 = whole(after(gathered(1, []), side0))
    c0, c1 = (
        side0[:, edges[3] + n * span : edges[3] + (n + 1) * span].reshape(shards, quarter, model)
        for n in range(2)
    )

    def arranged(attn, down):
        flat = attn[:, :LANES].reshape(shards, rows, LANES)[:, :vector_rows, :rows].astype(F32)
        lines = lax.optimization_barrier(flat[:, :8].transpose(1, 0, 2).reshape(8, model))
        whole = [lines[n : n + 1] for n in range(8)]
        bias_up_part = flat[:, 8:].reshape(shards, 2, unit)
        bias_up_part = choose(bias_up_part[:, 0], bias_up_part[:, 1]).reshape(1, -1)
        bias_q_part = choose(whole[0][:, :half], whole[0][:, half:])
        bias_v_part = choose(whole[1][:, :half], whole[1][:, half:])
        out = attn[:, edges[1] : edges[2]]
        held, handed = mine_of(out[:half], out[half:])
        arrived = swap(handed)
        return dict(
            qkv=attn[:, LANES : edges[1]],
            out=jnp.concatenate(mine_of(held, arrived), axis=1),
            up=attn[:, edges[2] :],
            down=down,
            bias_qkv=jnp.concatenate([bias_q_part, 0.0 * bias_q_part, bias_v_part], axis=1),
            bias_out=whole[2],
            gain_attn=whole[3],
            shift_attn=whole[4],
            bias_down=whole[5],
            gain_mlp=whole[6],
            shift_mlp=whole[7],
            bias_up=bias_up_part,
        )

    def vectors_of(grads):
        def widened(part):
            return jnp.concatenate([choose(part, 0.0), choose(0.0, part)], axis=1)

        names = ("bias_out", "gain_attn", "shift_attn", "bias_down", "gain_mlp", "shift_mlp")
        lines = [widened(grads["bias_q"]), widened(grads["bias_v"])]
        lines = jnp.concatenate(lines + [0.5 * grads[name] for name in names], axis=0)
        lines, spread = lax.optimization_barrier((lines, grads["bias_up"]))
        lines = lines.reshape(8, shards, rows).transpose(1, 0, 2)
        spread = widened(spread.reshape(shards, unit)).reshape(shards, -1, rows)
        return jnp.concatenate([lines, spread], axis=1)

    def sides_of(grads):
        held, handed = mine_of(grads["out"][:, :half], grads["out"][:, half:])
        return [grads["qkv"], jnp.concatenate(mine_of(held, swap(handed)), axis=0)]

    count = tokens.shape[0]
    seq_lengths = lengths[:, 0]

    first_weights = arranged(side0[:, : edges[3]], None)
    cn = gather_one(c0, "x")
    packed = forward_packed(tokens.reshape(-1, model), first_weights)
    cn, packed = together(cn, packed)
    cf = gather_two(c0, cn, "x")
    attended, kept0 = forward_attention(tokens.reshape(-1, model), packed, seq_lengths)
    activated = forward_hidden(attended, kept0, first_weights)
    cf, activated = together(cf, activated)
    first_weights["down"] = gather_end(c0, cn, cf, "x", 1).reshape(-1, model)
    cn = gather_one(after(c1, cf), "x")
    middle = forward_output(activated, kept0, first_weights)
    middle, side1 = together(middle, side1)
    second_weights = arranged(side1, None)
    packed = forward_packed(middle, second_weights)
    cn, packed = together(cn, packed)
    cf = gather_two(c1, cn, "x")
    attended, kept1 = forward_attention(middle, packed, seq_lengths)
    activated = forward_hidden(attended, kept1, second_weights)
    cf, activated = together(cf, activated)
    second_weights["down"] = gather_end(c1, cn, cf, "x", 1).reshape(-1, model)
    last = forward_output(activated, kept1, second_weights)

    def down_of(grads, kept):
        left = kept["activated"].reshape(-1, shards, RING, quarter).transpose(2, 0, 1, 3)
        left = left.reshape(RING, -1, shards * quarter)
        return products(left, grads["mixed"], (shards, quarter, model))

    def up_of(grads, kept):
        left = kept["hidden"].reshape(-1, RING, RING, rows).transpose(2, 0, 1, 3)
        return products(left.reshape(RING, -1, RING * rows), grads["upward"], (RING, rows, shards * unit))

    def side_by_side(pieces, ends):
        joined = placed(ends[-1], list(zip((0,) + ends, lax.optimization_barrier(pieces))))
        return joined.reshape(RING, RING, rows, -1)

    grad_hidden, grads1 = backward_mlp(cotangent.reshape(-1, model), kept1, second_weights)
    c1, b1 = (down_of(grads1, kept1), up_of(grads1, kept1))
    cn, bn = (scatter_one(c1, "x"), scatter_one(b1, "y"))
    grad_resid, grad_packed = backward_attention(grad_hidden, grads1, kept1, second_weights)
    cn, bn, grad_packed = together(cn, bn, grad_packed)
    cf, bf = (scatter_two(c1, cn, "x"), scatter_two(b1, bn, "y"))
    grad_middle = backward_inputs(grad_resid, grad_packed, grads1, kept1, second_weights)
    a1 = side_by_side(sides_of(grads1), (3 * half, 4 * half))
    a1, cf, bf, grad_middle = together(a1, cf, bf, grad_middle)
    c1, b1 = (scatter_end(c1, cn, cf, "x"), scatter_end(b1, bn, bf, "y"))
    a1 = slices(a1, 0)
    an1 = scatter_one(a1, "z")

    grad_hidden, grads0 = backward_mlp(grad_middle, kept0, first_weights)
    c0, b0 = (down_of(grads0, kept0), up_of(grads0, kept0))
    cn, bn = (scatter_one(c0, "x"), scatter_one(b0, "y"))
    grad_resid, grad_packed = backward_attention(grad_hidden, grads0, kept0, first_weights)
    an1, cn, bn, grad_packed = together(an1, cn, bn, grad_packed)
    af1 = scatter_two(a1, an1, "z")
    cf, bf = (scatter_two(c0, cn, "x"), scatter_two(b0, bn, "y"))
    grad_first = backward_inputs(grad_resid, grad_packed, grads0, kept0, first_weights)
    flat = jnp.concatenate([vectors_of(grads0), vectors_of(grads1)], axis=2).astype(BF)
    flat = jnp.pad(flat, ((0, 0), (0, rows - vector_rows), (0, LANES - 2 * rows)))
    a0 = side_by_side([flat.reshape(-1, LANES)] + sides_of(grads0), edges[:3])
    a0, af1, cf, bf = together(a0, af1, cf, bf)
    a1 = scatter_end(a1, an1, af1, "z")
    c0, b0 = (scatter_end(c0, cn, cf, "x"), scatter_end(b0, bn, bf, "y"))

    b = jnp.stack([b0, b1]).reshape(2, RING, RING, rows // RING, -1)
    c = jnp.stack([c0, c1]).reshape(2, RING, RING, quarter, model)
    a0, a1, b, c = (slices(a0, 0), slices(a1, 0), slices(b, 2), slices(c, 2))
    an, bn, cn, dn = together(
        scatter_one(a0, "z"), scatter_one(b, "x"), scatter_one(c, "y"), scatter_one(a1, "y")
    )
    af, bf, cf, df = together(
        scatter_two(a0, an, "z"), scatter_two(b, bn, "x"), scatter_two(c, cn, "y"), scatter_two(a1, dn, "y")
    )
    a0 = slices(scatter_end(a0, an, af, "z"), 0)
    a1 = slices(scatter_end(a1, dn, df, "y").reshape(RING, rows // RING, -1), 0)
    b, c = (slices(scatter_end(b, bn, bf, "x"), 1), slices(scatter_end(c, cn, cf, "y"), 1))
    an, bn, cn, dn = together(
        scatter_one(a0, "y"), scatter_one(b, "z"), scatter_one(c, "z"), scatter_one(a1, "x")
    )
    af, bf, cf, df = together(
        scatter_two(a0, an, "y"), scatter_two(b, bn, "z"), scatter_two(c, cn, "z"), scatter_two(a1, dn, "x")
    )
    a0 = scatter_end(a0, an, af, "y")
    a1 = scatter_end(a1, dn, df, "x")
    b, c = (scatter_end(b, bn, bf, "z"), scatter_end(c, cn, cf, "z"))
    wide = shards * unit
    rest = [b[0], c[0].reshape(-1, wide), b[1], c[1].reshape(-1, wide), a1]
    rest = placed(4 * wide + 4 * half, [(n * wide, piece) for n, piece in enumerate(rest)])
    others = [hop(a0, n) for n in range(1, RING)]
    spread = [hop(rest, n) for n in range(1, RING)]
    others, spread = together(others, spread)
    a0 = (a0.astype(F32) + sum(other.astype(F32) for other in others)).astype(BF)
    whole = put(jnp.zeros((RING,) + rest.shape, BF), rest, place["x"], 0)
    for n, piece in enumerate(spread):
        whole = put(whole, piece, (place["x"] - n - 1) % RING, 0)
    rest = whole.reshape(rows, -1)
    b0, c0, b1, c1 = (rest[:, n * wide : (n + 1) * wide] for n in range(4))
    summed_first = (a0[:, LANES:], b0, c0.reshape(unit, model))
    summed_second = (rest[:, 4 * wide :], b1, c1.reshape(unit, model))
    mine, sent = zip(*(mine_of(a, b) for a, b in zip(summed_first, summed_second)))
    both = [mine_of(a, swap(b)) for a, b in zip(mine, sent)]
    both = [[v.astype(F32) for v in pair] for pair in both]
    (side_a, side_b), (up_a, up_b), (down_a, down_b) = both
    flat = a0[:vector_rows, :LANES]
    flat = flat.astype(F32) + swap(flat).astype(F32)
    flat = choose(flat[:, :rows], flat[:, rows : 2 * rows])
    qkv_a, qkv_b = (side[:, : 3 * half].reshape(rows, 3, half) for side in (side_a, side_b))
    out_a, out_b = (side[:, 3 * half :] for side in (side_a, side_b))
    up_a, up_b = (up_a.reshape(rows, shards, unit), up_b.reshape(rows, shards, unit))
    whole = [flat[n] for n in range(8)]
    grads = (
        jnp.stack([qkv_a, qkv_b], axis=2).reshape(rows, -1),
        whole[0],
        whole[1],
        jnp.concatenate([out_a, out_b], axis=1),
        whole[2],
        whole[3],
        whole[4],
        jnp.stack([up_a, up_b], axis=2).reshape(rows, -1),
        flat[8:].reshape(-1),
        jnp.concatenate([down_a, down_b], axis=0),
        whole[5],
        whole[6],
        whole[7],
    )
    shape = (1, count, 1, -1, model)
    activations = choose(middle, last).reshape(shape)
    input_grads = choose(grad_first, grad_middle).reshape(shape)
    return (activations, input_grads) + tuple(member[None] for member in grads)


def solution(mesh):
    rows = P(None, ("dp", "shard"), None, None)
    matrix = P("section", "shard", None)
    vector = P("section", "shard")
    weight_specs = (matrix, vector, vector, matrix, vector, vector, vector)
    weight_specs += (matrix, vector, matrix, vector, vector, vector)
    in_specs = (rows, P(None, ("dp", "shard")), rows) + weight_specs
    result = P("section", None, ("dp", "shard"), None, None)
    return jax.shard_map(
        per_device,
        mesh=mesh,
        in_specs=in_specs,
        out_specs=(result, result) + weight_specs,
        check_vma=False,
    )
```
